32 devices in a mesh: groups: 2 (over y), gx: 4 (over z), gy: 2 (over core), gz: 2 (over x).
Axes of the slice: x: 2, y: 2, z: 4, core: 2. Of those that a mesh axis runs over, the one named last changes fastest.
Arguments:
- east_strip: bfloat16 [4, 8, 4, 64, 2048], P(('groups', 'gz'), 'gy', 'gx'), parts along dimension 0
- west_strip: bfloat16 [4, 8, 4, 64, 2048], P(('groups', 'gz'), 'gy', 'gx'), parts along dimension 0
- north_strip: bfloat16 [4, 8, 4, 64, 2048], P(('groups', 'gz'), 'gy', 'gx'), parts along dimension 0
- south_strip: bfloat16 [4, 8, 4, 64, 2048], P(('groups', 'gz'), 'gy', 'gx'), parts along dimension 0
- patch_start: int32 [16], replicated, may hold values from 0 to 1984, as said below
- segment_offset: float32 [4, 8, 4, 2], P(('groups', 'gz'), 'gy', 'gx'), parts along dimension 0, may hold values from -6 to 6
- col_stiffness: float32 [4, 8, 4], P(('groups', 'gz'), 'gy', 'gx'), parts along dimension 0, may hold values from 0.25 to 1
- row_stiffness: float32 [4, 8, 4], P(('groups', 'gz'), 'gy', 'gx'), parts along dimension 0, may hold values from 0.25 to 1
Outputs:
- patch_shift: float32 [4, 8, 4, 2, 2, 16], P(('groups', 'gz'), 'gy', 'gx'), parts along dimension 0
- placed_offset: float32 [4, 8, 4, 2], P(('groups', 'gz'), 'gy', 'gx'), parts along dimension 0
The draws below stay inside these ranges and needn't reach their ends.
There are 2 independent parts, one for each index of `groups`. The reference program is written for one: setup_inputs(seed, part) draws one part's arguments, and reference() takes and returns one part's arrays. A program takes and returns all parts, laid end to end along the dimension named above; an argument that names none is the same for every part. Nothing has to cross between parts.
Inputs may be any that keep to these rules, and one draw needn't show every extreme that they name: `patch_start`: increasing; patch k starts in the k-th of 16 equal cells of the edge and ends within it; the first start is 0 and the last is 1984.
All inputs are finite; a program needn't handle non-finite values.
Results may differ from the reference program's by a relative error of at most 0.0003.
Values may be sent and summed in bfloat16 or wider, within the bound.
No kernel may reach another device: no remote copies, remote signals or barrier semaphores. Data moves between devices by JAX's collectives and lax.ppermute only.
A program may use at most 64 MiB of HBM per device.

```python
import math
import jax
import jax.numpy as jnp
from jax import lax

P_SIZE = 64
SL = 2048
NPATCH = 16
ITERS = 3
NS = 2
NR = 8
NC = 4


def roll_tile(tile_pixels, shift_across, shift_along):
    return jnp.roll(jnp.roll(tile_pixels, shift_across, axis=0), shift_along, axis=1)


def paired_strips(key, salt, tile_axis):
    key = jax.random.fold_in(key, salt)
    keys = jax.random.split(key, 4)
    shape = (NS, NR, NC, P_SIZE, SL)
    first_strip = jax.random.normal(keys[0], shape, jnp.float32)
    noise = jax.random.normal(keys[1], shape, jnp.float32)
    shift_across = jax.random.randint(keys[2], shape[:3], -4, 5)
    shift_along = jax.random.randint(keys[3], shape[:3], -24, 25)
    rolled = jax.vmap(jax.vmap(jax.vmap(roll_tile)))(first_strip, shift_across, shift_along)
    count = shape[tile_axis]
    carried = jnp.concatenate([jnp.zeros_like(lax.slice_in_dim(rolled, 0, 1, axis=tile_axis)), lax.slice_in_dim(rolled, 0, count - 1, axis=tile_axis)], axis=tile_axis)
    second = 0.8 * carried + 0.6 * noise
    return (first_strip, second)


def draw_east_strip(key, part):
    return paired_strips(key, 21, 2)[0].astype(jnp.bfloat16)


def draw_west_strip(key, part):
    return paired_strips(key, 21, 2)[1].astype(jnp.bfloat16)


def draw_south_strip(key, part):
    return paired_strips(key, 22, 1)[0].astype(jnp.bfloat16)


def draw_north_strip(key, part):
    return paired_strips(key, 22, 1)[1].astype(jnp.bfloat16)


def draw_patch_start(key, part):
    key = jax.random.fold_in(key, 5)
    cell_size = SL // NPATCH
    starts = jnp.arange(NPATCH, dtype=jnp.int32) * cell_size
    jitter = jax.random.randint(key, (NPATCH,), 0, cell_size - P_SIZE + 1)
    starts = starts + jitter
    starts = starts.at[0].set(0)
    starts = starts.at[NPATCH - 1].set(SL - P_SIZE)
    return starts.astype(jnp.int32)


def levels(own_key, dims, cuts, low, largest):
    factor_of, own = 1.0, jax.random.fold_in(own_key, 6)
    for dim, parts in cuts:
        steps = jnp.exp(jax.random.uniform(jax.random.fold_in(own, dim), (parts,), jnp.float32, low / len(cuts), largest / len(cuts)))
        factor_of = factor_of * jnp.repeat(steps, dims[dim] // parts).reshape([-1 if axis == dim else 1 for axis in range(len(dims))])
    return factor_of


def normal_values(key, shape, scale, most, cuts=(), kind=jnp.bfloat16):
    level = levels(key, shape, cuts, -0.22, 0.18) if cuts else 1.0
    array = jax.random.normal(key, shape, jnp.float32) * scale * level
    return jnp.minimum(jnp.maximum(array, -most), most).astype(kind)


def setup_inputs(seed: int = 0, part: int = 0) -> dict:
    key_list = jax.random.split(jax.random.key(seed), 9)
    own_keys = jax.random.split(jax.random.fold_in(key_list[8], part), 9)
    east_strip = draw_east_strip(jax.random.fold_in(jax.random.fold_in(key_list[8], part), 71), part)
    west_strip = draw_west_strip(jax.random.fold_in(jax.random.fold_in(key_list[8], part), 71), part)
    north_strip = draw_north_strip(jax.random.fold_in(jax.random.fold_in(key_list[8], part), 71), part)
    south_strip = draw_south_strip(jax.random.fold_in(jax.random.fold_in(key_list[8], part), 71), part)
    patch_start = draw_patch_start(jax.random.fold_in(key_list[8], 71), part)
    segment_offset = normal_values(own_keys[5], (NS, NR, NC, 2), 1.0, 6.0, ((0, 2), (1, 2), (2, 4)), jnp.float32)
    col_stiffness = jnp.clip(jnp.exp(math.log(1.0) - 1.3862944 * jax.random.uniform(own_keys[6], (NS, NR, NC), jnp.float32) ** levels(own_keys[6], (NS, NR, NC), ((0, 2), (1, 2), (2, 4)), -0.2, 0.2)), 0.25, 1.0)
    row_stiffness = jnp.clip(jnp.exp(math.log(1.0) - 1.3862944 * jax.random.uniform(own_keys[7], (NS, NR, NC), jnp.float32) ** levels(own_keys[7], (NS, NR, NC), ((0, 2), (1, 2), (2, 4)), -0.2, 0.2)), 0.25, 1.0)
    return {"east_strip": east_strip, "west_strip": west_strip, "north_strip": north_strip, "south_strip": south_strip, "patch_start": patch_start, "segment_offset": segment_offset, "col_stiffness": col_stiffness, "row_stiffness": row_stiffness}


EPS_VAR = 1e-05
EPS_WEIGHT = 1e-06
STEP_SIZE = 0.12
LINK_STIFF = 0.5

def cut_patches(strip, patch_start):
    offsets = patch_start[:, None].astype(jnp.int32) + jnp.arange(P_SIZE, dtype=jnp.int32)[None, :]
    gathered = jnp.take(strip, offsets, axis=-1)
    return jnp.moveaxis(gathered, -2, -3).astype(jnp.float32)

def normalize(patches):
    centred = patches - lax.optimization_barrier(jnp.mean(patches, axis=(-2, -1), keepdims=True))
    return centred / jnp.sqrt(lax.optimization_barrier(jnp.mean(centred * centred, axis=(-2, -1), keepdims=True)) + EPS_VAR)

def correlate(first_patch, second):
    spec_first = jnp.fft.fft2(normalize(first_patch))
    spec_second = jnp.fft.fft2(normalize(second))
    surface = jnp.real(jnp.fft.ifft2(spec_first * jnp.conj(spec_second))) / (P_SIZE * P_SIZE)
    weight = surface * surface
    offsets = jnp.arange(P_SIZE)
    signed = jnp.where(offsets < P_SIZE // 2, offsets, offsets - P_SIZE).astype(jnp.float32)
    strength = lax.optimization_barrier(jnp.sum(weight, axis=(-2, -1)))
    across = lax.optimization_barrier(jnp.sum(weight * signed[:, None], axis=(-2, -1))) / (strength + EPS_WEIGHT)
    along_edge = lax.optimization_barrier(jnp.sum(weight * signed[None, :], axis=(-2, -1))) / (strength + EPS_WEIGHT)
    return (across, along_edge, strength)

def pair_offset(across, along_edge, strength):
    total = lax.optimization_barrier(jnp.sum(strength, axis=-1)) + EPS_WEIGHT
    return jnp.stack([lax.optimization_barrier(jnp.sum(strength * across, axis=-1)) / total, lax.optimization_barrier(jnp.sum(strength * along_edge, axis=-1)) / total], axis=-1)

def reference(east_strip, west_strip, north_strip, south_strip, patch_start, segment_offset, col_stiffness, row_stiffness):
    west_next = jnp.concatenate([west_strip[:, :, 1:], jnp.zeros_like(west_strip[:, :, :1])], axis=2)
    north_next = jnp.concatenate([north_strip[:, 1:], jnp.zeros_like(north_strip[:, :1])], axis=1)

    def per_section(pieces):
        east_s, west_s, south_s, north_s = pieces
        across_h, along_h, strength_h = correlate(cut_patches(east_s, patch_start), cut_patches(west_s, patch_start))
        across_v, along_v, strength_v = correlate(cut_patches(south_s, patch_start), cut_patches(north_s, patch_start))
        return (across_h, along_h, strength_h, across_v, along_v, strength_v)
    across_h, along_h, strength_h, across_v, along_v, strength_v = lax.map(per_section, (east_strip, west_next, south_strip, north_next))
    patch_shift = jnp.stack([jnp.stack([across_h, along_h], axis=3), jnp.stack([across_v, along_v], axis=3)], axis=3)
    offset_h = pair_offset(across_h, along_h, strength_h)
    offset_v = pair_offset(across_v, along_v, strength_v)
    has_east = (jnp.arange(NC) < NC - 1).astype(jnp.float32)
    has_south = (jnp.arange(NR) < NR - 1).astype(jnp.float32)
    col_eff = col_stiffness * has_east[None, None, :]
    row_eff = row_stiffness * has_south[None, :, None]
    stiff_w = jnp.concatenate([jnp.zeros_like(col_eff[:, :, :1]), col_eff[:, :, :-1]], axis=2)
    offset_w = jnp.concatenate([jnp.zeros_like(offset_h[:, :, :1]), offset_h[:, :, :-1]], axis=2)
    stiff_n = jnp.concatenate([jnp.zeros_like(row_eff[:, :1]), row_eff[:, :-1]], axis=1)
    offset_n = jnp.concatenate([jnp.zeros_like(offset_v[:, :1]), offset_v[:, :-1]], axis=1)
    sections = jnp.arange(NS)
    has_next = (sections < NS - 1).astype(jnp.float32)[:, None, None, None]
    has_prev = (sections > 0).astype(jnp.float32)[:, None, None, None]
    placed = segment_offset
    for repeat in range(ITERS):
        padded = jnp.pad(placed, ((1, 1), (1, 1), (1, 1), (0, 0)))
        force = col_eff[..., None] * (padded[1:-1, 1:-1, 2:] - placed - offset_h)
        force = force - stiff_w[..., None] * (placed - padded[1:-1, 1:-1, :-2] - offset_w)
        force = force + row_eff[..., None] * (padded[1:-1, 2:, 1:-1] - placed - offset_v)
        force = force - stiff_n[..., None] * (placed - padded[1:-1, :-2, 1:-1] - offset_n)
        force = force + LINK_STIFF * has_next * (padded[2:, 1:-1, 1:-1] - placed)
        force = force + LINK_STIFF * has_prev * (padded[:-2, 1:-1, 1:-1] - placed)
        placed = placed + STEP_SIZE * force
    return (patch_shift, placed)
```

```python
import functools
import math

import jax
import jax.numpy as jnp
import numpy as np
from jax import lax
from jax.experimental import pallas as pl
from jax.experimental.pallas import tpu as pltpu
from jax.sharding import PartitionSpec as P

ITERS = 3
EPS_VAR = 1e-05
EPS_WEIGHT = 1e-06
STEP_SIZE = 0.12
LINK_STIFF = 0.5
F32 = jnp.float32
BF16 = jnp.bfloat16
PART = ("gx", "gz", "gy")
VMEM_LIMIT = 48 * 1024 * 1024

EAST, SOUTH = 0, 32
D_SOUTH, D_EAST, POSITION, COL, ROW = 64, 66, 68, 70, 71


def waves(width):
    quarter = width // 4
    first = np.cos(2.0 * np.pi * np.arange(quarter + 1) / width)
    first[quarter] = 0.0
    cosine = np.zeros(width)
    cosine[: quarter + 1] = first
    cosine[quarter : 2 * quarter + 1] = -first[::-1]
    cosine[2 * quarter :] = -cosine[: 2 * quarter]
    return cosine, np.roll(cosine, quarter)


def basis(width):
    cosine, sine = waves(width)
    half = width // 2
    phase = np.arange(half)[:, None] * np.arange(width)[None, :] % width
    low, high = cosine[phase], sine[phase]
    high[0] = cosine[half * np.arange(width) % width]
    return np.concatenate([low, high], axis=0)


def two_terms(table):
    high = table.astype(np.float32).astype(jnp.bfloat16)
    low = (table - high.astype(np.float64)).astype(np.float32).astype(jnp.bfloat16)
    return high, low


def spread(table, width):
    half = width // 2
    wide = np.zeros((4, width, 2, 4, half))
    for patch in range(4):
        for side in range(2):
            wide[patch, :, side, patch, :] = table[:, side * half : (side + 1) * half]
    return wide.reshape(4 * width, 4 * width)


def tables(width, count):
    plain = basis(width)
    half = width // 2
    norm = np.full((width, 1), math.sqrt(2.0 / width))
    norm[0] = norm[half] = math.sqrt(1.0 / width)
    unit = plain * norm
    right_high, right_low = two_terms(spread(unit.T, width))
    right = np.concatenate([right_high, right_low], axis=0)
    left_high, left_low = two_terms(unit)
    left = np.concatenate([left_high, left_high, left_low], axis=1)
    back_high, back_low = two_terms(spread(plain.T, width).T)
    right_back = np.concatenate([back_high, back_high, back_low], axis=0)
    inv_high, inv_low = two_terms(plain.T)
    left_back = np.concatenate([inv_high, inv_high, inv_low], axis=1)
    energy = np.full(width, width / 2.0)
    energy[0] = energy[half] = width
    energy = energy / float(width) ** 4
    signed = np.where(np.arange(width) < half, np.arange(width), np.arange(width) - width)
    slot_sum = np.zeros((count // 4, 2, 4, half, 128))
    place_sum = np.zeros((count // 4, 4, width, 128))
    for quad in range(count // 4):
        for patch in range(4):
            for side in range(2):
                slot_sum[quad, side, patch, :, quad * 4 + patch] = energy[side * half : (side + 1) * half]
            place_sum[quad, patch, :, quad * 4 + patch] = signed * (width / 2.0) / float(width) ** 4
    sums = np.concatenate(
        [slot_sum.reshape(count * width, 128), place_sum.reshape(count * width, 128)], axis=1
    )
    ones = np.kron(np.eye(4), np.ones((half, half)))
    return (
        right,
        left,
        right_back,
        left_back,
        sums.astype(jnp.bfloat16),
        ones.astype(jnp.bfloat16),
    )


def dot(left, right):
    return jnp.dot(left, right, preferred_element_type=F32)


def split(value):
    high = value.astype(BF16)
    return high, (value - high.astype(F32)).astype(BF16)


def split3(value):
    high = value.astype(BF16)
    rest = value - high.astype(F32)
    middle = rest.astype(BF16)
    return high, middle, (rest - middle.astype(F32)).astype(BF16)


def exact_dot(value, table):
    rows = value.shape[0]
    high, middle, low = split3(value)
    out = dot(jnp.concatenate([high, middle, low], axis=0), table)
    return out[:rows] + out[rows : 2 * rows] + out[2 * rows :]


def cut_tile(start_ref, load, store, width, cell, count):
    lane = lax.broadcasted_iota(jnp.int32, (width, cell), 1)
    for pair in range(count // 2):
        parts = []
        for odd in range(2):
            k = 2 * pair + odd
            offset = start_ref[k] - k * cell
            turn = lax.rem(cell + odd * width - offset, cell)
            parts.append(pltpu.roll(load(k).astype(F32), turn, 1))
        store(pair // 2, pair % 2, jnp.where(lane < width, parts[0], parts[1]).astype(BF16))


def forward(d_ref, q_ref, e_ref, right_ref, left_ref, groups, width):
    span = 4 * width
    lane = lax.broadcasted_iota(jnp.int32, (8, span // 2), 1)
    row = lax.broadcasted_iota(jnp.int32, (8, span // 2), 0)
    keep = jnp.where((row == 0) & (lane % (width // 2) == 0), 0.0, 1.0)
    step = 4

    def body(i, carry):
        base = pl.multiple_of(i * step * width, step * width)
        data = d_ref[pl.ds(base, step * width), :]
        y = dot(jnp.concatenate([data, data], axis=1), right_ref[...])
        high, low = split(y)
        for j in range(step):
            rows = slice(j * width, (j + 1) * width)
            stack = jnp.concatenate([high[rows], low[rows], high[rows]], axis=0)
            q = dot(left_ref[...], stack)
            q_ref[i * step + j] = q
            head = q[0:8, : span // 2] * keep
            q_ref[i * step + j, 0:8, 0 : span // 2] = head
            squares = head * head
            for r in range(8, width, 8):
                squares = squares + q[r : r + 8, : span // 2] * q[r : r + 8, : span // 2]
            for r in range(0, width, 8):
                squares = squares + q[r : r + 8, span // 2 :] * q[r : r + 8, span // 2 :]
            e_ref[i * step + j] = squares
        return carry

    lax.fori_loop(0, groups // step, body, 0)


def products(f, g, width):
    half = width // 2
    span = 2 * width
    lane = lax.broadcasted_iota(jnp.int32, (8, span), 1)
    row = lax.broadcasted_iota(jnp.int32, (8, span), 0)
    plain_lane = lane % half != 0
    plain_row = row != 0
    out = [[], [], [], []]
    for r in range(0, half, 8):
        fcc, fcs = f[r : r + 8, :span], f[r : r + 8, span:]
        fsc, fss = f[half + r : half + r + 8, :span], f[half + r : half + r + 8, span:]
        gcc, gcs = g[r : r + 8, :span], g[r : r + 8, span:]
        gsc, gss = g[half + r : half + r + 8, :span], g[half + r : half + r + 8, span:]
        gcc_s = jnp.where(plain_lane, gcc, gcs)
        gsc_s = jnp.where(plain_lane, gsc, gss)
        gcs = jnp.where(plain_lane, gcs, 0.0)
        gss = jnp.where(plain_lane, gss, 0.0)
        hcc, hcs, hcc_s = gcc, gcs, gcc_s
        if r == 0:
            hcc = jnp.where(plain_row, gcc, gsc)
            hcs = jnp.where(plain_row, gcs, gss)
            hcc_s = jnp.where(plain_row, gcc_s, gsc_s)
            gsc = jnp.where(plain_row, gsc, 0.0)
            gss = jnp.where(plain_row, gss, 0.0)
            gsc_s = jnp.where(plain_row, gsc_s, 0.0)
        out[0].append((fcc * gcc + fcs * gcs) + (fsc * gsc + fss * gss))
        out[1].append((fcs * gcc_s - fcc * gcs) + (fss * gsc_s - fsc * gss))
        out[2].append((fsc * hcc + fss * hcs) - (fcc * gsc + fcs * gss))
        out[3].append((fss * hcc_s - fsc * hcs) - (fcs * gsc_s - fcc * gss))
    top = jnp.concatenate([jnp.concatenate(out[0], 0), jnp.concatenate(out[1], 0)], axis=1)
    low = jnp.concatenate([jnp.concatenate(out[2], 0), jnp.concatenate(out[3], 0)], axis=1)
    return jnp.concatenate([top, low], axis=0)


def backward(qf_ref, qg_ref, ef_ref, eg_ref, scale_ref, sum_ref, right_ref, left_ref, ones_ref, groups, width):
    span = 4 * width
    pixels = float(width * width)

    def factors(e_ref):
        energy = exact_dot(jnp.sum(e_ref[0:groups], axis=1), ones_ref[...])
        return lax.rsqrt(energy * (1.0 / pixels) + EPS_VAR)

    scale_ref[0:groups, 0, :] = factors(ef_ref) * factors(eg_ref)
    row = lax.broadcasted_iota(jnp.int32, (8, span), 0)
    special = jnp.where(row == 0, 2.0, 1.0)
    step = 4

    def body(i, carry):
        highs, lows = [], []
        for j in range(step):
            index = i * step + j
            scale = scale_ref[index]
            scale = jnp.concatenate([scale, scale], axis=1)
            z = products(qf_ref[index] * scale, qg_ref[index], width)
            high, low = split(z)
            highs.append(high)
            lows.append(low)
        high = jnp.concatenate(highs, axis=0)
        low = jnp.concatenate(lows, axis=0)
        v = dot(jnp.concatenate([high, low, high], axis=1), right_ref[...])
        for j in range(step):
            u = dot(left_ref[...], jnp.concatenate([highs[j], lows[j], highs[j]], axis=0))
            strength = jnp.zeros((8, span), F32)
            across = jnp.zeros((8, span), F32)
            along = jnp.zeros((8, span), F32)
            for r in range(0, width, 8):
                square = u[r : r + 8] * u[r : r + 8]
                strength = strength + square
                first = r if r < width // 2 else r - width
                across = across + square * (row + first).astype(F32)
                piece = v[j * width + r : j * width + r + 8]
                piece = piece * piece
                if r % (width // 2) == 0:
                    piece = piece * special
                along = along + piece
            lanes = slice(j * span, (j + 1) * span)
            for kind, value in enumerate((strength, across, along)):
                sum_ref[kind, pl.ds(i, 1), lanes] = jnp.sum(value, axis=0, keepdims=True)
        return carry

    lax.fori_loop(0, groups // step, body, 0)


def finish(sum_ref, sums_ref):
    both = exact_dot(jnp.concatenate([sum_ref[0], sum_ref[1]], axis=0), sums_ref[:, :128])
    strength, across = both[:8], both[8:]
    along = exact_dot(sum_ref[2], sums_ref[:, 128:])
    across = across / (strength + EPS_WEIGHT)
    along = along / (strength + EPS_WEIGHT)
    total = jnp.sum(strength, axis=1, keepdims=True) + EPS_WEIGHT
    first = jnp.sum(strength * across, axis=1, keepdims=True) / total
    second = jnp.sum(strength * along, axis=1, keepdims=True) / total
    return across, along, first, second


def at_lane(first, second, where):
    lane = lax.broadcasted_iota(jnp.int32, (8, 128), 1)
    return jnp.where(lane == where, first, 0.0) + jnp.where(lane == where + 1, second, 0.0)


def cut_kernel(sizes, start_ref, west_ref, east_ref, north_ref, west_out, east_out, north_out):
    width, cell, count, half_rows = sizes

    def one(source, tile, target, slot):
        def load(k):
            return source[0, tile, 0, :, k * cell : (k + 1) * cell]

        def store(quad, side, value):
            target[slot, quad, :, side * cell : (side + 1) * cell] = value

        cut_tile(start_ref, load, store, width, cell, count)

    one(north_ref, 0, north_out, 0)
    for slot in range(half_rows):
        one(west_ref, slot, west_out, slot)
        one(east_ref, slot, east_out, slot)


def fill(d_ref, slot, source_ref, tile, start_ref, sizes):
    width, cell, count = sizes

    def load(k):
        return source_ref[0, tile, 0, :, k * cell : (k + 1) * cell]

    def store(quad, side, value):
        base = (slot * (count // 4) + quad) * width
        d_ref[base : base + width, side * cell : (side + 1) * cell] = value

    cut_tile(start_ref, load, store, width, cell, count)


def copy_in(d_ref, slot, source_ref, tile, sizes):
    width, cell, count = sizes
    for quad in range(count // 4):
        base = (slot * (count // 4) + quad) * width
        d_ref[base : base + width, :] = source_ref[tile, quad]


def south_kernel(sizes, rows, start_ref, south_ref, north_ref, rim_ref, right_ref, left_ref, right_back_ref, left_back_ref, sums_ref, ones_ref, out_ref, d_ref, q_ref, e_ref, scale_ref, sum_ref):
    width, cell, count = sizes
    groups = rows * count // 4
    span = groups * width
    for tile in range(rows):
        fill(d_ref, tile, south_ref, tile, start_ref, sizes)
    for tile in range(rows - 1):
        fill(d_ref, rows + tile, north_ref, tile + 1, start_ref, sizes)
    copy_in(d_ref, 2 * rows - 1, rim_ref, 0, sizes)
    forward(d_ref, q_ref, e_ref, right_ref, left_ref, 2 * groups, width)
    sum_ref[...] = jnp.zeros_like(sum_ref)
    backward(q_ref.at[0:groups], q_ref.at[groups : 2 * groups], e_ref.at[0:groups], e_ref.at[groups : 2 * groups], scale_ref, sum_ref, right_back_ref, left_back_ref, ones_ref, groups, width)
    across, along, first, second = finish(sum_ref, sums_ref)
    out_ref[...] = pltpu.roll(across, SOUTH, 1) + pltpu.roll(along, SOUTH + 16, 1) + at_lane(first, second, D_SOUTH)


def east_kernel(sizes, rows, start_ref, east_ref, west_ref, from_east_ref, from_west_ref, south_ref, position_ref, col_ref, row_ref, right_ref, left_ref, right_back_ref, left_back_ref, sums_ref, ones_ref, out_ref, d_ref, q_ref, e_ref, scale_ref, sum_ref, place_ref):
    width, cell, count = sizes
    groups = rows * count // 4
    own = rows // 2
    for tile in range(own):
        fill(d_ref, tile, east_ref, tile, start_ref, sizes)
        copy_in(d_ref, rows + tile, from_east_ref, tile, sizes)
    for tile in range(own, rows):
        copy_in(d_ref, tile, from_west_ref, tile - own, sizes)
        fill(d_ref, rows + tile, west_ref, tile, start_ref, sizes)
    forward(d_ref, q_ref, e_ref, right_ref, left_ref, 2 * groups, width)
    sum_ref[...] = jnp.zeros_like(sum_ref)
    backward(q_ref.at[0:groups], q_ref.at[groups : 2 * groups], e_ref.at[0:groups], e_ref.at[groups : 2 * groups], scale_ref, sum_ref, right_back_ref, left_back_ref, ones_ref, groups, width)
    across, along, first, second = finish(sum_ref, sums_ref)
    place_ref[...] = jnp.zeros_like(place_ref)
    place_ref[0, 0:rows, 0:2] = position_ref[0, :, 0, :]
    place_ref[1, 0:rows, 0:1] = col_ref[0]
    place_ref[2, 0:rows, 0:1] = row_ref[0]
    packet = south_ref[...] + across + pltpu.roll(along, EAST + 16, 1) + at_lane(first, second, D_EAST)
    packet = packet + pltpu.roll(place_ref[0], POSITION, 1) + pltpu.roll(place_ref[1], COL, 1) + pltpu.roll(place_ref[2], ROW, 1)
    out_ref[...] = jnp.broadcast_to(packet[None], out_ref.shape)


def turned(value, by):
    count = value.shape[0]
    by = by % count
    return value if by == 0 else jnp.concatenate([value[by:], value[:by]], axis=0)


def relax_kernel(counts, rows, patches, all_ref, shift_ref, placed_ref, x_ref):
    nx, nz, ny = counts
    total = nx * nz * ny
    packet = all_ref[...]
    sub = lax.broadcasted_iota(jnp.int32, packet.shape, 1)
    device = lax.broadcasted_iota(jnp.int32, packet.shape, 0)
    gx, gz, gy = device // (nz * ny), device // ny % nz, device % ny

    def field(where):
        return pltpu.roll(packet, 128 - where, 2)

    def one(where):
        return jnp.broadcast_to(packet[:, :, where : where + 1], packet.shape)

    def east(value):
        return turned(value, nz * ny)

    def west(value):
        return turned(value, -nz * ny)

    def south(value):
        inside = pltpu.roll(value, 7, 1)
        beyond = pltpu.roll(turned(value, 1), rows - 1, 1)
        return jnp.where(sub == rows - 1, beyond, inside)

    def north(value):
        inside = pltpu.roll(value, 1, 1)
        beyond = pltpu.roll(turned(value, -1), 8 - (rows - 1), 1)
        return jnp.where(sub == 0, beyond, inside)

    x = field(POSITION)
    d_east = field(D_EAST)
    d_east = jnp.where(sub < rows // 2, d_east, east(d_east))
    d_south = field(D_SOUTH)
    ke = jnp.where(gx < nx - 1, one(COL), 0.0)
    ks = jnp.where((gy == ny - 1) & (sub == rows - 1), 0.0, one(ROW))
    kw, d_west = west(ke), west(d_east)
    kn, d_north = north(ks), north(d_south)
    has_next = jnp.where(gz < nz - 1, LINK_STIFF, 0.0)
    has_prev = jnp.where(gz > 0, LINK_STIFF, 0.0)
    for _ in range(ITERS):
        force = ke * (east(x) - x - d_east) - kw * (x - west(x) - d_west)
        force = force + ks * (south(x) - x - d_south) - kn * (x - north(x) - d_north)
        force = force + has_next * (turned(x, ny) - x) + has_prev * (turned(x, -ny) - x)
        x = x + STEP_SIZE * force
    x_ref[...] = x
    me = (lax.axis_index("gx") * nz + lax.axis_index("gz")) * ny + lax.axis_index("gy")
    next_east = lax.rem(me + nz * ny, total)
    placed_ref[0, :, 0, :] = x_ref[me, 0:rows, 0:2]
    own, other = all_ref[me], all_ref[next_east]
    row = lax.broadcasted_iota(jnp.int32, own.shape, 0)
    mixed = jnp.where(row < rows // 2, own, other)
    for kind, (source, where) in enumerate(((mixed, EAST), (own, SOUTH))):
        for part in range(2):
            value = source
            if where + part * patches:
                value = pltpu.roll(source, 128 - where - part * patches, 1)
            for tile in range(rows):
                shift_ref[0, tile, 0, kind, part : part + 1, :] = value[tile : tile + 1, :patches]


def neighbour(block, axis, distance):
    count = lax.axis_size(axis)
    route = [(i, i + distance) for i in range(count) if 0 <= i + distance < count]
    return lax.ppermute(block, axis, route)


def shards(east_strip, west_strip, north_strip, south_strip, patch_start, segment_offset, col_stiffness, row_stiffness):
    _, rows, _, width, length = east_strip.shape
    count = patch_start.shape[0]
    cell = length // count
    sizes = (width, cell, count)
    half_rows = rows // 2
    quads = count // 4
    span = 4 * width
    groups = rows * quads
    counts = tuple(lax.axis_size(axis) for axis in PART)
    total = math.prod(counts)
    constants = [jnp.asarray(table) for table in tables(width, count)]
    params = pltpu.CompilerParams(vmem_limit_bytes=VMEM_LIMIT)
    smem = pl.BlockSpec(memory_space=pltpu.SMEM)
    vmem = pl.BlockSpec(memory_space=pltpu.VMEM)

    def some_rows(number, block):
        return pl.BlockSpec((1, number, 1, width, length), lambda i: (0, block, 0, 0, 0))

    west_cut, east_cut, north_cut = pl.pallas_call(
        functools.partial(cut_kernel, (width, cell, count, half_rows)),
        grid=(1,),
        out_shape=[
            jax.ShapeDtypeStruct((half_rows, quads, width, span), BF16),
            jax.ShapeDtypeStruct((half_rows, quads, width, span), BF16),
            jax.ShapeDtypeStruct((1, quads, width, span), BF16),
        ],
        in_specs=[smem, some_rows(half_rows, 0), some_rows(half_rows, 1), some_rows(1, 0)],
        out_specs=[
            pl.BlockSpec((half_rows, quads, width, span), lambda i: (0, 0, 0, 0)),
            pl.BlockSpec((half_rows, quads, width, span), lambda i: (0, 0, 0, 0)),
            pl.BlockSpec((1, quads, width, span), lambda i: (0, 0, 0, 0)),
        ],
        compiler_params=params,
        name="cut",
    )(patch_start, west_strip, east_strip, north_strip)

    from_east = neighbour(west_cut, "gx", -1)
    from_west = neighbour(east_cut, "gx", 1)
    from_south = neighbour(north_cut, "gy", -1)

    scratch = [
        pltpu.VMEM((2 * groups * width, span), BF16),
        pltpu.VMEM((2 * groups, width, span), F32),
        pltpu.VMEM((2 * groups, 8, span // 2), F32),
        pltpu.VMEM((groups, 1, span // 2), F32),
        pltpu.VMEM((3, 8, quads * span), F32),
    ]
    cost = pl.CostEstimate(flops=6_000_000_000, bytes_accessed=4_000_000, transcendentals=0)
    south = pl.pallas_call(
        functools.partial(south_kernel, sizes, rows),
        out_shape=jax.ShapeDtypeStruct((8, 128), F32),
        in_specs=[smem] + [vmem] * 9,
        out_specs=vmem,
        scratch_shapes=scratch,
        compiler_params=params,
        cost_estimate=cost,
        name="south",
    )(patch_start, south_strip, north_strip, from_south, *constants)
    packet = pl.pallas_call(
        functools.partial(east_kernel, sizes, rows),
        out_shape=jax.ShapeDtypeStruct((total, 8, 128), F32),
        in_specs=[smem] + [vmem] * 14,
        out_specs=vmem,
        scratch_shapes=scratch + [pltpu.VMEM((3, 8, 128), F32)],
        compiler_params=params,
        cost_estimate=cost,
        name="east",
    )(patch_start, east_strip, west_strip, from_east, from_west, south, segment_offset, col_stiffness, row_stiffness, *constants)
    gathered = lax.all_to_all(packet, PART, 0, 0)
    return tuple(
        pl.pallas_call(
            functools.partial(relax_kernel, counts, rows, count),
            out_shape=[
                jax.ShapeDtypeStruct((1, rows, 1, 2, 2, count), F32),
                jax.ShapeDtypeStruct((1, rows, 1, 2), F32),
            ],
            in_specs=[vmem],
            out_specs=[vmem, vmem],
            scratch_shapes=[pltpu.VMEM((total, 8, 128), F32)],
            compiler_params=params,
            name="relax",
        )(gathered)
    )


def solution(mesh):
    placed = (
        P(("groups", "gz"), "gy", "gx", None, None),
        P(("groups", "gz"), "gy", "gx", None, None),
        P(("groups", "gz"), "gy", "gx", None, None),
        P(("groups", "gz"), "gy", "gx", None, None),
        P(),
        P(("groups", "gz"), "gy", "gx", None),
        P(("groups", "gz"), "gy", "gx"),
        P(("groups", "gz"), "gy", "gx"),
    )
    return jax.shard_map(
        shards,
        mesh=mesh,
        in_specs=placed,
        out_specs=(
            P(("groups", "gz"), "gy", "gx", None, None, None),
            P(("groups", "gz"), "gy", "gx", None),
        ),
        check_vma=False,
    )
```

```python
import functools
import math

import jax
import jax.numpy as jnp
import numpy as np
from jax import lax
from jax.experimental import pallas as pl
from jax.experimental.pallas import tpu as pltpu
from jax.sharding import PartitionSpec as P

ITERS = 3
EPS_VAR = 1e-05
EPS_WEIGHT = 1e-06
STEP_SIZE = 0.12
LINK_STIFF = 0.5
F32 = jnp.float32
BF16 = jnp.bfloat16
PART = ("gx", "gz", "gy")
MIB = 1024 * 1024
CUT_VMEM, SOUTH_VMEM, EAST_VMEM, RELAX_VMEM = 62 * MIB, 52 * MIB, 32 * MIB, 16 * MIB

EAST, SOUTH = 0, 32
D_SOUTH, D_EAST, POSITION, COL, ROW = 64, 66, 68, 70, 71


def waves(width):
    quarter = width // 4
    first = np.cos(2.0 * np.pi * np.arange(quarter + 1) / width)
    first[quarter] = 0.0
    cosine = np.zeros(width)
    cosine[: quarter + 1] = first
    cosine[quarter : 2 * quarter + 1] = -first[::-1]
    cosine[2 * quarter :] = -cosine[: 2 * quarter]
    return cosine, np.roll(cosine, quarter)


def basis(width):
    cosine, sine = waves(width)
    half = width // 2
    phase = np.arange(half)[:, None] * np.arange(width)[None, :] % width
    low, high = cosine[phase], sine[phase]
    high[0] = cosine[half * np.arange(width) % width]
    return np.concatenate([low, high], axis=0)


def two_terms(table):
    high = table.astype(np.float32).astype(jnp.bfloat16)
    low = (table - high.astype(np.float64)).astype(np.float32).astype(jnp.bfloat16)
    return high, low


def spread(table, width):
    half = width // 2
    wide = np.zeros((4, width, 2, 4, half))
    for patch in range(4):
        for side in range(2):
            wide[patch, :, side, patch, :] = table[:, side * half : (side + 1) * half]
    return wide.reshape(4 * width, 4 * width)


def tables(width):
    plain = basis(width)
    half = width // 2
    norm = np.full((width, 1), math.sqrt(2.0 / width))
    norm[0] = norm[half] = math.sqrt(1.0 / width)
    unit = plain * norm
    right = np.concatenate(two_terms(spread(unit.T, width)), axis=0)
    right_back = np.concatenate(two_terms(spread(plain.T, width).T), axis=0)
    lefts = []
    for table in (unit, plain.T):
        high, low = two_terms(table)
        lefts.append(np.concatenate([high, high, low], axis=1))
    energy = np.full(width, width / 2.0)
    energy[0] = energy[half] = width
    signed = np.where(np.arange(width) < half, np.arange(width), np.arange(width) - width) * (width / 2.0)
    slot_sum = np.zeros((2, 4, half, 128))
    place_sum = np.zeros((4, width, 128))
    for patch in range(4):
        for side in range(2):
            slot_sum[side, patch, :, patch] = energy[side * half : (side + 1) * half]
        place_sum[patch, :, patch] = signed
    sums = np.concatenate([slot_sum.reshape(4 * width, 128), place_sum.reshape(4 * width, 128)], axis=1)
    sums = sums / float(width) ** 4
    ones = np.kron(np.eye(4), np.ones((half, half)))
    return (right, right_back, np.stack(lefts), sums.astype(jnp.bfloat16), ones.astype(jnp.bfloat16))


def dot(left, right):
    return jnp.dot(left, right, preferred_element_type=F32)


def split(value):
    high = value.astype(BF16)
    return high, (value - high.astype(F32)).astype(BF16)


def split3(value):
    high = value.astype(BF16)
    rest = value - high.astype(F32)
    middle = rest.astype(BF16)
    return high, middle, (rest - middle.astype(F32)).astype(BF16)


def exact_dot(value, table):
    rows = value.shape[0]
    high, middle, low = split3(value)
    out = dot(jnp.concatenate([high, middle, low], axis=0), table)
    return out[:rows] + out[rows : 2 * rows] + out[2 * rows :]


def cut_tile(start_ref, load, store, width, cell, count):
    lane = lax.broadcasted_iota(jnp.int32, (width, cell), 1)
    for pair in range(count // 2):
        parts = []
        for odd in range(2):
            k = 2 * pair + odd
            offset = start_ref[k] - k * cell
            turn = lax.rem(cell + odd * width - offset, cell)
            parts.append(pltpu.roll(load(k).astype(F32), turn, 1))
        store(pair // 2, pair % 2, jnp.where(lane < width, parts[0], parts[1]).astype(BF16))


def forward(source, q_ref, e_ref, right_ref, left_ref, first, groups, width):
    span = 4 * width
    lane = lax.broadcasted_iota(jnp.int32, (8, span // 2), 1)
    row = lax.broadcasted_iota(jnp.int32, (8, span // 2), 0)
    keep = jnp.where((row == 0) & (lane % (width // 2) == 0), 0.0, 1.0)
    step = 4
    for i in range(0, groups, step):
        data = source(i)
        y = dot(jnp.concatenate([data, data], axis=1), right_ref[...])
        high, low = split(y)
        for j in range(step):
            rows = slice(j * width, (j + 1) * width)
            stack = jnp.concatenate([high[rows], low[rows], high[rows]], axis=0)
            q = dot(left_ref[0], stack)
            index = first + i + j
            head = q[0:8, : span // 2] * keep
            q_ref[index, 0:8, 0 : span // 2] = head
            q_ref[index, 0:8, span // 2 :] = q[0:8, span // 2 :]
            q_ref[index, 8:width, :] = q[8:width]
            squares = head * head
            for r in range(8, width, 8):
                squares = squares + q[r : r + 8, : span // 2] * q[r : r + 8, : span // 2]
            for r in range(0, width, 8):
                squares = squares + q[r : r + 8, span // 2 :] * q[r : r + 8, span // 2 :]
            e_ref[pl.ds(index, 1), :] = jnp.sum(squares, axis=0, keepdims=True)


def products(f, g, width):
    half = width // 2
    span = 2 * width
    lane = lax.broadcasted_iota(jnp.int32, (8, span), 1)
    row = lax.broadcasted_iota(jnp.int32, (8, span), 0)
    plain_lane = lane % half != 0
    plain_row = row != 0
    out = [[], [], [], []]
    for r in range(0, half, 8):
        fcc, fcs = f[r : r + 8, :span], f[r : r + 8, span:]
        fsc, fss = f[half + r : half + r + 8, :span], f[half + r : half + r + 8, span:]
        gcc, gcs = g[r : r + 8, :span], g[r : r + 8, span:]
        gsc, gss = g[half + r : half + r + 8, :span], g[half + r : half + r + 8, span:]
        gcc_s = jnp.where(plain_lane, gcc, gcs)
        gsc_s = jnp.where(plain_lane, gsc, gss)
        gcs = jnp.where(plain_lane, gcs, 0.0)
        gss = jnp.where(plain_lane, gss, 0.0)
        hcc, hcs, hcc_s = gcc, gcs, gcc_s
        if r == 0:
            hcc = jnp.where(plain_row, gcc, gsc)
            hcs = jnp.where(plain_row, gcs, gss)
            hcc_s = jnp.where(plain_row, gcc_s, gsc_s)
            gsc = jnp.where(plain_row, gsc, 0.0)
            gss = jnp.where(plain_row, gss, 0.0)
            gsc_s = jnp.where(plain_row, gsc_s, 0.0)
        out[0].append((fcc * gcc + fcs * gcs) + (fsc * gsc + fss * gss))
        out[1].append((fcs * gcc_s - fcc * gcs) + (fss * gsc_s - fsc * gss))
        out[2].append((fsc * hcc + fss * hcs) - (fcc * gsc + fcs * gss))
        out[3].append((fss * hcc_s - fsc * hcs) - (fcs * gsc_s - fcc * gss))
    top = jnp.concatenate([jnp.concatenate(out[0], 0), jnp.concatenate(out[1], 0)], axis=1)
    low = jnp.concatenate([jnp.concatenate(out[2], 0), jnp.concatenate(out[3], 0)], axis=1)
    return jnp.concatenate([top, low], axis=0)


def factors(e_ref, first, groups, ones_ref, width):
    energy = exact_dot(e_ref[first : first + groups], ones_ref[...])
    return lax.rsqrt(energy * (1.0 / (width * width)) + EPS_VAR)


def backward(load_f, load_g, scales, sum_ref, right_ref, left_ref, groups, width):
    span = 4 * width
    row = lax.broadcasted_iota(jnp.int32, (8, span), 0)
    special = jnp.where(row == 0, 2.0, 1.0)
    step = 4
    sum_ref[...] = jnp.zeros_like(sum_ref)
    table = right_ref[...]
    table = jnp.concatenate([table[:span], table[:span], table[span:]], axis=0)
    for i in range(0, groups, step):
        highs, lows = [], []
        for j in range(step):
            scale = jnp.broadcast_to(scales[i + j : i + j + 1], (width, span // 2))
            scale = jnp.concatenate([scale, scale], axis=1)
            z = products(load_f(i + j) * scale, load_g(i + j), width)
            high, low = split(z)
            highs.append(high)
            lows.append(low)
        high = jnp.concatenate(highs, axis=0)
        low = jnp.concatenate(lows, axis=0)
        v = dot(jnp.concatenate([high, low, high], axis=1), table)
        for j in range(step):
            u = dot(left_ref[1], jnp.concatenate([highs[j], lows[j], highs[j]], axis=0))
            strength = jnp.zeros((8, span), F32)
            across = jnp.zeros((8, span), F32)
            along = jnp.zeros((8, span), F32)
            for r in range(0, width, 8):
                square = u[r : r + 8] * u[r : r + 8]
                strength = strength + square
                first = r if r < width // 2 else r - width
                across = across + square * (row + first).astype(F32)
                piece = v[j * width + r : j * width + r + 8]
                piece = piece * piece
                if r % (width // 2) == 0:
                    piece = piece * special
                along = along + piece
            tile = i // step
            for kind, value in enumerate((strength, across, along)):
                sum_ref[kind, j, tile : tile + 1, :] = jnp.sum(value, axis=0, keepdims=True)


def finish(sum_ref, sums_ref):
    _, quads, rows, span = sum_ref.shape
    flat = jnp.concatenate([sum_ref[kind, quad] for kind in range(3) for quad in range(quads)], axis=0)
    done = exact_dot(flat, sums_ref[...])
    kinds = []
    for kind in range(3):
        value = jnp.zeros((rows, 128), F32)
        for quad in range(quads):
            base = (kind * quads + quad) * rows
            part = done[base : base + rows, :128] if kind < 2 else done[base : base + rows, 128:]
            value = value + (pltpu.roll(part, 4 * quad, 1) if quad else part)
        kinds.append(value)
    strength, across, along = kinds
    across = across / (strength + EPS_WEIGHT)
    along = along / (strength + EPS_WEIGHT)
    total = jnp.sum(strength, axis=1, keepdims=True) + EPS_WEIGHT
    first = jnp.sum(strength * across, axis=1, keepdims=True) / total
    second = jnp.sum(strength * along, axis=1, keepdims=True) / total
    return across, along, first, second


def at_lane(first, second, where):
    lane = lax.broadcasted_iota(jnp.int32, (8, 128), 1)
    return jnp.where(lane == where, first, 0.0) + jnp.where(lane == where + 1, second, 0.0)


class Copies:
    def __init__(self, sems):
        self.sems, self.count = sems, 0

    def start(self, source, target):
        copy = pltpu.make_async_copy(source, target, self.sems.at[self.count])
        self.count += 1
        copy.start()
        return copy

    def start_either(self, even, first, second, target):
        sem = self.sems.at[self.count]
        self.count += 1

        @pl.when(even)
        def _():
            pltpu.make_async_copy(first, target, sem).start()

        @pl.when(jnp.logical_not(even))
        def _():
            pltpu.make_async_copy(second, target, sem).start()

        return pltpu.make_async_copy(first, target, sem)


def is_even():
    return lax.rem(lax.axis_index("gy"), 2) == 0


def cut_into(target, source, start_ref, sizes):
    width, cell, count = sizes

    def load(k):
        return source[:, k * cell : (k + 1) * cell]

    def store(quad, side, value):
        target[quad, :, side * cell : (side + 1) * cell] = value

    cut_tile(start_ref, load, store, width, cell, count)


def cut_kernel(sizes, rows, start_hbm, west_ref, east_ref, north_ref, send_out, north_out, start_ref, raw_ref, cut_ref, sems):
    copies = Copies(sems)
    even = is_even()
    start = copies.start(start_hbm, start_ref)
    loads = []
    for tile in range(rows):
        loads.append(copies.start_either(even, west_ref.at[0, tile, 0], east_ref.at[0, tile, 0], raw_ref.at[tile]))
    loads.append(copies.start(north_ref.at[0, 0, 0], raw_ref.at[rows]))
    stores = []
    start.wait()
    for tile in range(rows + 1):
        loads[tile].wait()
        cut_into(cut_ref.at[tile], raw_ref.at[tile], start_ref, sizes)
        stores.append(copies.start(cut_ref.at[tile], send_out.at[tile] if tile < rows else north_out.at[0]))
    for store in stores:
        store.wait()


def south_kernel(sizes, rows, start_hbm, south_ref, north_ref, rim_ref, east_ref, west_ref, right_hbm, back_hbm, left_hbm, sums_hbm, ones_hbm, out_ref, q_out, e_out, start_ref, raw_ref, d_ref, q_ref, e_ref, sum_ref, right_ref, back_ref, left_ref, sums_ref, ones_ref, sems):
    width, cell, count = sizes
    quads = count // 4
    groups = rows * quads
    copies = Copies(sems)
    even = is_even()
    batches = [[copies.start(start_hbm, start_ref)], [], []]
    for tile in range(rows):
        batches[0].append(copies.start(south_ref.at[0, tile, 0], raw_ref.at[tile]))
    batches[0] += [copies.start(right_hbm, right_ref), copies.start(left_hbm, left_ref)]
    for tile in range(rows - 1):
        batches[1].append(copies.start(north_ref.at[0, tile + 1, 0], raw_ref.at[rows + tile]))
    for tile in range(rows):
        slot = 2 * rows + tile
        batches[2].append(copies.start_either(even, east_ref.at[0, tile, 0], west_ref.at[0, tile, 0], raw_ref.at[slot]))
    batches[2] += [copies.start(back_hbm, back_ref), copies.start(sums_hbm, sums_ref), copies.start(ones_hbm, ones_ref)]

    def arrive(batch):
        for copy in batches[batch]:
            copy.wait()

    def cut(batch):
        for slot in range(batch * rows, (batch + 1) * rows):
            if slot != 2 * rows - 1:
                cut_into(d_ref.at[slot], raw_ref.at[slot], start_ref, sizes)

    def transform(batch):
        def source(i):
            slot = batch * rows + i // quads
            value = rim_ref[0] if slot == 2 * rows - 1 else d_ref[slot]
            return value.reshape(quads * width, 4 * width)

        forward(source, q_ref, e_ref, right_ref, left_ref, batch * groups, groups, width)

    arrive(0)
    cut(0)
    arrive(1)
    transform(0)
    cut(1)
    arrive(2)
    transform(1)
    cut(2)
    transform(2)
    own = copies.start(q_ref.at[2 * groups : 3 * groups], q_out)
    e_out[...] = e_ref[2 * groups : 3 * groups]
    scales = factors(e_ref, 0, groups, ones_ref, width) * factors(e_ref, groups, groups, ones_ref, width)
    backward(lambda i: q_ref[i], lambda i: q_ref[groups + i], scales, sum_ref, back_ref, left_ref, groups, width)
    across, along, first, second = finish(sum_ref, sums_ref)
    out_ref[...] = pltpu.roll(across, SOUTH, 1) + pltpu.roll(along, SOUTH + 16, 1) + at_lane(first, second, D_SOUTH)
    own.wait()


def east_kernel(sizes, rows, received_ref, q_own, e_own, south_ref, position_ref, col_ref, row_ref, right_hbm, back_hbm, left_hbm, sums_hbm, ones_hbm, out_ref, q_ref, e_ref, sum_ref, right_ref, back_ref, left_ref, sums_ref, ones_ref, place_ref, sems):
    width, cell, count = sizes
    quads = count // 4
    groups = rows * quads
    copies = Copies(sems)
    arriving = [copies.start(right_hbm, right_ref), copies.start(left_hbm, left_ref)]
    own = [copies.start(q_own, q_ref.at[0]), copies.start(back_hbm, back_ref), copies.start(sums_hbm, sums_ref), copies.start(ones_hbm, ones_ref)]
    for copy in arriving:
        copy.wait()

    def source(i):
        return received_ref[i // quads].reshape(quads * width, 4 * width)

    forward(source, q_ref.at[1], e_ref, right_ref, left_ref, 0, groups, width)
    for copy in own:
        copy.wait()
    scales = factors(e_ref, 0, groups, ones_ref, width) * factors(e_own, 0, groups, ones_ref, width)
    odd = lax.rem(lax.axis_index("gy"), 2)
    backward(lambda i: q_ref[odd, i], lambda i: q_ref[1 - odd, i], scales, sum_ref, back_ref, left_ref, groups, width)
    across, along, first, second = finish(sum_ref, sums_ref)
    place_ref[...] = jnp.zeros_like(place_ref)
    place_ref[0:2, 0:rows] = position_ref[0, 0]
    place_ref[2:3, 0:rows] = col_ref[0]
    place_ref[3:4, 0:rows] = row_ref[0]
    lane = lax.broadcasted_iota(jnp.int32, (8, 128), 1)
    row = lax.broadcasted_iota(jnp.int32, (8, 128), 0)
    packet = south_ref[...] + across + pltpu.roll(along, EAST + 16, 1) + at_lane(first, second, D_EAST)
    for field, where in enumerate((POSITION, POSITION + 1, COL, ROW)):
        value = jnp.where(lane == row, place_ref[field : field + 1, :], 0.0)
        packet = packet + jnp.where(lane == where, jnp.sum(value, axis=1, keepdims=True), 0.0)
    out_ref[...] = jnp.broadcast_to(packet[None], out_ref.shape)


def turned(value, by):
    count = value.shape[0]
    by = by % count
    return value if by == 0 else jnp.concatenate([value[by:], value[:by]], axis=0)


def relax_kernel(counts, rows, patches, all_ref, shift_ref, placed_ref, x_ref):
    nx, nz, ny = counts
    total = nx * nz * ny
    packet = all_ref[...]
    sub = lax.broadcasted_iota(jnp.int32, packet.shape, 1)
    device = lax.broadcasted_iota(jnp.int32, packet.shape, 0)
    gx, gz, gy = device // (nz * ny), device // ny % nz, device % ny

    def field(where):
        return pltpu.roll(packet, 128 - where, 2)

    def one(where):
        return jnp.broadcast_to(packet[:, :, where : where + 1], packet.shape)

    def east(value):
        return turned(value, nz * ny)

    def west(value):
        return turned(value, -nz * ny)

    def south(value):
        inside = pltpu.roll(value, 7, 1)
        beyond = pltpu.roll(turned(value, 1), rows - 1, 1)
        return jnp.where(sub == rows - 1, beyond, inside)

    def north(value):
        inside = pltpu.roll(value, 1, 1)
        beyond = pltpu.roll(turned(value, -1), 8 - (rows - 1), 1)
        return jnp.where(sub == 0, beyond, inside)

    x = field(POSITION)
    d_east = field(D_EAST)
    d_east = jnp.where(gy % 2 == 0, d_east, east(d_east))
    d_south = field(D_SOUTH)
    ke = jnp.where(gx < nx - 1, one(COL), 0.0)
    ks = jnp.where((gy == ny - 1) & (sub == rows - 1), 0.0, one(ROW))
    kw, d_west = west(ke), west(d_east)
    kn, d_north = north(ks), north(d_south)
    has_next = jnp.where(gz < nz - 1, LINK_STIFF, 0.0)
    has_prev = jnp.where(gz > 0, LINK_STIFF, 0.0)
    for _ in range(ITERS):
        force = ke * (east(x) - x - d_east) - kw * (x - west(x) - d_west)
        force = force + ks * (south(x) - x - d_south) - kn * (x - north(x) - d_north)
        force = force + has_next * (turned(x, ny) - x) + has_prev * (turned(x, -ny) - x)
        x = x + STEP_SIZE * force
    x_ref[...] = x
    mine = lax.axis_index("gy")
    me = (lax.axis_index("gx") * nz + lax.axis_index("gz")) * ny + mine
    holder = lax.rem(me + lax.rem(mine, 2) * (nz * ny), total)
    lane = lax.broadcasted_iota(jnp.int32, (8, 128), 1)
    row = lax.broadcasted_iota(jnp.int32, (8, 128), 0)
    own = x_ref[me]
    for part in range(2):
        value = jnp.where((lane == row) & (row < rows), own[:, part : part + 1], 0.0)
        placed_ref[0, 0, part : part + 1, :] = jnp.sum(value, axis=0, keepdims=True)[:, :rows]
    for kind, (source, where) in enumerate(((all_ref[holder], EAST), (all_ref[me], SOUTH))):
        for part in range(2):
            value = source
            if where + part * patches:
                value = pltpu.roll(source, 128 - where - part * patches, 1)
            for tile in range(rows):
                shift_ref[0, tile, 0, kind, part : part + 1, :] = value[tile : tile + 1, :patches]


def to_pair_owner(block):
    nx, ny = lax.axis_size("gx"), lax.axis_size("gy")
    route = []
    for x in range(nx):
        for y in range(ny):
            target = x - 1 if y % 2 == 0 else x + 1
            if 0 <= target < nx:
                route.append((x * ny + y, target * ny + y))
    return lax.ppermute(block, ("gx", "gy"), route)


def to_north(block):
    return lax.ppermute(block, "gy", [(i, i - 1) for i in range(1, lax.axis_size("gy"))])


def shards(east_strip, west_strip, north_strip, south_strip, patch_start, segment_offset, col_stiffness, row_stiffness):
    _, rows, _, width, length = east_strip.shape
    count = patch_start.shape[0]
    sizes = (width, length // count, count)
    quads = count // 4
    span = 4 * width
    groups = rows * quads
    counts = tuple(lax.axis_size(axis) for axis in PART)
    total = math.prod(counts)
    constants = [jnp.asarray(table) for table in tables(width)]
    vmem = pl.BlockSpec(memory_space=pltpu.VMEM)
    hbm = pl.BlockSpec(memory_space=pl.ANY)

    send, north_cut = pl.pallas_call(
        functools.partial(cut_kernel, sizes, rows),
        out_shape=[
            jax.ShapeDtypeStruct((rows, quads, width, span), BF16),
            jax.ShapeDtypeStruct((1, quads, width, span), BF16),
        ],
        in_specs=[hbm, hbm, hbm, hbm],
        out_specs=[hbm, hbm],
        scratch_shapes=[
            pltpu.SMEM((count,), jnp.int32),
            pltpu.VMEM((rows + 1, width, length), BF16),
            pltpu.VMEM((rows + 1, quads, width, span), BF16),
            pltpu.SemaphoreType.DMA((2 * rows + 3,)),
        ],
        compiler_params=pltpu.CompilerParams(vmem_limit_bytes=CUT_VMEM),
        name="cut",
    )(patch_start, west_strip, east_strip, north_strip)
    received = to_pair_owner(send)
    rim = to_north(north_cut)

    tables_in_vmem = [pltpu.VMEM(table.shape, table.dtype) for table in constants]
    sums = pltpu.VMEM((3, quads, 8, span), F32)
    south, q_own, e_own = pl.pallas_call(
        functools.partial(south_kernel, sizes, rows),
        out_shape=[
            jax.ShapeDtypeStruct((8, 128), F32),
            jax.ShapeDtypeStruct((groups, width, span), F32),
            jax.ShapeDtypeStruct((groups, span // 2), F32),
        ],
        in_specs=[hbm] * 3 + [vmem] + [hbm] * 7,
        out_specs=[vmem, hbm, vmem],
        scratch_shapes=[
            pltpu.SMEM((count,), jnp.int32),
            pltpu.VMEM((3 * rows, width, length), BF16),
            pltpu.VMEM((3 * rows, quads, width, span), BF16),
            pltpu.VMEM((3 * groups, width, span), F32),
            pltpu.VMEM((3 * groups, span // 2), F32),
            sums,
            *tables_in_vmem,
            pltpu.SemaphoreType.DMA((3 * rows + len(constants) + 1,)),
        ],
        compiler_params=pltpu.CompilerParams(vmem_limit_bytes=SOUTH_VMEM),
        cost_estimate=pl.CostEstimate(flops=6_000_000_000, bytes_accessed=8_000_000, transcendentals=0),
        name="south",
    )(patch_start, south_strip, north_strip, rim, east_strip, west_strip, *constants)
    packet = pl.pallas_call(
        functools.partial(east_kernel, sizes, rows),
        out_shape=jax.ShapeDtypeStruct((total, 8, 128), F32),
        in_specs=[vmem, hbm] + [vmem] * 5 + [hbm] * 5,
        out_specs=vmem,
        scratch_shapes=[
            pltpu.VMEM((2, groups, width, span), F32),
            pltpu.VMEM((groups, span // 2), F32),
            sums,
            *tables_in_vmem,
            pltpu.VMEM((8, 128), F32),
            pltpu.SemaphoreType.DMA((1 + len(constants),)),
        ],
        compiler_params=pltpu.CompilerParams(vmem_limit_bytes=EAST_VMEM),
        cost_estimate=pl.CostEstimate(flops=3_000_000_000, bytes_accessed=2_000_000, transcendentals=0),
        name="east",
    )(
        received,
        q_own,
        e_own,
        south,
        jnp.transpose(segment_offset, (0, 2, 3, 1)),
        jnp.transpose(col_stiffness, (0, 2, 1)),
        jnp.transpose(row_stiffness, (0, 2, 1)),
        *constants,
    )
    gathered = lax.all_to_all(packet, PART, 0, 0)
    patch_shift, placed = pl.pallas_call(
        functools.partial(relax_kernel, counts, rows, count),
        out_shape=[
            jax.ShapeDtypeStruct((1, rows, 1, 2, 2, count), F32),
            jax.ShapeDtypeStruct((1, 1, 2, rows), F32),
        ],
        in_specs=[vmem],
        out_specs=[vmem, vmem],
        scratch_shapes=[pltpu.VMEM((total, 8, 128), F32)],
        compiler_params=pltpu.CompilerParams(vmem_limit_bytes=RELAX_VMEM),
        name="relax",
    )(gathered)
    return patch_shift, jnp.transpose(placed, (0, 3, 1, 2))


def solution(mesh):
    placed = (
        P(("groups", "gz"), "gy", "gx", None, None),
        P(("groups", "gz"), "gy", "gx", None, None),
        P(("groups", "gz"), "gy", "gx", None, None),
        P(("groups", "gz"), "gy", "gx", None, None),
        P(),
        P(("groups", "gz"), "gy", "gx", None),
        P(("groups", "gz"), "gy", "gx"),
        P(("groups", "gz"), "gy", "gx"),
    )
    return jax.shard_map(
        shards,
        mesh=mesh,
        in_specs=placed,
        out_specs=(
            P(("groups", "gz"), "gy", "gx", None, None, None),
            P(("groups", "gz"), "gy", "gx", None),
        ),
        check_vma=False,
    )
```

```python
import functools
import math

import jax
import jax.numpy as jnp
import numpy as np
from jax import lax
from jax.experimental import pallas as pl
from jax.experimental.pallas import tpu as pltpu
from jax.sharding import PartitionSpec as P

ITERS = 3
EPS_VAR = 1e-05
EPS_WEIGHT = 1e-06
STEP_SIZE = 0.12
LINK_STIFF = 0.5
F32 = jnp.float32
BF16 = jnp.bfloat16
PART = ("gx", "gz", "gy")
MIB = 1024 * 1024
CUT_VMEM, SOUTH_VMEM, EAST_VMEM, RELAX_VMEM = 62 * MIB, 52 * MIB, 52 * MIB, 16 * MIB

EAST, SOUTH = 0, 32
D_SOUTH, D_EAST, POSITION, COL, ROW = 64, 66, 68, 70, 71


def waves(width):
    quarter = width // 4
    first = np.cos(2.0 * np.pi * np.arange(quarter + 1) / width)
    first[quarter] = 0.0
    cosine = np.zeros(width)
    cosine[: quarter + 1] = first
    cosine[quarter : 2 * quarter + 1] = -first[::-1]
    cosine[2 * quarter :] = -cosine[: 2 * quarter]
    return cosine, np.roll(cosine, quarter)


def basis(width):
    cosine, sine = waves(width)
    half = width // 2
    phase = np.arange(half)[:, None] * np.arange(width)[None, :] % width
    low, high = cosine[phase], sine[phase]
    high[0] = cosine[half * np.arange(width) % width]
    return np.concatenate([low, high], axis=0)


def two_terms(table):
    high = table.astype(np.float32).astype(jnp.bfloat16)
    low = (table - high.astype(np.float64)).astype(np.float32).astype(jnp.bfloat16)
    return high, low


def spread(table, width):
    half = width // 2
    wide = np.zeros((4, width, 2, 4, half))
    for patch in range(4):
        for side in range(2):
            wide[patch, :, side, patch, :] = table[:, side * half : (side + 1) * half]
    return wide.reshape(4 * width, 4 * width)


def tables(width):
    plain = basis(width)
    half = width // 2
    norm = np.full((width, 1), math.sqrt(2.0 / width))
    norm[0] = norm[half] = math.sqrt(1.0 / width)
    unit = plain * norm
    right = np.concatenate(two_terms(spread(unit.T, width)), axis=0)
    right_back = np.concatenate(two_terms(spread(plain.T, width).T), axis=0)
    lefts = []
    for table in (unit, plain.T):
        high, low = two_terms(table)
        lefts.append(np.concatenate([high, high, low], axis=1))
    energy = np.full(width, width / 2.0)
    energy[0] = energy[half] = width
    signed = np.where(np.arange(width) < half, np.arange(width), np.arange(width) - width) * (width / 2.0)
    slot_sum = np.zeros((2, 4, half, 128))
    place_sum = np.zeros((4, width, 128))
    for patch in range(4):
        for side in range(2):
            slot_sum[side, patch, :, patch] = energy[side * half : (side + 1) * half]
        place_sum[patch, :, patch] = signed
    sums = np.concatenate([slot_sum.reshape(4 * width, 128), place_sum.reshape(4 * width, 128)], axis=1)
    sums = sums / float(width) ** 4
    ones = np.kron(np.eye(4), np.ones((half, half)))
    return (right, right_back, np.stack(lefts), sums.astype(jnp.bfloat16), ones.astype(jnp.bfloat16))


def dot(left, right):
    return jnp.dot(left, right, preferred_element_type=F32)


def split(value):
    high = value.astype(BF16)
    return high, (value - high.astype(F32)).astype(BF16)


def split3(value):
    high = value.astype(BF16)
    rest = value - high.astype(F32)
    middle = rest.astype(BF16)
    return high, middle, (rest - middle.astype(F32)).astype(BF16)


def exact_dot(value, table):
    rows = value.shape[0]
    high, middle, low = split3(value)
    out = dot(jnp.concatenate([high, middle, low], axis=0), table)
    return out[:rows] + out[rows : 2 * rows] + out[2 * rows :]


def cut_tile(start_ref, load, store, width, cell, count):
    lane = lax.broadcasted_iota(jnp.int32, (width, cell), 1)
    for pair in range(count // 2):
        parts = []
        for odd in range(2):
            k = 2 * pair + odd
            offset = start_ref[k] - k * cell
            turn = lax.rem(cell + odd * width - offset, cell)
            parts.append(pltpu.roll(load(k).astype(F32), turn, 1))
        store(pair // 2, pair % 2, jnp.where(lane < width, parts[0], parts[1]).astype(BF16))


def forward(source, q_ref, e_ref, right_ref, left_ref, first, groups, width):
    span = 4 * width
    lane = lax.broadcasted_iota(jnp.int32, (8, span // 2), 1)
    row = lax.broadcasted_iota(jnp.int32, (8, span // 2), 0)
    keep = jnp.where((row == 0) & (lane % (width // 2) == 0), 0.0, 1.0)
    step = 4
    for i in range(0, groups, step):
        data = source(i)
        y = dot(jnp.concatenate([data, data], axis=1), right_ref[...])
        high, low = split(y)
        for j in range(step):
            rows = slice(j * width, (j + 1) * width)
            stack = jnp.concatenate([high[rows], low[rows], high[rows]], axis=0)
            q = dot(left_ref[0], stack)
            index = first + i + j
            head = q[0:8, : span // 2] * keep
            q_ref[index, 0:8, 0 : span // 2] = head
            q_ref[index, 0:8, span // 2 :] = q[0:8, span // 2 :]
            q_ref[index, 8:width, :] = q[8:width]
            squares = head * head
            for r in range(8, width, 8):
                squares = squares + q[r : r + 8, : span // 2] * q[r : r + 8, : span // 2]
            for r in range(0, width, 8):
                squares = squares + q[r : r + 8, span // 2 :] * q[r : r + 8, span // 2 :]
            e_ref[pl.ds(index, 1), :] = jnp.sum(squares, axis=0, keepdims=True)


def products(f, g, width):
    half = width // 2
    span = 2 * width
    lane = lax.broadcasted_iota(jnp.int32, (8, span), 1)
    row = lax.broadcasted_iota(jnp.int32, (8, span), 0)
    plain_lane = lane % half != 0
    plain_row = row != 0
    out = [[], [], [], []]
    for r in range(0, half, 8):
        fcc, fcs = f[r : r + 8, :span], f[r : r + 8, span:]
        fsc, fss = f[half + r : half + r + 8, :span], f[half + r : half + r + 8, span:]
        gcc, gcs = g[r : r + 8, :span], g[r : r + 8, span:]
        gsc, gss = g[half + r : half + r + 8, :span], g[half + r : half + r + 8, span:]
        gcc_s = jnp.where(plain_lane, gcc, gcs)
        gsc_s = jnp.where(plain_lane, gsc, gss)
        gcs = jnp.where(plain_lane, gcs, 0.0)
        gss = jnp.where(plain_lane, gss, 0.0)
        hcc, hcs, hcc_s = gcc, gcs, gcc_s
        if r == 0:
            hcc = jnp.where(plain_row, gcc, gsc)
            hcs = jnp.where(plain_row, gcs, gss)
            hcc_s = jnp.where(plain_row, gcc_s, gsc_s)
            gsc = jnp.where(plain_row, gsc, 0.0)
            gss = jnp.where(plain_row, gss, 0.0)
            gsc_s = jnp.where(plain_row, gsc_s, 0.0)
        out[0].append((fcc * gcc + fcs * gcs) + (fsc * gsc + fss * gss))
        out[1].append((fcs * gcc_s - fcc * gcs) + (fss * gsc_s - fsc * gss))
        out[2].append((fsc * hcc + fss * hcs) - (fcc * gsc + fcs * gss))
        out[3].append((fss * hcc_s - fsc * hcs) - (fcs * gsc_s - fcc * gss))
    top = jnp.concatenate([jnp.concatenate(out[0], 0), jnp.concatenate(out[1], 0)], axis=1)
    low = jnp.concatenate([jnp.concatenate(out[2], 0), jnp.concatenate(out[3], 0)], axis=1)
    return jnp.concatenate([top, low], axis=0)


def factors(e_ref, first, groups, ones_ref, width):
    energy = exact_dot(e_ref[first : first + groups], ones_ref[...])
    return lax.rsqrt(energy * (1.0 / (width * width)) + EPS_VAR)


def backward(load_f, load_g, scales, sum_ref, right_ref, left_ref, groups, width):
    span = 4 * width
    row = lax.broadcasted_iota(jnp.int32, (8, span), 0)
    special = jnp.where(row == 0, 2.0, 1.0)
    step = 4
    table = right_ref[...]
    table = jnp.concatenate([table[:span], table[:span], table[span:]], axis=0)
    for i in range(0, groups, step):
        highs, lows = [], []
        for j in range(step):
            scale = jnp.broadcast_to(scales[i + j : i + j + 1], (width, span // 2))
            scale = jnp.concatenate([scale, scale], axis=1)
            z = products(load_f(i + j) * scale, load_g(i + j), width)
            high, low = split(z)
            highs.append(high)
            lows.append(low)
        high = jnp.concatenate(highs, axis=0)
        low = jnp.concatenate(lows, axis=0)
        v = dot(jnp.concatenate([high, low, high], axis=1), table)
        for j in range(step):
            u = dot(left_ref[1], jnp.concatenate([highs[j], lows[j], highs[j]], axis=0))
            strength = jnp.zeros((8, span), F32)
            across = jnp.zeros((8, span), F32)
            along = jnp.zeros((8, span), F32)
            for r in range(0, width, 8):
                square = u[r : r + 8] * u[r : r + 8]
                strength = strength + square
                first = r if r < width // 2 else r - width
                across = across + square * (row + first).astype(F32)
                piece = v[j * width + r : j * width + r + 8]
                piece = piece * piece
                if r % (width // 2) == 0:
                    piece = piece * special
                along = along + piece
            tile = i // step
            for kind, value in enumerate((strength, across, along)):
                sum_ref[kind, j, tile : tile + 1, :] = jnp.sum(value, axis=0, keepdims=True)


def finish(sum_ref, sums_ref):
    _, quads, rows, span = sum_ref.shape
    flat = jnp.concatenate([sum_ref[kind, quad] for kind in range(3) for quad in range(quads)], axis=0)
    done = exact_dot(flat, sums_ref[...])
    kinds = []
    for kind in range(3):
        value = jnp.zeros((rows, 128), F32)
        for quad in range(quads):
            base = (kind * quads + quad) * rows
            part = done[base : base + rows, :128] if kind < 2 else done[base : base + rows, 128:]
            value = value + (pltpu.roll(part, 4 * quad, 1) if quad else part)
        kinds.append(value)
    strength, across, along = kinds
    across = across / (strength + EPS_WEIGHT)
    along = along / (strength + EPS_WEIGHT)
    return strength, across, along


def pack(strength, across, along, where, offset):
    lane = lax.broadcasted_iota(jnp.int32, (8, 128), 1)
    total = jnp.sum(strength, axis=1, keepdims=True) + EPS_WEIGHT
    first = jnp.sum(strength * across, axis=1, keepdims=True) / total
    second = jnp.sum(strength * along, axis=1, keepdims=True) / total
    shifts = (pltpu.roll(across, where, 1) if where else across) + pltpu.roll(along, where + 16, 1)
    return shifts + jnp.where(lane == offset, first, 0.0) + jnp.where(lane == offset + 1, second, 0.0)


class Copies:
    def __init__(self, sems):
        self.sems, self.count = sems, 0

    def start(self, source, target):
        copy = pltpu.make_async_copy(source, target, self.sems.at[self.count])
        self.count += 1
        copy.start()
        return copy

    def start_either(self, even, first, second, target):
        sem = self.sems.at[self.count]
        self.count += 1

        @pl.when(even)
        def _():
            pltpu.make_async_copy(first, target, sem).start()

        @pl.when(jnp.logical_not(even))
        def _():
            pltpu.make_async_copy(second, target, sem).start()

        return pltpu.make_async_copy(first, target, sem)


def is_even():
    return lax.rem(lax.axis_index("gy"), 2) == 0


def cut_into(target, source, start_ref, sizes):
    width, cell, count = sizes

    def load(k):
        return source[:, k * cell : (k + 1) * cell]

    def store(quad, side, value):
        target[quad, :, side * cell : (side + 1) * cell] = value

    cut_tile(start_ref, load, store, width, cell, count)


def cut_kernel(sizes, rows, start_hbm, west_ref, east_ref, north_ref, send_ref, rim_ref, start_ref, raw_ref, sems):
    copies = Copies(sems)
    even = is_even()
    start = copies.start(start_hbm, start_ref)
    loads = []
    for tile in range(rows):
        loads.append(copies.start_either(even, west_ref.at[0, tile, 0], east_ref.at[0, tile, 0], raw_ref.at[tile]))
    loads.append(copies.start(north_ref.at[0, 0, 0], raw_ref.at[rows]))
    start.wait()
    for tile in range(rows + 1):
        loads[tile].wait()
        target = send_ref.at[tile] if tile < rows else rim_ref.at[0]
        cut_into(target, raw_ref.at[tile], start_ref, sizes)


def south_kernel(sizes, rows, start_hbm, south_ref, north_ref, east_ref, west_ref, position_ref, col_ref, row_ref, right_ref, back_ref, left_ref, sums_ref, ones_ref, out_ref, q_out, e_out, start_ref, raw_ref, d_ref, q_ref, e_ref, sum_ref, place_ref, sems):
    width, cell, count = sizes
    quads = count // 4
    groups = rows * quads
    inner = groups - quads
    copies = Copies(sems)
    even = is_even()
    batches = [[copies.start(start_hbm, start_ref)], [], []]
    for tile in range(rows - 1):
        batches[0].append(copies.start(south_ref.at[0, tile, 0], raw_ref.at[tile]))
    for tile in range(rows - 1):
        batches[1].append(copies.start(north_ref.at[0, tile + 1, 0], raw_ref.at[rows - 1 + tile]))
    batches[2].append(copies.start(south_ref.at[0, rows - 1, 0], raw_ref.at[2 * rows - 2]))
    for tile in range(rows):
        slot = 2 * rows - 1 + tile
        batches[2].append(copies.start_either(even, east_ref.at[0, tile, 0], west_ref.at[0, tile, 0], raw_ref.at[slot]))
    slots = [range(0, rows - 1), range(rows - 1, 2 * rows - 2), range(2 * rows - 2, 3 * rows - 1)]

    def arrive(batch):
        for copy in batches[batch]:
            copy.wait()

    def cut(batch):
        for slot in slots[batch]:
            cut_into(d_ref.at[slot], raw_ref.at[slot], start_ref, sizes)

    def transform(batch):
        first = slots[batch][0]

        def source(i):
            return d_ref[first + i // quads].reshape(quads * width, 4 * width)

        forward(source, q_ref, e_ref, right_ref, left_ref, first * quads, len(slots[batch]) * quads, width)

    arrive(0)
    cut(0)
    arrive(1)
    transform(0)
    cut(1)
    arrive(2)
    transform(1)
    cut(2)
    transform(2)
    kept = slots[2][0] * quads
    own = copies.start(q_ref.at[kept : kept + groups + quads], q_out)
    e_out[...] = e_ref[kept : kept + groups + quads]
    scales = factors(e_ref, 0, inner, ones_ref, width) * factors(e_ref, inner, inner, ones_ref, width)
    sum_ref[...] = jnp.zeros_like(sum_ref)
    backward(lambda i: q_ref[i], lambda i: q_ref[inner + i], scales, sum_ref, back_ref, left_ref, inner, width)
    strength, across, along = finish(sum_ref, sums_ref)
    place_ref[...] = jnp.zeros_like(place_ref)
    place_ref[0:2, 0:rows] = position_ref[0, 0]
    place_ref[2:3, 0:rows] = col_ref[0]
    place_ref[3:4, 0:rows] = row_ref[0]
    lane = lax.broadcasted_iota(jnp.int32, (8, 128), 1)
    row = lax.broadcasted_iota(jnp.int32, (8, 128), 0)
    packet = pack(strength, across, along, SOUTH, D_SOUTH)
    for field, where in enumerate((POSITION, POSITION + 1, COL, ROW)):
        value = jnp.where(lane == row, place_ref[field : field + 1, :], 0.0)
        packet = packet + jnp.where(lane == where, jnp.sum(value, axis=1, keepdims=True), 0.0)
    out_ref[...] = packet
    own.wait()


def east_kernel(sizes, rows, received_ref, rim_ref, q_own, e_own, south_ref, right_ref, back_ref, left_ref, sums_ref, ones_ref, out_ref, q_ref, e_ref, sum_ref, sems):
    width, cell, count = sizes
    quads = count // 4
    groups = rows * quads
    own = Copies(sems).start(q_own, q_ref.at[0])

    def source(i):
        value = rim_ref[0] if i < quads else received_ref[i // quads - 1]
        return value.reshape(quads * width, 4 * width)

    forward(source, q_ref.at[1], e_ref, right_ref, left_ref, 0, quads + groups, width)
    scales = factors(e_ref, 0, quads + groups, ones_ref, width) * factors(e_own, 0, quads + groups, ones_ref, width)
    own.wait()
    odd = lax.rem(lax.axis_index("gy"), 2)
    sum_ref[...] = jnp.zeros_like(sum_ref)
    backward(
        lambda i: q_ref[0 if i < quads else odd, i],
        lambda i: q_ref[1 if i < quads else 1 - odd, i],
        scales,
        sum_ref,
        back_ref,
        left_ref,
        quads + groups,
        width,
    )
    strength, across, along = finish(sum_ref, sums_ref)
    row = lax.broadcasted_iota(jnp.int32, (8, 128), 0)

    def only(value, keep):
        return jnp.where(keep, value, 0.0)

    rim = [only(pltpu.roll(value, rows - 1, 0), row == rows - 1) for value in (strength, across, along)]
    east = [only(pltpu.roll(value, 7, 0), row < rows) for value in (strength, across, along)]
    packet = south_ref[...] + pack(*rim, SOUTH, D_SOUTH) + pack(*east, EAST, D_EAST)
    out_ref[...] = jnp.broadcast_to(packet[None], out_ref.shape)


def turned(value, by):
    count = value.shape[0]
    by = by % count
    return value if by == 0 else jnp.concatenate([value[by:], value[:by]], axis=0)


def relax_kernel(counts, rows, patches, all_ref, shift_ref, placed_ref, x_ref):
    nx, nz, ny = counts
    total = nx * nz * ny
    packet = all_ref[...]
    sub = lax.broadcasted_iota(jnp.int32, packet.shape, 1)
    device = lax.broadcasted_iota(jnp.int32, packet.shape, 0)
    gx, gz, gy = device // (nz * ny), device // ny % nz, device % ny

    def field(where):
        return pltpu.roll(packet, 128 - where, 2)

    def one(where):
        return jnp.broadcast_to(packet[:, :, where : where + 1], packet.shape)

    def east(value):
        return turned(value, nz * ny)

    def west(value):
        return turned(value, -nz * ny)

    def south(value):
        inside = pltpu.roll(value, 7, 1)
        beyond = pltpu.roll(turned(value, 1), rows - 1, 1)
        return jnp.where(sub == rows - 1, beyond, inside)

    def north(value):
        inside = pltpu.roll(value, 1, 1)
        beyond = pltpu.roll(turned(value, -1), 8 - (rows - 1), 1)
        return jnp.where(sub == 0, beyond, inside)

    x = field(POSITION)
    d_east = field(D_EAST)
    d_east = jnp.where(gy % 2 == 0, d_east, east(d_east))
    d_south = field(D_SOUTH)
    ke = jnp.where(gx < nx - 1, one(COL), 0.0)
    ks = jnp.where((gy == ny - 1) & (sub == rows - 1), 0.0, one(ROW))
    kw, d_west = west(ke), west(d_east)
    kn, d_north = north(ks), north(d_south)
    has_next = jnp.where(gz < nz - 1, LINK_STIFF, 0.0)
    has_prev = jnp.where(gz > 0, LINK_STIFF, 0.0)
    for _ in range(ITERS):
        force = ke * (east(x) - x - d_east) - kw * (x - west(x) - d_west)
        force = force + ks * (south(x) - x - d_south) - kn * (x - north(x) - d_north)
        force = force + has_next * (turned(x, ny) - x) + has_prev * (turned(x, -ny) - x)
        x = x + STEP_SIZE * force
    x_ref[...] = x
    mine = lax.axis_index("gy")
    me = (lax.axis_index("gx") * nz + lax.axis_index("gz")) * ny + mine
    holder = lax.rem(me + lax.rem(mine, 2) * (nz * ny), total)
    lane = lax.broadcasted_iota(jnp.int32, (8, 128), 1)
    row = lax.broadcasted_iota(jnp.int32, (8, 128), 0)
    own = x_ref[me]
    for part in range(2):
        value = jnp.where((lane == row) & (row < rows), own[:, part : part + 1], 0.0)
        placed_ref[0, 0, part : part + 1, :] = jnp.sum(value, axis=0, keepdims=True)[:, :rows]
    for kind, (source, where) in enumerate(((all_ref[holder], EAST), (all_ref[me], SOUTH))):
        for part in range(2):
            value = source
            if where + part * patches:
                value = pltpu.roll(source, 128 - where - part * patches, 1)
            for tile in range(rows):
                shift_ref[0, tile, 0, kind, part : part + 1, :] = value[tile : tile + 1, :patches]


def to_pair_owner(block):
    nx, ny = lax.axis_size("gx"), lax.axis_size("gy")
    route = []
    for x in range(nx):
        for y in range(ny):
            target = x - 1 if y % 2 == 0 else x + 1
            if 0 <= target < nx:
                route.append((x * ny + y, target * ny + y))
    return lax.ppermute(block, ("gx", "gy"), route)


def to_north(block):
    return lax.ppermute(block, "gy", [(i, i - 1) for i in range(1, lax.axis_size("gy"))])


def shards(east_strip, west_strip, north_strip, south_strip, patch_start, segment_offset, col_stiffness, row_stiffness):
    _, rows, _, width, length = east_strip.shape
    count = patch_start.shape[0]
    sizes = (width, length // count, count)
    quads = count // 4
    span = 4 * width
    groups = rows * quads
    counts = tuple(lax.axis_size(axis) for axis in PART)
    total = math.prod(counts)
    constants = [jnp.asarray(table) for table in tables(width)]
    vmem = pl.BlockSpec(memory_space=pltpu.VMEM)
    hbm = pl.BlockSpec(memory_space=pl.ANY)

    send, rim_cut = pl.pallas_call(
        functools.partial(cut_kernel, sizes, rows),
        out_shape=[
            jax.ShapeDtypeStruct((rows, quads, width, span), BF16),
            jax.ShapeDtypeStruct((1, quads, width, span), BF16),
        ],
        in_specs=[hbm] * 4,
        out_specs=[vmem, vmem],
        scratch_shapes=[
            pltpu.SMEM((count,), jnp.int32),
            pltpu.VMEM((rows + 1, width, length), BF16),
            pltpu.SemaphoreType.DMA((rows + 2,)),
        ],
        compiler_params=pltpu.CompilerParams(vmem_limit_bytes=CUT_VMEM),
        name="cut",
    )(patch_start, west_strip, east_strip, north_strip)
    received = to_pair_owner(send)
    rim = to_north(rim_cut)

    sums = pltpu.VMEM((3, quads, 8, span), F32)
    kept = groups + quads
    south, q_own, e_own = pl.pallas_call(
        functools.partial(south_kernel, sizes, rows),
        out_shape=[
            jax.ShapeDtypeStruct((8, 128), F32),
            jax.ShapeDtypeStruct((kept, width, span), F32),
            jax.ShapeDtypeStruct((kept, span // 2), F32),
        ],
        in_specs=[hbm] * 5 + [vmem] * 8,
        out_specs=[vmem, hbm, vmem],
        scratch_shapes=[
            pltpu.SMEM((count,), jnp.int32),
            pltpu.VMEM((3 * rows - 1, width, length), BF16),
            pltpu.VMEM((3 * rows - 1, quads, width, span), BF16),
            pltpu.VMEM((3 * groups - quads, width, span), F32),
            pltpu.VMEM((3 * groups - quads, span // 2), F32),
            sums,
            pltpu.VMEM((8, 128), F32),
            pltpu.SemaphoreType.DMA((3 * rows + 1,)),
        ],
        compiler_params=pltpu.CompilerParams(vmem_limit_bytes=SOUTH_VMEM),
        cost_estimate=pl.CostEstimate(flops=1_000, bytes_accessed=1_000, transcendentals=0),
        name="south",
    )(
        patch_start,
        south_strip,
        north_strip,
        east_strip,
        west_strip,
        jnp.transpose(segment_offset, (0, 2, 3, 1)),
        jnp.transpose(col_stiffness, (0, 2, 1)),
        jnp.transpose(row_stiffness, (0, 2, 1)),
        *constants,
    )
    packet = pl.pallas_call(
        functools.partial(east_kernel, sizes, rows),
        out_shape=jax.ShapeDtypeStruct((total, 8, 128), F32),
        in_specs=[vmem, vmem, hbm] + [vmem] * 7,
        out_specs=vmem,
        scratch_shapes=[
            pltpu.VMEM((2, kept, width, span), F32),
            pltpu.VMEM((kept, span // 2), F32),
            sums,
            pltpu.SemaphoreType.DMA((1,)),
        ],
        compiler_params=pltpu.CompilerParams(vmem_limit_bytes=EAST_VMEM),
        cost_estimate=pl.CostEstimate(flops=3_000_000_000, bytes_accessed=2_000_000, transcendentals=0),
        name="east",
    )(received, rim, q_own, e_own, south, *constants)
    gathered = lax.all_to_all(packet, PART, 0, 0)
    patch_shift, placed = pl.pallas_call(
        functools.partial(relax_kernel, counts, rows, count),
        out_shape=[
            jax.ShapeDtypeStruct((1, rows, 1, 2, 2, count), F32),
            jax.ShapeDtypeStruct((1, 1, 2, rows), F32),
        ],
        in_specs=[vmem],
        out_specs=[vmem, vmem],
        scratch_shapes=[pltpu.VMEM((total, 8, 128), F32)],
        compiler_params=pltpu.CompilerParams(vmem_limit_bytes=RELAX_VMEM),
        name="relax",
    )(gathered)
    return patch_shift, jnp.transpose(placed, (0, 3, 1, 2))


def solution(mesh):
    placed = (
        P(("groups", "gz"), "gy", "gx", None, None),
        P(("groups", "gz"), "gy", "gx", None, None),
        P(("groups", "gz"), "gy", "gx", None, None),
        P(("groups", "gz"), "gy", "gx", None, None),
        P(),
        P(("groups", "gz"), "gy", "gx", None),
        P(("groups", "gz"), "gy", "gx"),
        P(("groups", "gz"), "gy", "gx"),
    )
    return jax.shard_map(
        shards,
        mesh=mesh,
        in_specs=placed,
        out_specs=(
            P(("groups", "gz"), "gy", "gx", None, None, None),
            P(("groups", "gz"), "gy", "gx", None),
        ),
        check_vma=False,
    )
```

```python
import functools
import math

import jax
import jax.numpy as jnp
import numpy as np
from jax import lax
from jax.experimental import pallas as pl
from jax.experimental.pallas import tpu as pltpu
from jax.sharding import PartitionSpec as P

ITERS = 3
EPS_VAR = 1e-05
EPS_WEIGHT = 1e-06
STEP_SIZE = 0.12
LINK_STIFF = 0.5
F32 = jnp.float32
BF16 = jnp.bfloat16
PART = ("gx", "gz", "gy")
MIB = 1024 * 1024
CUT_VMEM, SOUTH_VMEM, EAST_VMEM, RELAX_VMEM = 62 * MIB, 52 * MIB, 52 * MIB, 16 * MIB

EAST, SOUTH = 0, 32
D_SOUTH, D_EAST, POSITION, COL, ROW = 64, 66, 68, 70, 71


def waves(width):
    quarter = width // 4
    first = np.cos(2.0 * np.pi * np.arange(quarter + 1) / width)
    first[quarter] = 0.0
    cosine = np.zeros(width)
    cosine[: quarter + 1] = first
    cosine[quarter : 2 * quarter + 1] = -first[::-1]
    cosine[2 * quarter :] = -cosine[: 2 * quarter]
    return cosine, np.roll(cosine, quarter)


def basis(width):
    cosine, sine = waves(width)
    half = width // 2
    phase = np.arange(half)[:, None] * np.arange(width)[None, :] % width
    low, high = cosine[phase], sine[phase]
    high[0] = cosine[half * np.arange(width) % width]
    return np.concatenate([low, high], axis=0)


def two_terms(table):
    high = table.astype(np.float32).astype(jnp.bfloat16)
    low = (table - high.astype(np.float64)).astype(np.float32).astype(jnp.bfloat16)
    return high, low


def spread(table, width):
    half = width // 2
    wide = np.zeros((4, width, 2, 4, half))
    for patch in range(4):
        for side in range(2):
            wide[patch, :, side, patch, :] = table[:, side * half : (side + 1) * half]
    return wide.reshape(4 * width, 4 * width)


def tables(width):
    plain = basis(width)
    half = width // 2
    norm = np.full((width, 1), math.sqrt(2.0 / width))
    norm[0] = norm[half] = math.sqrt(1.0 / width)
    unit = plain * norm
    right = np.concatenate(two_terms(spread(unit.T, width)), axis=0)
    right_back = np.concatenate(two_terms(spread(plain.T, width).T), axis=0)
    lefts = []
    for table in (unit, plain.T):
        high, low = two_terms(table)
        lefts.append(np.concatenate([high, high, low], axis=1))
    energy = np.full(width, width / 2.0)
    energy[0] = energy[half] = width
    signed = np.where(np.arange(width) < half, np.arange(width), np.arange(width) - width) * (width / 2.0)
    slot_sum = np.zeros((2, 4, half, 128))
    place_sum = np.zeros((4, width, 128))
    for patch in range(4):
        for side in range(2):
            slot_sum[side, patch, :, patch] = energy[side * half : (side + 1) * half]
        place_sum[patch, :, patch] = signed
    sums = np.concatenate([slot_sum.reshape(4 * width, 128), place_sum.reshape(4 * width, 128)], axis=1)
    sums = sums / float(width) ** 4
    ones = np.kron(np.eye(4), np.ones((half, half)))
    return (right, right_back, np.stack(lefts), sums.astype(jnp.bfloat16), ones.astype(jnp.bfloat16))


def dot(left, right):
    return jnp.dot(left, right, preferred_element_type=F32)


def split(value):
    high = value.astype(BF16)
    return high, (value - high.astype(F32)).astype(BF16)


def split3(value):
    high = value.astype(BF16)
    rest = value - high.astype(F32)
    middle = rest.astype(BF16)
    return high, middle, (rest - middle.astype(F32)).astype(BF16)


def exact_dot(value, table):
    rows = value.shape[0]
    high, middle, low = split3(value)
    out = dot(jnp.concatenate([high, middle, low], axis=0), table)
    return out[:rows] + out[rows : 2 * rows] + out[2 * rows :]


def cut_tile(start_ref, load, store, width, cell, count):
    lane = lax.broadcasted_iota(jnp.int32, (width, cell), 1)
    for pair in range(count // 2):
        parts = []
        for odd in range(2):
            k = 2 * pair + odd
            offset = start_ref[k] - k * cell
            turn = lax.rem(cell + odd * width - offset, cell)
            parts.append(pltpu.roll(load(k).astype(F32), turn, 1))
        store(pair // 2, pair % 2, jnp.where(lane < width, parts[0], parts[1]).astype(BF16))


def forward(source, q_ref, e_ref, right_ref, left_ref, first, groups, width):
    span = 4 * width
    lane = lax.broadcasted_iota(jnp.int32, (8, span // 2), 1)
    row = lax.broadcasted_iota(jnp.int32, (8, span // 2), 0)
    keep = jnp.where((row == 0) & (lane % (width // 2) == 0), 0.0, 1.0)
    step = 4
    for i in range(0, groups, step):
        data = source(i)
        y = dot(jnp.concatenate([data, data], axis=1), right_ref[...])
        high, low = split(y)
        for j in range(step):
            rows = slice(j * width, (j + 1) * width)
            stack = jnp.concatenate([high[rows], low[rows], high[rows]], axis=0)
            q = dot(left_ref[0], stack)
            index = first + i + j
            head = q[0:8, : span // 2] * keep
            q_ref[index, 0:8, 0 : span // 2] = head
            q_ref[index, 0:8, span // 2 :] = q[0:8, span // 2 :]
            q_ref[index, 8:width, :] = q[8:width]
            squares = head * head
            for r in range(8, width, 8):
                squares = squares + q[r : r + 8, : span // 2] * q[r : r + 8, : span // 2]
            for r in range(0, width, 8):
                squares = squares + q[r : r + 8, span // 2 :] * q[r : r + 8, span // 2 :]
            e_ref[pl.ds(index, 1), :] = jnp.sum(squares, axis=0, keepdims=True)


def products(f, g, width):
    half = width // 2
    span = 2 * width
    lane = lax.broadcasted_iota(jnp.int32, (8, span), 1)
    row = lax.broadcasted_iota(jnp.int32, (8, span), 0)
    plain_lane = lane % half != 0
    plain_row = row != 0
    out = [[], [], [], []]
    for r in range(0, half, 8):
        fcc, fcs = f[r : r + 8, :span], f[r : r + 8, span:]
        fsc, fss = f[half + r : half + r + 8, :span], f[half + r : half + r + 8, span:]
        gcc, gcs = g[r : r + 8, :span], g[r : r + 8, span:]
        gsc, gss = g[half + r : half + r + 8, :span], g[half + r : half + r + 8, span:]
        gcc_s = jnp.where(plain_lane, gcc, gcs)
        gsc_s = jnp.where(plain_lane, gsc, gss)
        gcs = jnp.where(plain_lane, gcs, 0.0)
        gss = jnp.where(plain_lane, gss, 0.0)
        hcc, hcs, hcc_s = gcc, gcs, gcc_s
        if r == 0:
            hcc = jnp.where(plain_row, gcc, gsc)
            hcs = jnp.where(plain_row, gcs, gss)
            hcc_s = jnp.where(plain_row, gcc_s, gsc_s)
            gsc = jnp.where(plain_row, gsc, 0.0)
            gss = jnp.where(plain_row, gss, 0.0)
            gsc_s = jnp.where(plain_row, gsc_s, 0.0)
        out[0].append((fcc * gcc + fcs * gcs) + (fsc * gsc + fss * gss))
        out[1].append((fcs * gcc_s - fcc * gcs) + (fss * gsc_s - fsc * gss))
        out[2].append((fsc * hcc + fss * hcs) - (fcc * gsc + fcs * gss))
        out[3].append((fss * hcc_s - fsc * hcs) - (fcs * gsc_s - fcc * gss))
    top = jnp.concatenate([jnp.concatenate(out[0], 0), jnp.concatenate(out[1], 0)], axis=1)
    low = jnp.concatenate([jnp.concatenate(out[2], 0), jnp.concatenate(out[3], 0)], axis=1)
    return jnp.concatenate([top, low], axis=0)


def factors(energies, ones_ref, width):
    energy = exact_dot(energies, ones_ref[...])
    return lax.rsqrt(energy * (1.0 / (width * width)) + EPS_VAR)


def backward(load_f, load_g, scales, sum_ref, right_ref, left_ref, groups, width):
    span = 4 * width
    row = lax.broadcasted_iota(jnp.int32, (8, span), 0)
    special = jnp.where(row == 0, 2.0, 1.0)
    step = 4
    table = right_ref[...]
    table = jnp.concatenate([table[:span], table[:span], table[span:]], axis=0)
    for i in range(0, groups, step):
        highs, lows = [], []
        for j in range(step):
            scale = jnp.broadcast_to(scales[i + j : i + j + 1], (width, span // 2))
            scale = jnp.concatenate([scale, scale], axis=1)
            z = products(load_f(i + j) * scale, load_g(i + j), width)
            high, low = split(z)
            highs.append(high)
            lows.append(low)
        high = jnp.concatenate(highs, axis=0)
        low = jnp.concatenate(lows, axis=0)
        v = dot(jnp.concatenate([high, low, high], axis=1), table)
        for j in range(step):
            u = dot(left_ref[1], jnp.concatenate([highs[j], lows[j], highs[j]], axis=0))
            strength = jnp.zeros((8, span), F32)
            across = jnp.zeros((8, span), F32)
            along = jnp.zeros((8, span), F32)
            for r in range(0, width, 8):
                square = u[r : r + 8] * u[r : r + 8]
                strength = strength + square
                first = r if r < width // 2 else r - width
                across = across + square * (row + first).astype(F32)
                piece = v[j * width + r : j * width + r + 8]
                piece = piece * piece
                if r % (width // 2) == 0:
                    piece = piece * special
                along = along + piece
            tile = i // step
            for kind, value in enumerate((strength, across, along)):
                sum_ref[kind, j, tile : tile + 1, :] = jnp.sum(value, axis=0, keepdims=True)


def finish(sum_ref, sums_ref):
    _, quads, rows, span = sum_ref.shape
    flat = jnp.concatenate([sum_ref[kind, quad] for kind in range(3) for quad in range(quads)], axis=0)
    done = exact_dot(flat, sums_ref[...])
    kinds = []
    for kind in range(3):
        value = jnp.zeros((rows, 128), F32)
        for quad in range(quads):
            base = (kind * quads + quad) * rows
            part = done[base : base + rows, :128] if kind < 2 else done[base : base + rows, 128:]
            value = value + (pltpu.roll(part, 4 * quad, 1) if quad else part)
        kinds.append(value)
    strength, across, along = kinds
    across = across / (strength + EPS_WEIGHT)
    along = along / (strength + EPS_WEIGHT)
    return strength, across, along


def pack(strength, across, along, where, offset):
    lane = lax.broadcasted_iota(jnp.int32, (8, 128), 1)
    total = jnp.sum(strength, axis=1, keepdims=True) + EPS_WEIGHT
    first = jnp.sum(strength * across, axis=1, keepdims=True) / total
    second = jnp.sum(strength * along, axis=1, keepdims=True) / total
    shifts = (pltpu.roll(across, where, 1) if where else across) + pltpu.roll(along, where + 16, 1)
    return shifts + jnp.where(lane == offset, first, 0.0) + jnp.where(lane == offset + 1, second, 0.0)


class Copies:
    def __init__(self, sems):
        self.sems, self.count = sems, 0

    def start(self, source, target):
        copy = pltpu.make_async_copy(source, target, self.sems.at[self.count])
        self.count += 1
        copy.start()
        return copy

    def start_either(self, even, first, second, target):
        sem = self.sems.at[self.count]
        self.count += 1

        @pl.when(even)
        def _():
            pltpu.make_async_copy(first, target, sem).start()

        @pl.when(jnp.logical_not(even))
        def _():
            pltpu.make_async_copy(second, target, sem).start()

        return pltpu.make_async_copy(first, target, sem)


def gx_is_odd():
    return lax.rem(lax.axis_index("gx"), 2)


def cut_into(target, source, start_ref, sizes):
    width, cell, count = sizes

    def load(k):
        return source[:, k * cell : (k + 1) * cell]

    def store(quad, side, value):
        target[quad, :, side * cell : (side + 1) * cell] = value

    cut_tile(start_ref, load, store, width, cell, count)


def cut_kernel(sizes, rows, start_hbm, west_ref, east_ref, north_ref, first_ref, second_ref, rim_ref, start_ref, raw_ref, sems):
    half = rows // 2
    copies = Copies(sems)
    even = gx_is_odd() == 1
    start = copies.start(start_hbm, start_ref)
    loads = []
    for tile in range(rows):
        up, down = west_ref.at[0, tile % half, 0], east_ref.at[0, half + tile % half, 0]
        if tile < half:
            loads.append(copies.start_either(even, down, up, raw_ref.at[tile]))
        else:
            loads.append(copies.start_either(even, up, down, raw_ref.at[tile]))
    loads.append(copies.start(north_ref.at[0, 0, 0], raw_ref.at[rows]))
    start.wait()
    for tile in range(rows + 1):
        loads[tile].wait()
        if tile < half:
            target = first_ref.at[tile]
        else:
            target = second_ref.at[tile - half] if tile < rows else rim_ref.at[0]
        cut_into(target, raw_ref.at[tile], start_ref, sizes)


def south_kernel(sizes, rows, start_hbm, south_ref, north_ref, east_ref, west_ref, position_ref, col_ref, row_ref, right_ref, back_ref, left_ref, sums_ref, ones_ref, out_ref, q_out, e_out, start_ref, raw_ref, d_ref, q_ref, e_ref, sum_ref, place_ref, sems):
    width, cell, count = sizes
    quads = count // 4
    groups = rows * quads
    inner = groups - quads
    copies = Copies(sems)
    batches = [[copies.start(start_hbm, start_ref)], [], []]
    for tile in range(rows - 1):
        batches[0].append(copies.start(south_ref.at[0, tile, 0], raw_ref.at[tile]))
    for tile in range(rows - 1):
        batches[1].append(copies.start(north_ref.at[0, tile + 1, 0], raw_ref.at[rows - 1 + tile]))
    batches[2].append(copies.start(south_ref.at[0, rows - 1, 0], raw_ref.at[2 * rows - 2]))
    for tile in range(rows):
        slot = 2 * rows - 1 + tile
        source = east_ref if tile < rows // 2 else west_ref
        batches[2].append(copies.start(source.at[0, tile, 0], raw_ref.at[slot]))
    slots = [range(0, rows - 1), range(rows - 1, 2 * rows - 2), range(2 * rows - 2, 3 * rows - 1)]

    def arrive(batch):
        for copy in batches[batch]:
            copy.wait()

    def cut(batch):
        for slot in slots[batch]:
            cut_into(d_ref.at[slot], raw_ref.at[slot], start_ref, sizes)

    def transform(batch):
        first = slots[batch][0]

        def source(i):
            return d_ref[first + i // quads].reshape(quads * width, 4 * width)

        forward(source, q_ref, e_ref, right_ref, left_ref, first * quads, len(slots[batch]) * quads, width)

    arrive(0)
    cut(0)
    arrive(1)
    transform(0)
    cut(1)
    arrive(2)
    transform(1)
    cut(2)
    transform(2)
    kept = slots[2][0] * quads
    own = copies.start(q_ref.at[kept : kept + groups + quads], q_out)
    e_out[...] = e_ref[kept : kept + groups + quads]
    scales = factors(e_ref[:inner], ones_ref, width) * factors(e_ref[inner : 2 * inner], ones_ref, width)
    sum_ref[...] = jnp.zeros_like(sum_ref)
    backward(lambda i: q_ref[i], lambda i: q_ref[inner + i], scales, sum_ref, back_ref, left_ref, inner, width)
    strength, across, along = finish(sum_ref, sums_ref)
    place_ref[...] = jnp.zeros_like(place_ref)
    place_ref[0:2, 0:rows] = position_ref[0, 0]
    place_ref[2:3, 0:rows] = col_ref[0]
    place_ref[3:4, 0:rows] = row_ref[0]
    lane = lax.broadcasted_iota(jnp.int32, (8, 128), 1)
    row = lax.broadcasted_iota(jnp.int32, (8, 128), 0)
    packet = pack(strength, across, along, SOUTH, D_SOUTH)
    for field, where in enumerate((POSITION, POSITION + 1, COL, ROW)):
        value = jnp.where(lane == row, place_ref[field : field + 1, :], 0.0)
        packet = packet + jnp.where(lane == where, jnp.sum(value, axis=1, keepdims=True), 0.0)
    out_ref[...] = packet
    own.wait()


def east_kernel(sizes, rows, first_ref, second_ref, rim_ref, q_own, e_own, south_ref, right_ref, back_ref, left_ref, sums_ref, ones_ref, out_ref, q_ref, e_ref, sum_ref, sems):
    width, cell, count = sizes
    quads = count // 4
    groups = rows * quads
    half = groups // 2
    own = Copies(sems).start(q_own, q_ref.at[0])

    def source(i):
        tile = i // quads - 1
        if tile < 0:
            value = rim_ref[0]
        else:
            value = first_ref[tile] if tile < rows // 2 else second_ref[tile - rows // 2]
        return value.reshape(quads * width, 4 * width)

    forward(source, q_ref.at[1], e_ref, right_ref, left_ref, 0, quads + groups, width)
    odd = gx_is_odd()
    from_east, from_west = quads + (1 - odd) * half, quads + odd * half
    has_rim = jnp.where(lax.axis_index("gy") < lax.axis_size("gy") - 1, 1.0, 0.0)
    received = factors(e_ref[...], ones_ref, width)
    e_ref[...] = received
    mine = factors(e_own[...], ones_ref, width)
    scales = jnp.concatenate(
        [
            has_rim * received[:quads] * mine[:quads],
            e_ref[pl.ds(from_east, half), :] * mine[quads : quads + half],
            e_ref[pl.ds(from_west, half), :] * mine[quads + half :],
        ],
        axis=0,
    )
    own.wait()
    sum_ref[...] = jnp.zeros_like(sum_ref)

    def load_first(i):
        return q_ref[0, i] if i < quads + half else q_ref[1, from_west + (i - quads - half)]

    def load_second(i):
        if i < quads:
            return q_ref[1, i]
        return q_ref[1, from_east + (i - quads)] if i < quads + half else q_ref[0, i]

    backward(load_first, load_second, scales, sum_ref, back_ref, left_ref, quads + groups, width)
    strength, across, along = finish(sum_ref, sums_ref)
    row = lax.broadcasted_iota(jnp.int32, (8, 128), 0)

    def only(value, keep):
        return jnp.where(keep, value, 0.0)

    rim = [only(pltpu.roll(value, rows - 1, 0), row == rows - 1) for value in (strength, across, along)]
    east = [only(pltpu.roll(value, 7, 0), row < rows) for value in (strength, across, along)]
    packet = south_ref[...] + pack(*rim, SOUTH, D_SOUTH) + pack(*east, EAST, D_EAST)
    out_ref[...] = jnp.broadcast_to(packet[None, 0 : out_ref.shape[1]], out_ref.shape)


def turned(value, by):
    count = value.shape[0]
    by = by % count
    return value if by == 0 else jnp.concatenate([value[by:], value[:by]], axis=0)


def relax_kernel(counts, rows, patches, all_ref, shift_ref, placed_ref, x_ref):
    nx, nz, ny = counts
    total = nx * nz * ny
    x_ref[...] = jnp.zeros_like(x_ref)
    x_ref[:, 0:rows, :] = all_ref[...]
    packet = x_ref[...]
    sub = lax.broadcasted_iota(jnp.int32, packet.shape, 1)
    device = lax.broadcasted_iota(jnp.int32, packet.shape, 0)
    gx, gz, gy = device // (nz * ny), device // ny % nz, device % ny

    def field(where):
        return pltpu.roll(packet, 128 - where, 2)

    def one(where):
        return jnp.broadcast_to(packet[:, :, where : where + 1], packet.shape)

    def east(value):
        return turned(value, nz * ny)

    def west(value):
        return turned(value, -nz * ny)

    def south(value):
        inside = pltpu.roll(value, 7, 1)
        beyond = pltpu.roll(turned(value, 1), rows - 1, 1)
        return jnp.where(sub == rows - 1, beyond, inside)

    def north(value):
        inside = pltpu.roll(value, 1, 1)
        beyond = pltpu.roll(turned(value, -1), 8 - (rows - 1), 1)
        return jnp.where(sub == 0, beyond, inside)

    x = field(POSITION)
    d_east = field(D_EAST)
    d_east = jnp.where(sub < rows // 2, d_east, east(d_east))
    d_south = field(D_SOUTH)
    ke = jnp.where(gx < nx - 1, one(COL), 0.0)
    ks = jnp.where((gy == ny - 1) & (sub == rows - 1), 0.0, one(ROW))
    kw, d_west = west(ke), west(d_east)
    kn, d_north = north(ks), north(d_south)
    has_next = jnp.where(gz < nz - 1, LINK_STIFF, 0.0)
    has_prev = jnp.where(gz > 0, LINK_STIFF, 0.0)
    for _ in range(ITERS):
        force = ke * (east(x) - x - d_east) - kw * (x - west(x) - d_west)
        force = force + ks * (south(x) - x - d_south) - kn * (x - north(x) - d_north)
        force = force + has_next * (turned(x, ny) - x) + has_prev * (turned(x, -ny) - x)
        x = x + STEP_SIZE * force
    x_ref[...] = x
    me = (lax.axis_index("gx") * nz + lax.axis_index("gz")) * ny + lax.axis_index("gy")
    holder = lax.rem(me + nz * ny, total)
    lane = lax.broadcasted_iota(jnp.int32, (8, 128), 1)
    row = lax.broadcasted_iota(jnp.int32, (8, 128), 0)
    own = x_ref[me]
    for part in range(2):
        value = jnp.where((lane == row) & (row < rows), own[:, part : part + 1], 0.0)
        placed_ref[0, 0, part : part + 1, :] = jnp.sum(value, axis=0, keepdims=True)[:, :rows]
    mixed = jnp.where(row[:rows] < rows // 2, all_ref[me], all_ref[holder])
    for kind, (source, where) in enumerate(((mixed, EAST), (all_ref[me], SOUTH))):
        for part in range(2):
            value = source
            if where + part * patches:
                value = pltpu.roll(source, 128 - where - part * patches, 1)
            for tile in range(rows):
                shift_ref[0, tile, 0, kind, part : part + 1, :] = value[tile : tile + 1, :patches]


def exchange(block, first):
    route = []
    for low in range(first, lax.axis_size("gx") - 1, 2):
        route += [(low, low + 1), (low + 1, low)]
    return lax.ppermute(block, "gx", route)


def to_north(block):
    count = lax.axis_size("gy")
    route = [(1, 0), (0, 1)] if count == 2 else [(i, i - 1) for i in range(1, count)]
    return lax.ppermute(block, "gy", route)


def shards(east_strip, west_strip, north_strip, south_strip, patch_start, segment_offset, col_stiffness, row_stiffness):
    _, rows, _, width, length = east_strip.shape
    count = patch_start.shape[0]
    sizes = (width, length // count, count)
    quads = count // 4
    span = 4 * width
    groups = rows * quads
    counts = tuple(lax.axis_size(axis) for axis in PART)
    total = math.prod(counts)
    constants = [jnp.asarray(table) for table in tables(width)]
    vmem = pl.BlockSpec(memory_space=pltpu.VMEM)
    hbm = pl.BlockSpec(memory_space=pl.ANY)

    first_cut, second_cut, rim_cut = pl.pallas_call(
        functools.partial(cut_kernel, sizes, rows),
        out_shape=[
            jax.ShapeDtypeStruct((rows // 2, quads, width, span), BF16),
            jax.ShapeDtypeStruct((rows // 2, quads, width, span), BF16),
            jax.ShapeDtypeStruct((1, quads, width, span), BF16),
        ],
        in_specs=[hbm] * 4,
        out_specs=[vmem, vmem, vmem],
        scratch_shapes=[
            pltpu.SMEM((count,), jnp.int32),
            pltpu.VMEM((rows + 1, width, length), BF16),
            pltpu.SemaphoreType.DMA((rows + 2,)),
        ],
        compiler_params=pltpu.CompilerParams(vmem_limit_bytes=CUT_VMEM),
        name="cut",
    )(patch_start, west_strip, east_strip, north_strip)
    first = exchange(first_cut, 1)
    second = exchange(second_cut, 0)
    rim = to_north(rim_cut)

    sums = pltpu.VMEM((3, quads, 8, span), F32)
    kept = groups + quads
    south, q_own, e_own = pl.pallas_call(
        functools.partial(south_kernel, sizes, rows),
        out_shape=[
            jax.ShapeDtypeStruct((8, 128), F32),
            jax.ShapeDtypeStruct((kept, width, span), F32),
            jax.ShapeDtypeStruct((kept, span // 2), F32),
        ],
        in_specs=[hbm] * 5 + [vmem] * 8,
        out_specs=[vmem, hbm, vmem],
        scratch_shapes=[
            pltpu.SMEM((count,), jnp.int32),
            pltpu.VMEM((3 * rows - 1, width, length), BF16),
            pltpu.VMEM((3 * rows - 1, quads, width, span), BF16),
            pltpu.VMEM((3 * groups - quads, width, span), F32),
            pltpu.VMEM((3 * groups - quads, span // 2), F32),
            sums,
            pltpu.VMEM((8, 128), F32),
            pltpu.SemaphoreType.DMA((3 * rows + 1,)),
        ],
        compiler_params=pltpu.CompilerParams(vmem_limit_bytes=SOUTH_VMEM),
        cost_estimate=pl.CostEstimate(flops=1_000, bytes_accessed=1_000, transcendentals=0),
        name="south",
    )(
        patch_start,
        south_strip,
        north_strip,
        east_strip,
        west_strip,
        jnp.transpose(segment_offset, (0, 2, 3, 1)),
        jnp.transpose(col_stiffness, (0, 2, 1)),
        jnp.transpose(row_stiffness, (0, 2, 1)),
        *constants,
    )
    packet = pl.pallas_call(
        functools.partial(east_kernel, sizes, rows),
        out_shape=jax.ShapeDtypeStruct((total, rows, 128), F32),
        in_specs=[vmem, vmem, vmem, hbm] + [vmem] * 7,
        out_specs=vmem,
        scratch_shapes=[
            pltpu.VMEM((2, kept, width, span), F32),
            pltpu.VMEM((kept, span // 2), F32),
            sums,
            pltpu.SemaphoreType.DMA((1,)),
        ],
        compiler_params=pltpu.CompilerParams(vmem_limit_bytes=EAST_VMEM),
        cost_estimate=pl.CostEstimate(flops=1_000, bytes_accessed=1_000, transcendentals=0),
        name="east",
    )(first, second, rim, q_own, e_own, south, *constants)
    gathered = lax.all_to_all(packet, PART, 0, 0)
    patch_shift, placed = pl.pallas_call(
        functools.partial(relax_kernel, counts, rows, count),
        out_shape=[
            jax.ShapeDtypeStruct((1, rows, 1, 2, 2, count), F32),
            jax.ShapeDtypeStruct((1, 1, 2, rows), F32),
        ],
        in_specs=[vmem],
        out_specs=[vmem, vmem],
        scratch_shapes=[pltpu.VMEM((total, 8, 128), F32)],
        compiler_params=pltpu.CompilerParams(vmem_limit_bytes=RELAX_VMEM),
        name="relax",
    )(gathered)
    return patch_shift, jnp.transpose(placed, (0, 3, 1, 2))


def solution(mesh):
    placed = (
        P(("groups", "gz"), "gy", "gx", None, None),
        P(("groups", "gz"), "gy", "gx", None, None),
        P(("groups", "gz"), "gy", "gx", None, None),
        P(("groups", "gz"), "gy", "gx", None, None),
        P(),
        P(("groups", "gz"), "gy", "gx", None),
        P(("groups", "gz"), "gy", "gx"),
        P(("groups", "gz"), "gy", "gx"),
    )
    return jax.shard_map(
        shards,
        mesh=mesh,
        in_specs=placed,
        out_specs=(
            P(("groups", "gz"), "gy", "gx", None, None, None),
            P(("groups", "gz"), "gy", "gx", None),
        ),
        check_vma=False,
    )
```

```python
import functools
import math

import jax
import jax.numpy as jnp
import numpy as np
from jax import lax
from jax.experimental import pallas as pl
from jax.experimental.pallas import tpu as pltpu
from jax.sharding import PartitionSpec as P

ITERS = 3
EPS_VAR = 1e-05
EPS_WEIGHT = 1e-06
STEP_SIZE = 0.12
LINK_STIFF = 0.5
F32 = jnp.float32
BF16 = jnp.bfloat16
PART = ("gx", "gz", "gy")
MIB = 1024 * 1024
CUT_VMEM, SOUTH_VMEM, EAST_VMEM, RELAX_VMEM = 62 * MIB, 52 * MIB, 52 * MIB, 16 * MIB

EAST, SOUTH = 0, 32
D_SOUTH, D_EAST, POSITION, COL, ROW = 64, 66, 68, 70, 71


def waves(width):
    quarter = width // 4
    first = np.cos(2.0 * np.pi * np.arange(quarter + 1) / width)
    first[quarter] = 0.0
    cosine = np.zeros(width)
    cosine[: quarter + 1] = first
    cosine[quarter : 2 * quarter + 1] = -first[::-1]
    cosine[2 * quarter :] = -cosine[: 2 * quarter]
    return cosine, np.roll(cosine, quarter)


def basis(width):
    cosine, sine = waves(width)
    half = width // 2
    phase = np.arange(half)[:, None] * np.arange(width)[None, :] % width
    low, high = cosine[phase], sine[phase]
    high[0] = cosine[half * np.arange(width) % width]
    return np.concatenate([low, high], axis=0)


def two_terms(table):
    high = table.astype(np.float32).astype(jnp.bfloat16)
    low = (table - high.astype(np.float64)).astype(np.float32).astype(jnp.bfloat16)
    return high, low


def spread(table, width):
    half = width // 2
    wide = np.zeros((4, width, 2, 4, half))
    for patch in range(4):
        for side in range(2):
            wide[patch, :, side, patch, :] = table[:, side * half : (side + 1) * half]
    return wide.reshape(4 * width, 4 * width)


def tables(width):
    plain = basis(width)
    half = width // 2
    norm = np.full((width, 1), math.sqrt(2.0 / width))
    norm[0] = norm[half] = math.sqrt(1.0 / width)
    unit = plain * norm
    right = np.concatenate(two_terms(spread(unit.T, width)), axis=0)
    right_back = np.concatenate(two_terms(spread(plain.T, width).T), axis=0)
    lefts = []
    for table in (unit, plain.T):
        high, low = two_terms(table)
        lefts.append(np.concatenate([high, high, low], axis=1))
    energy = np.full(width, width / 2.0)
    energy[0] = energy[half] = width
    signed = np.where(np.arange(width) < half, np.arange(width), np.arange(width) - width) * (width / 2.0)
    slot_sum = np.zeros((2, 4, half, 128))
    place_sum = np.zeros((4, width, 128))
    for patch in range(4):
        for side in range(2):
            slot_sum[side, patch, :, patch] = energy[side * half : (side + 1) * half]
        place_sum[patch, :, patch] = signed
    sums = np.concatenate([slot_sum.reshape(4 * width, 128), place_sum.reshape(4 * width, 128)], axis=1)
    sums = sums / float(width) ** 4
    ones = np.kron(np.eye(4), np.ones((half, half)))
    return (right, right_back, np.stack(lefts), sums.astype(jnp.bfloat16), ones.astype(jnp.bfloat16))


def dot(left, right):
    return jnp.dot(left, right, preferred_element_type=F32)


def split(value):
    high = value.astype(BF16)
    return high, (value - high.astype(F32)).astype(BF16)


def split3(value):
    high = value.astype(BF16)
    rest = value - high.astype(F32)
    middle = rest.astype(BF16)
    return high, middle, (rest - middle.astype(F32)).astype(BF16)


def exact_dot(value, table):
    rows = value.shape[0]
    high, middle, low = split3(value)
    out = dot(jnp.concatenate([high, middle, low], axis=0), table)
    return out[:rows] + out[rows : 2 * rows] + out[2 * rows :]


def cut_tile(start_ref, load, store, width, cell, count):
    lane = lax.broadcasted_iota(jnp.int32, (width, cell), 1)
    for pair in range(count // 2):
        parts = []
        for odd in range(2):
            k = 2 * pair + odd
            offset = start_ref[k] - k * cell
            turn = lax.rem(cell + odd * width - offset, cell)
            parts.append(pltpu.roll(load(k).astype(F32), turn, 1))
        store(pair // 2, pair % 2, jnp.where(lane < width, parts[0], parts[1]).astype(BF16))


def forward(source, q_ref, e_ref, right_ref, left_ref, first, groups, width):
    span = 4 * width
    lane = lax.broadcasted_iota(jnp.int32, (8, span // 2), 1)
    row = lax.broadcasted_iota(jnp.int32, (8, span // 2), 0)
    keep = jnp.where((row == 0) & (lane % (width // 2) == 0), 0.0, 1.0)
    step = 4
    for i in range(0, groups, step):
        data = source(i)
        y = dot(jnp.concatenate([data, data], axis=1), right_ref[...])
        high, low = split(y)
        for j in range(step):
            rows = slice(j * width, (j + 1) * width)
            stack = jnp.concatenate([high[rows], low[rows], high[rows]], axis=0)
            q = dot(left_ref[0], stack)
            index = first + i + j
            head = q[0:8, : span // 2] * keep
            q_ref[index, 0:8, 0 : span // 2] = head
            q_ref[index, 0:8, span // 2 :] = q[0:8, span // 2 :]
            q_ref[index, 8:width, :] = q[8:width]
            squares = head * head
            for r in range(8, width, 8):
                squares = squares + q[r : r + 8, : span // 2] * q[r : r + 8, : span // 2]
            for r in range(0, width, 8):
                squares = squares + q[r : r + 8, span // 2 :] * q[r : r + 8, span // 2 :]
            e_ref[pl.ds(index, 1), :] = jnp.sum(squares, axis=0, keepdims=True)


def products(f, g, width):
    half = width // 2
    span = 2 * width
    lane = lax.broadcasted_iota(jnp.int32, (8, span), 1)
    row = lax.broadcasted_iota(jnp.int32, (8, span), 0)
    plain_lane = lane % half != 0
    plain_row = row != 0
    out = [[], [], [], []]
    for r in range(0, half, 8):
        fcc, fcs = f[r : r + 8, :span], f[r : r + 8, span:]
        fsc, fss = f[half + r : half + r + 8, :span], f[half + r : half + r + 8, span:]
        gcc, gcs = g[r : r + 8, :span], g[r : r + 8, span:]
        gsc, gss = g[half + r : half + r + 8, :span], g[half + r : half + r + 8, span:]
        gcc_s = jnp.where(plain_lane, gcc, gcs)
        gsc_s = jnp.where(plain_lane, gsc, gss)
        gcs = jnp.where(plain_lane, gcs, 0.0)
        gss = jnp.where(plain_lane, gss, 0.0)
        hcc, hcs, hcc_s = gcc, gcs, gcc_s
        if r == 0:
            hcc = jnp.where(plain_row, gcc, gsc)
            hcs = jnp.where(plain_row, gcs, gss)
            hcc_s = jnp.where(plain_row, gcc_s, gsc_s)
            gsc = jnp.where(plain_row, gsc, 0.0)
            gss = jnp.where(plain_row, gss, 0.0)
            gsc_s = jnp.where(plain_row, gsc_s, 0.0)
        out[0].append((fcc * gcc + fcs * gcs) + (fsc * gsc + fss * gss))
        out[1].append((fcs * gcc_s - fcc * gcs) + (fss * gsc_s - fsc * gss))
        out[2].append((fsc * hcc + fss * hcs) - (fcc * gsc + fcs * gss))
        out[3].append((fss * hcc_s - fsc * hcs) - (fcs * gsc_s - fcc * gss))
    top = jnp.concatenate([jnp.concatenate(out[0], 0), jnp.concatenate(out[1], 0)], axis=1)
    low = jnp.concatenate([jnp.concatenate(out[2], 0), jnp.concatenate(out[3], 0)], axis=1)
    return jnp.concatenate([top, low], axis=0)


def factors(energies, ones_ref, width):
    energy = exact_dot(energies, ones_ref[...])
    return lax.rsqrt(energy * (1.0 / (width * width)) + EPS_VAR)


def backward(load_f, load_g, scales, sum_ref, right_ref, left_ref, groups, width, place=None):
    span = 4 * width
    row = lax.broadcasted_iota(jnp.int32, (8, span), 0)
    special = jnp.where(row == 0, 2.0, 1.0)
    step = 4
    table = right_ref[...]
    table = jnp.concatenate([table[:span], table[:span], table[span:]], axis=0)
    for i in range(0, groups, step):
        highs, lows = [], []
        for j in range(step):
            scale = jnp.broadcast_to(scales[i + j : i + j + 1], (width, span // 2))
            scale = jnp.concatenate([scale, scale], axis=1)
            z = products(load_f(i + j) * scale, load_g(i + j), width)
            high, low = split(z)
            highs.append(high)
            lows.append(low)
        high = jnp.concatenate(highs, axis=0)
        low = jnp.concatenate(lows, axis=0)
        v = dot(jnp.concatenate([high, low, high], axis=1), table)
        for j in range(step):
            u = dot(left_ref[1], jnp.concatenate([highs[j], lows[j], highs[j]], axis=0))
            strength = jnp.zeros((8, span), F32)
            across = jnp.zeros((8, span), F32)
            along = jnp.zeros((8, span), F32)
            for r in range(0, width, 8):
                square = u[r : r + 8] * u[r : r + 8]
                strength = strength + square
                first = r if r < width // 2 else r - width
                across = across + square * (row + first).astype(F32)
                piece = v[j * width + r : j * width + r + 8]
                piece = piece * piece
                if r % (width // 2) == 0:
                    piece = piece * special
                along = along + piece
            tile = i // step if place is None else place[i // step]
            for kind, value in enumerate((strength, across, along)):
                sum_ref[kind, j, pl.ds(tile, 1), :] = jnp.sum(value, axis=0, keepdims=True)


def finish(sum_ref, sums_ref):
    _, quads, rows, span = sum_ref.shape
    flat = jnp.concatenate([sum_ref[kind, quad] for kind in range(3) for quad in range(quads)], axis=0)
    done = exact_dot(flat, sums_ref[...])
    kinds = []
    for kind in range(3):
        value = jnp.zeros((rows, 128), F32)
        for quad in range(quads):
            base = (kind * quads + quad) * rows
            part = done[base : base + rows, :128] if kind < 2 else done[base : base + rows, 128:]
            value = value + (pltpu.roll(part, 4 * quad, 1) if quad else part)
        kinds.append(value)
    strength, across, along = kinds
    across = across / (strength + EPS_WEIGHT)
    along = along / (strength + EPS_WEIGHT)
    return strength, across, along


def pack(strength, across, along, where, offset):
    lane = lax.broadcasted_iota(jnp.int32, (8, 128), 1)
    total = jnp.sum(strength, axis=1, keepdims=True) + EPS_WEIGHT
    first = jnp.sum(strength * across, axis=1, keepdims=True) / total
    second = jnp.sum(strength * along, axis=1, keepdims=True) / total
    shifts = (pltpu.roll(across, where, 1) if where else across) + pltpu.roll(along, where + 16, 1)
    return shifts + jnp.where(lane == offset, first, 0.0) + jnp.where(lane == offset + 1, second, 0.0)


class Copies:
    def __init__(self, sems):
        self.sems, self.count = sems, 0

    def start(self, source, target):
        copy = pltpu.make_async_copy(source, target, self.sems.at[self.count])
        self.count += 1
        copy.start()
        return copy

    def start_either(self, even, first, second, target):
        sem = self.sems.at[self.count]
        self.count += 1

        @pl.when(even)
        def _():
            pltpu.make_async_copy(first, target, sem).start()

        @pl.when(jnp.logical_not(even))
        def _():
            pltpu.make_async_copy(second, target, sem).start()

        return pltpu.make_async_copy(first, target, sem)


def gx_is_odd():
    return lax.rem(lax.axis_index("gx"), 2)


def cut_into(target, source, start_ref, sizes):
    width, cell, count = sizes

    def load(k):
        return source[:, k * cell : (k + 1) * cell]

    def store(quad, side, value):
        target[quad, :, side * cell : (side + 1) * cell] = value

    cut_tile(start_ref, load, store, width, cell, count)


def cut_kernel(sizes, rows, start_hbm, west_ref, east_ref, south_ref, first_out, second_out, rim_out, start_ref, raw_ref, cut_ref, sems):
    half = rows // 2
    copies = Copies(sems)
    even = gx_is_odd() == 1
    start = copies.start(start_hbm, start_ref)
    loads = []
    for tile in range(rows):
        up, down = west_ref.at[0, tile % half, 0], east_ref.at[0, half + tile % half, 0]
        if tile < half:
            loads.append(copies.start_either(even, down, up, raw_ref.at[tile]))
        else:
            loads.append(copies.start_either(even, up, down, raw_ref.at[tile]))
    loads.append(copies.start(south_ref.at[0, rows - 1, 0], raw_ref.at[rows]))
    stores = []
    start.wait()
    for tile in range(rows + 1):
        loads[tile].wait()
        cut_into(cut_ref.at[tile], raw_ref.at[tile], start_ref, sizes)
        if tile < half:
            target = first_out.at[tile]
        else:
            target = second_out.at[tile - half] if tile < rows else rim_out.at[0]
        stores.append(copies.start(cut_ref.at[tile], target))
    for store in stores:
        store.wait()


def south_kernel(sizes, rows, start_hbm, south_ref, north_ref, east_ref, west_ref, position_ref, col_ref, row_ref, right_ref, back_ref, left_ref, sums_ref, ones_ref, out_ref, q_out, e_out, start_ref, raw_ref, d_ref, q_ref, e_ref, sum_ref, place_ref, sems):
    width, cell, count = sizes
    quads = count // 4
    groups = rows * quads
    inner = groups - quads
    copies = Copies(sems)
    batches = [[copies.start(start_hbm, start_ref)], [], []]
    for tile in range(rows - 1):
        batches[0].append(copies.start(south_ref.at[0, tile, 0], raw_ref.at[tile]))
    for tile in range(rows - 1):
        batches[1].append(copies.start(north_ref.at[0, tile + 1, 0], raw_ref.at[rows - 1 + tile]))
    for tile in range(rows):
        slot = 2 * rows - 2 + tile
        source = east_ref if tile < rows // 2 else west_ref
        batches[2].append(copies.start(source.at[0, tile, 0], raw_ref.at[slot]))
    batches[2].append(copies.start(north_ref.at[0, 0, 0], raw_ref.at[3 * rows - 2]))
    slots = [range(0, rows - 1), range(rows - 1, 2 * rows - 2), range(2 * rows - 2, 3 * rows - 1)]

    def arrive(batch):
        for copy in batches[batch]:
            copy.wait()

    def cut(batch):
        for slot in slots[batch]:
            cut_into(d_ref.at[slot], raw_ref.at[slot], start_ref, sizes)

    def transform(batch):
        first = slots[batch][0]

        def source(i):
            return d_ref[first + i // quads].reshape(quads * width, 4 * width)

        forward(source, q_ref, e_ref, right_ref, left_ref, first * quads, len(slots[batch]) * quads, width)

    arrive(0)
    cut(0)
    arrive(1)
    transform(0)
    cut(1)
    arrive(2)
    transform(1)
    cut(2)
    transform(2)
    kept = slots[2][0] * quads
    own = copies.start(q_ref.at[kept : kept + groups + quads], q_out)
    e_out[...] = e_ref[kept : kept + groups + quads]
    scales = factors(e_ref[:inner], ones_ref, width) * factors(e_ref[inner : 2 * inner], ones_ref, width)
    sum_ref[...] = jnp.zeros_like(sum_ref)
    backward(lambda i: q_ref[i], lambda i: q_ref[inner + i], scales, sum_ref, back_ref, left_ref, inner, width)
    strength, across, along = finish(sum_ref, sums_ref)
    place_ref[...] = jnp.zeros_like(place_ref)
    place_ref[0:2, 0:rows] = position_ref[0, 0]
    place_ref[2:3, 0:rows] = col_ref[0]
    place_ref[3:4, 0:rows] = row_ref[0]
    lane = lax.broadcasted_iota(jnp.int32, (8, 128), 1)
    row = lax.broadcasted_iota(jnp.int32, (8, 128), 0)
    packet = pack(strength, across, along, SOUTH, D_SOUTH)
    for field, where in enumerate((POSITION, POSITION + 1, COL, ROW)):
        value = jnp.where(lane == row, place_ref[field : field + 1, :], 0.0)
        packet = packet + jnp.where(lane == where, jnp.sum(value, axis=1, keepdims=True), 0.0)
    out_ref[...] = packet
    own.wait()


def east_kernel(sizes, rows, first_ref, second_ref, rim_ref, q_own, e_own, south_ref, right_ref, back_ref, left_ref, sums_ref, ones_ref, out_ref, q_first, q_second, q_rim, e_first, e_second, e_rim, sum_ref, sems):
    width, cell, count = sizes
    quads = count // 4
    half = rows // 2 * quads
    copies = Copies(sems)
    odd = gx_is_odd()
    first, second = pl.multiple_of((1 - odd) * half, half), pl.multiple_of(odd * half, half)
    own = [
        copies.start(q_own.at[pl.ds(first, half)], q_first.at[0]),
        copies.start(q_own.at[pl.ds(second, half)], q_second.at[0]),
        copies.start(q_own.at[2 * half : 2 * half + quads], q_rim.at[0]),
    ]
    sum_ref[...] = jnp.zeros_like(sum_ref)

    def transform(source, q_ref, e_ref, number):
        def data(i):
            return source[i // quads].reshape(quads * width, 4 * width)

        forward(data, q_ref.at[1], e_ref, right_ref, left_ref, 0, number, width)

    def scales(energies, base):
        number = energies.shape[0]
        found = factors(jnp.concatenate([energies, e_own[pl.ds(base, number), :]], axis=0), ones_ref, width)
        return found[:number] * found[number:]

    def correlate(q_ref, mine, factor, place):
        def load_first(i):
            return q_ref[1 - mine, i]

        def load_second(i):
            return q_ref[mine, i]

        backward(load_first, load_second, factor, sum_ref, back_ref, left_ref, factor.shape[0], width, place)

    def work(with_rim):
        transform(first_ref, q_first, e_first, half)
        transform(second_ref, q_second, e_second, half)
        if with_rim:
            transform(rim_ref, q_rim, e_rim, quads)
        first_scales = scales(e_first[...], first)
        second_scales = scales(e_second[...], second)
        for copy in own:
            copy.wait()
        correlate(q_first, odd, first_scales, [(1 - odd) * (rows // 2) + tile for tile in range(rows // 2)])
        correlate(q_second, 1 - odd, second_scales, [odd * (rows // 2) + tile for tile in range(rows // 2)])
        if with_rim:
            correlate(q_rim, 0, scales(e_rim[...], 2 * half), [rows])

    has_rim = lax.axis_index("gy") > 0

    @pl.when(has_rim)
    def _():
        work(True)

    @pl.when(jnp.logical_not(has_rim))
    def _():
        work(False)

    found = finish(sum_ref, sums_ref)
    row = lax.broadcasted_iota(jnp.int32, (8, 128), 0)
    east = [jnp.where(row < rows, value, 0.0) for value in found]
    rim = [jnp.where(row == rows - 1, pltpu.roll(value, 7, 0), 0.0) for value in found]
    packet = south_ref[...] + pack(*rim, SOUTH, D_SOUTH) + pack(*east, EAST, D_EAST)
    out_ref[...] = jnp.broadcast_to(packet[None, 0 : out_ref.shape[1]], out_ref.shape)


def turned(value, by):
    count = value.shape[0]
    by = by % count
    return value if by == 0 else jnp.concatenate([value[by:], value[:by]], axis=0)


def relax_kernel(counts, rows, patches, all_ref, shift_ref, placed_ref, x_ref):
    nx, nz, ny = counts
    total = nx * nz * ny
    x_ref[...] = jnp.zeros_like(x_ref)
    x_ref[:, 0:rows, :] = all_ref[...]
    packet = x_ref[...]
    sub = lax.broadcasted_iota(jnp.int32, packet.shape, 1)
    device = lax.broadcasted_iota(jnp.int32, packet.shape, 0)
    gx, gz, gy = device // (nz * ny), device // ny % nz, device % ny

    def field(where):
        return pltpu.roll(packet, 128 - where, 2)

    def one(where):
        return jnp.broadcast_to(packet[:, :, where : where + 1], packet.shape)

    def east(value):
        return turned(value, nz * ny)

    def west(value):
        return turned(value, -nz * ny)

    def south(value):
        inside = pltpu.roll(value, 7, 1)
        beyond = pltpu.roll(turned(value, 1), rows - 1, 1)
        return jnp.where(sub == rows - 1, beyond, inside)

    def north(value):
        inside = pltpu.roll(value, 1, 1)
        beyond = pltpu.roll(turned(value, -1), 8 - (rows - 1), 1)
        return jnp.where(sub == 0, beyond, inside)

    x = field(POSITION)
    d_east = field(D_EAST)
    d_east = jnp.where(sub < rows // 2, d_east, east(d_east))
    d_south = field(D_SOUTH)
    d_south = jnp.where(sub < rows - 1, d_south, turned(d_south, 1))
    ke = jnp.where(gx < nx - 1, one(COL), 0.0)
    ks = jnp.where((gy == ny - 1) & (sub == rows - 1), 0.0, one(ROW))
    kw, d_west = west(ke), west(d_east)
    kn, d_north = north(ks), north(d_south)
    has_next = jnp.where(gz < nz - 1, LINK_STIFF, 0.0)
    has_prev = jnp.where(gz > 0, LINK_STIFF, 0.0)
    for _ in range(ITERS):
        force = ke * (east(x) - x - d_east) - kw * (x - west(x) - d_west)
        force = force + ks * (south(x) - x - d_south) - kn * (x - north(x) - d_north)
        force = force + has_next * (turned(x, ny) - x) + has_prev * (turned(x, -ny) - x)
        x = x + STEP_SIZE * force
    x_ref[...] = x
    me = (lax.axis_index("gx") * nz + lax.axis_index("gz")) * ny + lax.axis_index("gy")
    holder, below = lax.rem(me + nz * ny, total), lax.rem(me + 1, total)
    lane = lax.broadcasted_iota(jnp.int32, (8, 128), 1)
    row = lax.broadcasted_iota(jnp.int32, (8, 128), 0)
    own = x_ref[me]
    for part in range(2):
        value = jnp.where((lane == row) & (row < rows), own[:, part : part + 1], 0.0)
        placed_ref[0, 0, part : part + 1, :] = jnp.sum(value, axis=0, keepdims=True)[:, :rows]
    row, own = row[:rows], all_ref[me]
    easts = jnp.where(row < rows // 2, own, all_ref[holder])
    souths = jnp.where(row < rows - 1, own, all_ref[below])
    for kind, (source, where) in enumerate(((easts, EAST), (souths, SOUTH))):
        for part in range(2):
            value = source
            if where + part * patches:
                value = pltpu.roll(source, 128 - where - part * patches, 1)
            for tile in range(rows):
                shift_ref[0, tile, 0, kind, part : part + 1, :] = value[tile : tile + 1, :patches]


def exchange(block, first):
    route = []
    for low in range(first, lax.axis_size("gx") - 1, 2):
        route += [(low, low + 1), (low + 1, low)]
    return lax.ppermute(block, "gx", route)


def to_south(block):
    count = lax.axis_size("gy")
    route = [(0, 1), (1, 0)] if count == 2 else [(i - 1, i) for i in range(1, count)]
    return lax.ppermute(block, "gy", route)


def shards(east_strip, west_strip, north_strip, south_strip, patch_start, segment_offset, col_stiffness, row_stiffness):
    _, rows, _, width, length = east_strip.shape
    count = patch_start.shape[0]
    sizes = (width, length // count, count)
    quads = count // 4
    span = 4 * width
    groups = rows * quads
    counts = tuple(lax.axis_size(axis) for axis in PART)
    total = math.prod(counts)
    constants = [jnp.asarray(table) for table in tables(width)]
    vmem = pl.BlockSpec(memory_space=pltpu.VMEM)
    hbm = pl.BlockSpec(memory_space=pl.ANY)

    first_cut, second_cut, rim_cut = pl.pallas_call(
        functools.partial(cut_kernel, sizes, rows),
        out_shape=[
            jax.ShapeDtypeStruct((rows // 2, quads, width, span), BF16),
            jax.ShapeDtypeStruct((rows // 2, quads, width, span), BF16),
            jax.ShapeDtypeStruct((1, quads, width, span), BF16),
        ],
        in_specs=[hbm] * 4,
        out_specs=[hbm, hbm, hbm],
        scratch_shapes=[
            pltpu.SMEM((count,), jnp.int32),
            pltpu.VMEM((rows + 1, width, length), BF16),
            pltpu.VMEM((rows + 1, quads, width, span), BF16),
            pltpu.SemaphoreType.DMA((2 * rows + 3,)),
        ],
        compiler_params=pltpu.CompilerParams(vmem_limit_bytes=CUT_VMEM),
        name="cut",
    )(patch_start, west_strip, east_strip, south_strip)
    first = exchange(first_cut, 1)
    second = exchange(second_cut, 0)
    rim = to_south(rim_cut)

    sums = pltpu.VMEM((3, quads, 8, span), F32)
    kept = groups + quads
    south, q_own, e_own = pl.pallas_call(
        functools.partial(south_kernel, sizes, rows),
        out_shape=[
            jax.ShapeDtypeStruct((8, 128), F32),
            jax.ShapeDtypeStruct((kept, width, span), F32),
            jax.ShapeDtypeStruct((kept, span // 2), F32),
        ],
        in_specs=[hbm] * 5 + [vmem] * 8,
        out_specs=[vmem, hbm, vmem],
        scratch_shapes=[
            pltpu.SMEM((count,), jnp.int32),
            pltpu.VMEM((3 * rows - 1, width, length), BF16),
            pltpu.VMEM((3 * rows - 1, quads, width, span), BF16),
            pltpu.VMEM((3 * groups - quads, width, span), F32),
            pltpu.VMEM((3 * groups - quads, span // 2), F32),
            sums,
            pltpu.VMEM((8, 128), F32),
            pltpu.SemaphoreType.DMA((3 * rows + 1,)),
        ],
        compiler_params=pltpu.CompilerParams(vmem_limit_bytes=SOUTH_VMEM),
        cost_estimate=pl.CostEstimate(flops=1_000, bytes_accessed=1_000, transcendentals=0),
        name="south",
    )(
        patch_start,
        south_strip,
        north_strip,
        east_strip,
        west_strip,
        jnp.transpose(segment_offset, (0, 2, 3, 1)),
        jnp.transpose(col_stiffness, (0, 2, 1)),
        jnp.transpose(row_stiffness, (0, 2, 1)),
        *constants,
    )
    packet = pl.pallas_call(
        functools.partial(east_kernel, sizes, rows),
        out_shape=jax.ShapeDtypeStruct((total, rows, 128), F32),
        in_specs=[vmem, vmem, vmem, hbm] + [vmem] * 7,
        out_specs=vmem,
        scratch_shapes=[
            pltpu.VMEM((2, groups // 2, width, span), F32),
            pltpu.VMEM((2, groups // 2, width, span), F32),
            pltpu.VMEM((2, quads, width, span), F32),
            pltpu.VMEM((groups // 2, span // 2), F32),
            pltpu.VMEM((groups // 2, span // 2), F32),
            pltpu.VMEM((quads, span // 2), F32),
            sums,
            pltpu.SemaphoreType.DMA((3,)),
        ],
        compiler_params=pltpu.CompilerParams(vmem_limit_bytes=EAST_VMEM),
        cost_estimate=pl.CostEstimate(flops=1_000, bytes_accessed=1_000, transcendentals=0),
        name="east",
    )(first, second, rim, q_own, e_own, south, *constants)
    gathered = lax.all_to_all(packet, PART, 0, 0)
    patch_shift, placed = pl.pallas_call(
        functools.partial(relax_kernel, counts, rows, count),
        out_shape=[
            jax.ShapeDtypeStruct((1, rows, 1, 2, 2, count), F32),
            jax.ShapeDtypeStruct((1, 1, 2, rows), F32),
        ],
        in_specs=[vmem],
        out_specs=[vmem, vmem],
        scratch_shapes=[pltpu.VMEM((total, 8, 128), F32)],
        compiler_params=pltpu.CompilerParams(vmem_limit_bytes=RELAX_VMEM),
        name="relax",
    )(gathered)
    return patch_shift, jnp.transpose(placed, (0, 3, 1, 2))


def solution(mesh):
    placed = (
        P(("groups", "gz"), "gy", "gx", None, None),
        P(("groups", "gz"), "gy", "gx", None, None),
        P(("groups", "gz"), "gy", "gx", None, None),
        P(("groups", "gz"), "gy", "gx", None, None),
        P(),
        P(("groups", "gz"), "gy", "gx", None),
        P(("groups", "gz"), "gy", "gx"),
        P(("groups", "gz"), "gy", "gx"),
    )
    return jax.shard_map(
        shards,
        mesh=mesh,
        in_specs=placed,
        out_specs=(
            P(("groups", "gz"), "gy", "gx", None, None, None),
            P(("groups", "gz"), "gy", "gx", None),
        ),
        check_vma=False,
    )
```

```python
import functools
import math

import jax
import jax.numpy as jnp
import numpy as np
from jax import lax
from jax.experimental import pallas as pl
from jax.experimental.pallas import tpu as pltpu
from jax.sharding import PartitionSpec as P

ITERS = 3
EPS_VAR = 1e-05
EPS_WEIGHT = 1e-06
STEP_SIZE = 0.12
LINK_STIFF = 0.5
F32 = jnp.float32
BF16 = jnp.bfloat16
PART = ("gx", "gz", "gy")
MIB = 1024 * 1024
CUT_VMEM, SOUTH_VMEM, EAST_VMEM, RELAX_VMEM = 62 * MIB, 52 * MIB, 52 * MIB, 16 * MIB

EAST, SOUTH = 0, 32
D_SOUTH, D_EAST, POSITION, COL, ROW = 64, 66, 68, 70, 71


def waves(width):
    quarter = width // 4
    first = np.cos(2.0 * np.pi * np.arange(quarter + 1) / width)
    first[quarter] = 0.0
    cosine = np.zeros(width)
    cosine[: quarter + 1] = first
    cosine[quarter : 2 * quarter + 1] = -first[::-1]
    cosine[2 * quarter :] = -cosine[: 2 * quarter]
    return cosine, np.roll(cosine, quarter)


def basis(width):
    cosine, sine = waves(width)
    half = width // 2
    phase = np.arange(half)[:, None] * np.arange(width)[None, :] % width
    low, high = cosine[phase], sine[phase]
    high[0] = cosine[half * np.arange(width) % width]
    return np.concatenate([low, high], axis=0)


def two_terms(table):
    high = table.astype(np.float32).astype(jnp.bfloat16)
    low = (table - high.astype(np.float64)).astype(np.float32).astype(jnp.bfloat16)
    return high, low


def spread(table, width):
    half = width // 2
    wide = np.zeros((4, width, 2, 4, half))
    for patch in range(4):
        for side in range(2):
            wide[patch, :, side, patch, :] = table[:, side * half : (side + 1) * half]
    return wide.reshape(4 * width, 4 * width)


def tables(width):
    plain = basis(width)
    half = width // 2
    norm = np.full((width, 1), math.sqrt(2.0 / width))
    norm[0] = norm[half] = math.sqrt(1.0 / width)
    unit = plain * norm
    right = np.concatenate(two_terms(spread(unit.T, width)), axis=0)
    right_back = np.concatenate(two_terms(spread(plain.T, width).T), axis=0)
    lefts = []
    for table in (unit, plain.T):
        high, low = two_terms(table)
        lefts.append(np.concatenate([high, high, low], axis=1))
    energy = np.full(width, width / 2.0)
    energy[0] = energy[half] = width
    signed = np.where(np.arange(width) < half, np.arange(width), np.arange(width) - width) * (width / 2.0)
    slot_sum = np.zeros((2, 4, half, 128))
    place_sum = np.zeros((4, width, 128))
    for patch in range(4):
        for side in range(2):
            slot_sum[side, patch, :, patch] = energy[side * half : (side + 1) * half]
        place_sum[patch, :, patch] = signed
    sums = np.concatenate([slot_sum.reshape(4 * width, 128), place_sum.reshape(4 * width, 128)], axis=1)
    sums = sums / float(width) ** 4
    ones = np.kron(np.eye(4), np.ones((half, half)))
    return (right, right_back, np.stack(lefts), sums.astype(jnp.bfloat16), ones.astype(jnp.bfloat16))


def dot(left, right):
    return jnp.dot(left, right, preferred_element_type=F32)


def split(value):
    high = value.astype(BF16)
    return high, (value - high.astype(F32)).astype(BF16)


def split3(value):
    high = value.astype(BF16)
    rest = value - high.astype(F32)
    middle = rest.astype(BF16)
    return high, middle, (rest - middle.astype(F32)).astype(BF16)


def exact_dot(value, table):
    rows = value.shape[0]
    high, middle, low = split3(value)
    out = dot(jnp.concatenate([high, middle, low], axis=0), table)
    return out[:rows] + out[rows : 2 * rows] + out[2 * rows :]


def turns_of(start_ref, sizes):
    width, cell, count = sizes
    offsets = [start_ref[k] - k * cell for k in range(count)]
    return [width - offset if k % 2 else (cell - offset) & (cell - 1) for k, offset in enumerate(offsets)]


def cut_into(target, source, turns, sizes):
    width, cell, count = sizes
    lane = lax.broadcasted_iota(jnp.int32, (width, cell), 1)
    for pair in range(count // 2):
        even, odd = (
            pltpu.roll(source[:, k * cell : (k + 1) * cell], turns[k], 1) for k in (2 * pair, 2 * pair + 1)
        )
        side = slice(pair % 2 * cell, (pair % 2 + 1) * cell)
        target[pair // 2, :, side] = jnp.where(lane < width, even, odd)


def forward(source, q_ref, e_ref, right_ref, left_ref, first, groups, width):
    span = 4 * width
    lane = lax.broadcasted_iota(jnp.int32, (8, span // 2), 1)
    row = lax.broadcasted_iota(jnp.int32, (8, span // 2), 0)
    keep = jnp.where((row == 0) & (lane % (width // 2) == 0), 0.0, 1.0)
    step = 4
    for i in range(0, groups, step):
        data = source(i)
        y = dot(jnp.concatenate([data, data], axis=1), right_ref[...])
        high, low = split(y)
        for j in range(step):
            rows = slice(j * width, (j + 1) * width)
            stack = jnp.concatenate([high[rows], low[rows], high[rows]], axis=0)
            q = dot(left_ref[0], stack)
            index = first + i + j
            head = q[0:8, : span // 2] * keep
            q_ref[index, 0:8, 0 : span // 2] = head
            q_ref[index, 0:8, span // 2 :] = q[0:8, span // 2 :]
            q_ref[index, 8:width, :] = q[8:width]
            squares = head * head
            for r in range(8, width, 8):
                squares = squares + q[r : r + 8, : span // 2] * q[r : r + 8, : span // 2]
            for r in range(0, width, 8):
                squares = squares + q[r : r + 8, span // 2 :] * q[r : r + 8, span // 2 :]
            e_ref[pl.ds(index, 1), :] = jnp.sum(squares, axis=0, keepdims=True)


def products(f, g, width):
    half = width // 2
    span = 2 * width
    lane = lax.broadcasted_iota(jnp.int32, (8, span), 1)
    row = lax.broadcasted_iota(jnp.int32, (8, span), 0)
    plain_lane = lane % half != 0
    plain_row = row != 0
    out = [[], [], [], []]
    for r in range(0, half, 8):
        fcc, fcs = f[r : r + 8, :span], f[r : r + 8, span:]
        fsc, fss = f[half + r : half + r + 8, :span], f[half + r : half + r + 8, span:]
        gcc, gcs = g[r : r + 8, :span], g[r : r + 8, span:]
        gsc, gss = g[half + r : half + r + 8, :span], g[half + r : half + r + 8, span:]
        gcc_s = jnp.where(plain_lane, gcc, gcs)
        gsc_s = jnp.where(plain_lane, gsc, gss)
        gcs = jnp.where(plain_lane, gcs, 0.0)
        gss = jnp.where(plain_lane, gss, 0.0)
        hcc, hcs, hcc_s = gcc, gcs, gcc_s
        if r == 0:
            hcc = jnp.where(plain_row, gcc, gsc)
            hcs = jnp.where(plain_row, gcs, gss)
            hcc_s = jnp.where(plain_row, gcc_s, gsc_s)
            gsc = jnp.where(plain_row, gsc, 0.0)
            gss = jnp.where(plain_row, gss, 0.0)
            gsc_s = jnp.where(plain_row, gsc_s, 0.0)
        out[0].append((fcc * gcc + fcs * gcs) + (fsc * gsc + fss * gss))
        out[1].append((fcs * gcc_s - fcc * gcs) + (fss * gsc_s - fsc * gss))
        out[2].append((fsc * hcc + fss * hcs) - (fcc * gsc + fcs * gss))
        out[3].append((fss * hcc_s - fsc * hcs) - (fcs * gsc_s - fcc * gss))
    top = jnp.concatenate([jnp.concatenate(out[0], 0), jnp.concatenate(out[1], 0)], axis=1)
    low = jnp.concatenate([jnp.concatenate(out[2], 0), jnp.concatenate(out[3], 0)], axis=1)
    return jnp.concatenate([top, low], axis=0)


def factors(energies, ones_ref, width):
    energy = exact_dot(energies, ones_ref[...])
    return lax.rsqrt(energy * (1.0 / (width * width)) + EPS_VAR)


def backward(load_f, load_g, scales, sum_ref, right_ref, left_ref, groups, width, place=None):
    span = 4 * width
    row = lax.broadcasted_iota(jnp.int32, (8, span), 0)
    special = jnp.where(row == 0, 2.0, 1.0)
    step = 4
    table = right_ref[...]
    table = jnp.concatenate([table[:span], table[:span], table[span:]], axis=0)
    for i in range(0, groups, step):
        highs, lows = [], []
        for j in range(step):
            scale = jnp.broadcast_to(scales[i + j : i + j + 1], (width, span // 2))
            scale = jnp.concatenate([scale, scale], axis=1)
            z = products(load_f(i + j) * scale, load_g(i + j), width)
            high, low = split(z)
            highs.append(high)
            lows.append(low)
        high = jnp.concatenate(highs, axis=0)
        low = jnp.concatenate(lows, axis=0)
        v = dot(jnp.concatenate([high, low, high], axis=1), table)
        for j in range(step):
            u = dot(left_ref[1], jnp.concatenate([highs[j], lows[j], highs[j]], axis=0))
            strength = jnp.zeros((8, span), F32)
            across = jnp.zeros((8, span), F32)
            along = jnp.zeros((8, span), F32)
            for r in range(0, width, 8):
                square = u[r : r + 8] * u[r : r + 8]
                strength = strength + square
                first = r if r < width // 2 else r - width
                across = across + square * (row + first).astype(F32)
                piece = v[j * width + r : j * width + r + 8]
                piece = piece * piece
                if r % (width // 2) == 0:
                    piece = piece * special
                along = along + piece
            tile = i // step if place is None else place[i // step]
            for kind, value in enumerate((strength, across, along)):
                sum_ref[kind, j, pl.ds(tile, 1), :] = jnp.sum(value, axis=0, keepdims=True)


def finish(sum_ref, sums_ref):
    _, quads, rows, span = sum_ref.shape
    flat = jnp.concatenate([sum_ref[kind, quad] for kind in range(3) for quad in range(quads)], axis=0)
    done = exact_dot(flat, sums_ref[...])
    kinds = []
    for kind in range(3):
        value = jnp.zeros((rows, 128), F32)
        for quad in range(quads):
            base = (kind * quads + quad) * rows
            part = done[base : base + rows, :128] if kind < 2 else done[base : base + rows, 128:]
            value = value + (pltpu.roll(part, 4 * quad, 1) if quad else part)
        kinds.append(value)
    strength, across, along = kinds
    across = across / (strength + EPS_WEIGHT)
    along = along / (strength + EPS_WEIGHT)
    return strength, across, along


def pack(strength, across, along, where, offset):
    lane = lax.broadcasted_iota(jnp.int32, (8, 128), 1)
    total = jnp.sum(strength, axis=1, keepdims=True) + EPS_WEIGHT
    first = jnp.sum(strength * across, axis=1, keepdims=True) / total
    second = jnp.sum(strength * along, axis=1, keepdims=True) / total
    shifts = (pltpu.roll(across, where, 1) if where else across) + pltpu.roll(along, where + 16, 1)
    return shifts + jnp.where(lane == offset, first, 0.0) + jnp.where(lane == offset + 1, second, 0.0)


class Copies:
    def __init__(self, sems):
        self.sems, self.count = sems, 0

    def start(self, source, target):
        copy = pltpu.make_async_copy(source, target, self.sems.at[self.count])
        self.count += 1
        copy.start()
        return copy

    def start_either(self, even, first, second, target):
        sem = self.sems.at[self.count]
        self.count += 1

        @pl.when(even)
        def _():
            pltpu.make_async_copy(first, target, sem).start()

        @pl.when(jnp.logical_not(even))
        def _():
            pltpu.make_async_copy(second, target, sem).start()

        return pltpu.make_async_copy(first, target, sem)


def gx_is_odd():
    return lax.rem(lax.axis_index("gx"), 2)


def cut_kernel(sizes, rows, start_hbm, west_ref, east_ref, south_ref, first_out, second_out, rim_out, start_ref, raw_ref, cut_ref, sems):
    half = rows // 2
    copies = Copies(sems)
    even = gx_is_odd() == 1
    start = copies.start(start_hbm, start_ref)
    loads = []
    for tile in range(rows):
        up, down = west_ref.at[0, tile % half, 0], east_ref.at[0, half + tile % half, 0]
        if tile < half:
            loads.append(copies.start_either(even, down, up, raw_ref.at[tile]))
        else:
            loads.append(copies.start_either(even, up, down, raw_ref.at[tile]))
    loads.append(copies.start(south_ref.at[0, rows - 1, 0], raw_ref.at[rows]))
    stores = []
    start.wait()
    turns = turns_of(start_ref, sizes)
    for tile in range(rows + 1):
        loads[tile].wait()
        cut_into(cut_ref.at[tile], raw_ref.at[tile], turns, sizes)
        if tile < half:
            target = first_out.at[tile]
        else:
            target = second_out.at[tile - half] if tile < rows else rim_out.at[0]
        stores.append(copies.start(cut_ref.at[tile], target))
    for store in stores:
        store.wait()


def south_kernel(sizes, rows, start_hbm, south_ref, north_ref, east_ref, west_ref, position_ref, col_ref, row_ref, right_ref, back_ref, left_ref, sums_ref, ones_ref, out_ref, q_out, e_out, start_ref, raw_ref, d_ref, q_ref, e_ref, sum_ref, place_ref, sems):
    width, cell, count = sizes
    quads = count // 4
    groups = rows * quads
    inner = groups - quads
    copies = Copies(sems)
    batches = [[copies.start(start_hbm, start_ref)], [], []]
    for tile in range(rows - 1):
        batches[0].append(copies.start(south_ref.at[0, tile, 0], raw_ref.at[tile]))
    for tile in range(rows - 1):
        batches[1].append(copies.start(north_ref.at[0, tile + 1, 0], raw_ref.at[rows - 1 + tile]))
    for tile in range(rows):
        slot = 2 * rows - 2 + tile
        source = east_ref if tile < rows // 2 else west_ref
        batches[2].append(copies.start(source.at[0, tile, 0], raw_ref.at[slot]))
    batches[2].append(copies.start(north_ref.at[0, 0, 0], raw_ref.at[3 * rows - 2]))
    slots = [range(0, rows - 1), range(rows - 1, 2 * rows - 2), range(2 * rows - 2, 3 * rows - 1)]

    def arrive(batch):
        for copy in batches[batch]:
            copy.wait()

    def cut(batch):
        for slot in slots[batch]:
            cut_into(d_ref.at[slot], raw_ref.at[slot], turns, sizes)

    def transform(batch):
        first = slots[batch][0]

        def source(i):
            return d_ref[first + i // quads].reshape(quads * width, 4 * width)

        forward(source, q_ref, e_ref, right_ref, left_ref, first * quads, len(slots[batch]) * quads, width)

    arrive(0)
    turns = turns_of(start_ref, sizes)
    cut(0)
    arrive(1)
    transform(0)
    cut(1)
    arrive(2)
    transform(1)
    cut(2)
    transform(2)
    kept = slots[2][0] * quads
    own = copies.start(q_ref.at[kept : kept + groups + quads], q_out)
    e_out[...] = factors(e_ref[kept : kept + groups + quads], ones_ref, width)
    scales = factors(e_ref[:inner], ones_ref, width) * factors(e_ref[inner : 2 * inner], ones_ref, width)
    sum_ref[...] = jnp.zeros_like(sum_ref)
    backward(lambda i: q_ref[i], lambda i: q_ref[inner + i], scales, sum_ref, back_ref, left_ref, inner, width)
    strength, across, along = finish(sum_ref, sums_ref)
    place_ref[...] = jnp.zeros_like(place_ref)
    place_ref[0:2, 0:rows] = position_ref[0, 0]
    place_ref[2:3, 0:rows] = col_ref[0]
    place_ref[3:4, 0:rows] = row_ref[0]
    lane = lax.broadcasted_iota(jnp.int32, (8, 128), 1)
    row = lax.broadcasted_iota(jnp.int32, (8, 128), 0)
    packet = pack(strength, across, along, SOUTH, D_SOUTH)
    for field, where in enumerate((POSITION, POSITION + 1, COL, ROW)):
        value = jnp.where(lane == row, place_ref[field : field + 1, :], 0.0)
        packet = packet + jnp.where(lane == where, jnp.sum(value, axis=1, keepdims=True), 0.0)
    out_ref[...] = packet
    own.wait()


def east_kernel(sizes, rows, first_ref, second_ref, rim_ref, q_own, own_factors, south_ref, right_ref, back_ref, left_ref, sums_ref, ones_ref, out_ref, q_first, q_second, q_rim, e_first, e_second, e_rim, sum_ref, sems):
    width, cell, count = sizes
    quads = count // 4
    half = rows // 2 * quads
    copies = Copies(sems)
    odd = gx_is_odd()
    first, second = pl.multiple_of((1 - odd) * half, half), pl.multiple_of(odd * half, half)
    own = [
        copies.start(q_own.at[pl.ds(first, half)], q_first.at[0]),
        copies.start(q_own.at[pl.ds(second, half)], q_second.at[0]),
        copies.start(q_own.at[2 * half : 2 * half + quads], q_rim.at[0]),
    ]
    sum_ref[...] = jnp.zeros_like(sum_ref)

    def transform(source, q_ref, e_ref, number):
        def data(i):
            return source[i // quads].reshape(quads * width, 4 * width)

        forward(data, q_ref.at[1], e_ref, right_ref, left_ref, 0, number, width)

    def scales(energies, base):
        return factors(energies, ones_ref, width) * own_factors[pl.ds(base, energies.shape[0]), :]

    def correlate(q_ref, mine, factor, place):
        def load_first(i):
            return q_ref[1 - mine, i]

        def load_second(i):
            return q_ref[mine, i]

        backward(load_first, load_second, factor, sum_ref, back_ref, left_ref, factor.shape[0], width, place)

    def work(with_rim):
        transform(first_ref, q_first, e_first, half)
        transform(second_ref, q_second, e_second, half)
        if with_rim:
            transform(rim_ref, q_rim, e_rim, quads)
        first_scales = scales(e_first[...], first)
        second_scales = scales(e_second[...], second)
        for copy in own:
            copy.wait()
        correlate(q_first, odd, first_scales, [(1 - odd) * (rows // 2) + tile for tile in range(rows // 2)])
        correlate(q_second, 1 - odd, second_scales, [odd * (rows // 2) + tile for tile in range(rows // 2)])
        if with_rim:
            correlate(q_rim, 0, scales(e_rim[...], 2 * half), [rows])

    has_rim = lax.axis_index("gy") > 0

    @pl.when(has_rim)
    def _():
        work(True)

    @pl.when(jnp.logical_not(has_rim))
    def _():
        work(False)

    found = finish(sum_ref, sums_ref)
    row = lax.broadcasted_iota(jnp.int32, (8, 128), 0)
    east = [jnp.where(row < rows, value, 0.0) for value in found]
    rim = [jnp.where(row == rows - 1, pltpu.roll(value, 7, 0), 0.0) for value in found]
    packet = south_ref[...] + pack(*rim, SOUTH, D_SOUTH) + pack(*east, EAST, D_EAST)
    out_ref[...] = jnp.broadcast_to(packet[None, 0 : out_ref.shape[1]], out_ref.shape)


def turned(value, by):
    count = value.shape[0]
    by = by % count
    return value if by == 0 else jnp.concatenate([value[by:], value[:by]], axis=0)


def relax_kernel(counts, rows, patches, all_ref, shift_ref, placed_ref, x_ref):
    nx, nz, ny = counts
    column = ny * rows
    every = all_ref[...].reshape(nx * nz, ny, rows, 128)
    for gy in range(ny):
        x_ref[:, gy * rows : (gy + 1) * rows, :] = every[:, gy]
    packet = x_ref[...]
    sub = lax.broadcasted_iota(jnp.int32, packet.shape, 1)
    stack = lax.broadcasted_iota(jnp.int32, packet.shape, 0)
    gx, gz = stack // nz, stack % nz

    def field(where):
        return pltpu.roll(packet, 128 - where, 2)

    def one(where):
        return jnp.broadcast_to(packet[:, :, where : where + 1], packet.shape)

    def east(value):
        return turned(value, nz)

    def west(value):
        return turned(value, -nz)

    def south(value):
        return pltpu.roll(value, column - 1, 1)

    def north(value):
        return pltpu.roll(value, 1, 1)

    x = field(POSITION)
    d_east = field(D_EAST)
    d_east = jnp.where(sub % rows < rows // 2, d_east, east(d_east))
    d_south = field(D_SOUTH)
    d_south = jnp.where(sub % rows < rows - 1, d_south, pltpu.roll(d_south, column - rows, 1))
    ke = jnp.where(gx < nx - 1, one(COL), 0.0)
    ks = jnp.where(sub < column - 1, one(ROW), 0.0)
    kw, d_west = west(ke), west(d_east)
    kn, d_north = north(ks), north(d_south)
    has_next = jnp.where(gz < nz - 1, LINK_STIFF, 0.0)
    has_prev = jnp.where(gz > 0, LINK_STIFF, 0.0)
    for _ in range(ITERS):
        force = ke * (east(x) - x - d_east) - kw * (x - west(x) - d_west)
        force = force + ks * (south(x) - x - d_south) - kn * (x - north(x) - d_north)
        force = force + has_next * (turned(x, 1) - x) + has_prev * (turned(x, -1) - x)
        x = x + STEP_SIZE * force
    x_ref[...] = x
    mine = lax.axis_index("gy")
    place = lax.axis_index("gx") * nz + lax.axis_index("gz")
    me, total = place * ny + mine, nx * nz * ny
    holder, below = lax.rem(me + nz * ny, total), lax.rem(me + 1, total)
    lane = lax.broadcasted_iota(jnp.int32, (column, 128), 1)
    row = lax.broadcasted_iota(jnp.int32, (column, 128), 0)
    own = x_ref[place]
    for part in range(2):
        value = jnp.where((lane < rows) & (lane + mine * rows == row), own[:, part : part + 1], 0.0)
        placed_ref[0, 0, part : part + 1, :] = jnp.sum(value, axis=0, keepdims=True)[:, :rows]
    row, own = row[:rows], all_ref[me]
    easts = jnp.where(row < rows // 2, own, all_ref[holder])
    souths = jnp.where(row < rows - 1, own, all_ref[below])
    for kind, (source, where) in enumerate(((easts, EAST), (souths, SOUTH))):
        for part in range(2):
            value = source
            if where + part * patches:
                value = pltpu.roll(source, 128 - where - part * patches, 1)
            for tile in range(rows):
                shift_ref[0, tile, 0, kind, part : part + 1, :] = value[tile : tile + 1, :patches]


def exchange(block, first):
    route = []
    for low in range(first, lax.axis_size("gx") - 1, 2):
        route += [(low, low + 1), (low + 1, low)]
    return lax.ppermute(block, "gx", route)


def to_south(block):
    count = lax.axis_size("gy")
    route = [(0, 1), (1, 0)] if count == 2 else [(i - 1, i) for i in range(1, count)]
    return lax.ppermute(block, "gy", route)


def shards(east_strip, west_strip, north_strip, south_strip, patch_start, segment_offset, col_stiffness, row_stiffness):
    _, rows, _, width, length = east_strip.shape
    count = patch_start.shape[0]
    sizes = (width, length // count, count)
    quads = count // 4
    span = 4 * width
    groups = rows * quads
    counts = tuple(lax.axis_size(axis) for axis in PART)
    total = math.prod(counts)
    constants = [jnp.asarray(table) for table in tables(width)]
    vmem = pl.BlockSpec(memory_space=pltpu.VMEM)
    hbm = pl.BlockSpec(memory_space=pl.ANY)

    first_cut, second_cut, rim_cut = pl.pallas_call(
        functools.partial(cut_kernel, sizes, rows),
        out_shape=[
            jax.ShapeDtypeStruct((rows // 2, quads, width, span), BF16),
            jax.ShapeDtypeStruct((rows // 2, quads, width, span), BF16),
            jax.ShapeDtypeStruct((1, quads, width, span), BF16),
        ],
        in_specs=[hbm] * 4,
        out_specs=[hbm, hbm, hbm],
        scratch_shapes=[
            pltpu.SMEM((count,), jnp.int32),
            pltpu.VMEM((rows + 1, width, length), BF16),
            pltpu.VMEM((rows + 1, quads, width, span), BF16),
            pltpu.SemaphoreType.DMA((2 * rows + 3,)),
        ],
        compiler_params=pltpu.CompilerParams(vmem_limit_bytes=CUT_VMEM),
        name="cut",
    )(patch_start, west_strip, east_strip, south_strip)
    first = exchange(first_cut, 1)
    second = exchange(second_cut, 0)
    rim = to_south(rim_cut)

    sums = pltpu.VMEM((3, quads, 8, span), F32)
    kept = groups + quads
    south, q_own, e_own = pl.pallas_call(
        functools.partial(south_kernel, sizes, rows),
        out_shape=[
            jax.ShapeDtypeStruct((8, 128), F32),
            jax.ShapeDtypeStruct((kept, width, span), F32),
            jax.ShapeDtypeStruct((kept, span // 2), F32),
        ],
        in_specs=[hbm] * 5 + [vmem] * 8,
        out_specs=[vmem, hbm, vmem],
        scratch_shapes=[
            pltpu.SMEM((count,), jnp.int32),
            pltpu.VMEM((3 * rows - 1, width, length), BF16),
            pltpu.VMEM((3 * rows - 1, quads, width, span), BF16),
            pltpu.VMEM((3 * groups - quads, width, span), F32),
            pltpu.VMEM((3 * groups - quads, span // 2), F32),
            sums,
            pltpu.VMEM((8, 128), F32),
            pltpu.SemaphoreType.DMA((3 * rows + 1,)),
        ],
        compiler_params=pltpu.CompilerParams(vmem_limit_bytes=SOUTH_VMEM),
        cost_estimate=pl.CostEstimate(flops=1_000, bytes_accessed=1_000, transcendentals=0),
        name="south",
    )(
        patch_start,
        south_strip,
        north_strip,
        east_strip,
        west_strip,
        jnp.transpose(segment_offset, (0, 2, 3, 1)),
        jnp.transpose(col_stiffness, (0, 2, 1)),
        jnp.transpose(row_stiffness, (0, 2, 1)),
        *constants,
    )
    packet = pl.pallas_call(
        functools.partial(east_kernel, sizes, rows),
        out_shape=jax.ShapeDtypeStruct((total, rows, 128), F32),
        in_specs=[vmem, vmem, vmem, hbm] + [vmem] * 7,
        out_specs=vmem,
        scratch_shapes=[
            pltpu.VMEM((2, groups // 2, width, span), F32),
            pltpu.VMEM((2, groups // 2, width, span), F32),
            pltpu.VMEM((2, quads, width, span), F32),
            pltpu.VMEM((groups // 2, span // 2), F32),
            pltpu.VMEM((groups // 2, span // 2), F32),
            pltpu.VMEM((quads, span // 2), F32),
            sums,
            pltpu.SemaphoreType.DMA((3,)),
        ],
        compiler_params=pltpu.CompilerParams(vmem_limit_bytes=EAST_VMEM),
        cost_estimate=pl.CostEstimate(flops=1_000, bytes_accessed=1_000, transcendentals=0),
        name="east",
    )(first, second, rim, q_own, e_own, south, *constants)
    gathered = lax.all_to_all(packet, PART, 0, 0)
    patch_shift, placed = pl.pallas_call(
        functools.partial(relax_kernel, counts, rows, count),
        out_shape=[
            jax.ShapeDtypeStruct((1, rows, 1, 2, 2, count), F32),
            jax.ShapeDtypeStruct((1, 1, 2, rows), F32),
        ],
        in_specs=[vmem],
        out_specs=[vmem, vmem],
        scratch_shapes=[pltpu.VMEM((total // counts[2], counts[2] * rows, 128), F32)],
        compiler_params=pltpu.CompilerParams(vmem_limit_bytes=RELAX_VMEM),
        name="relax",
    )(gathered)
    return patch_shift, jnp.transpose(placed, (0, 3, 1, 2))


def solution(mesh):
    placed = (
        P(("groups", "gz"), "gy", "gx", None, None),
        P(("groups", "gz"), "gy", "gx", None, None),
        P(("groups", "gz"), "gy", "gx", None, None),
        P(("groups", "gz"), "gy", "gx", None, None),
        P(),
        P(("groups", "gz"), "gy", "gx", None),
        P(("groups", "gz"), "gy", "gx"),
        P(("groups", "gz"), "gy", "gx"),
    )
    return jax.shard_map(
        shards,
        mesh=mesh,
        in_specs=placed,
        out_specs=(
            P(("groups", "gz"), "gy", "gx", None, None, None),
            P(("groups", "gz"), "gy", "gx", None),
        ),
        check_vma=False,
    )
```

```python
import functools
import math

import jax
import jax.numpy as jnp
import numpy as np
from jax import lax
from jax.experimental import pallas as pl
from jax.experimental.pallas import tpu as pltpu
from jax.sharding import PartitionSpec as P

ITERS = 3
EPS_VAR = 1e-05
EPS_WEIGHT = 1e-06
STEP_SIZE = 0.12
LINK_STIFF = 0.5
F32 = jnp.float32
BF16 = jnp.bfloat16
PART = ("gx", "gz", "gy")
MIB = 1024 * 1024
CUT_VMEM, SOUTH_VMEM, EAST_VMEM, RELAX_VMEM = 62 * MIB, 52 * MIB, 52 * MIB, 16 * MIB

EAST, SOUTH = 0, 32
D_SOUTH, D_EAST, POSITION, COL, ROW = 64, 66, 68, 70, 71


def waves(width):
    quarter = width // 4
    first = np.cos(2.0 * np.pi * np.arange(quarter + 1) / width)
    first[quarter] = 0.0
    cosine = np.zeros(width)
    cosine[: quarter + 1] = first
    cosine[quarter : 2 * quarter + 1] = -first[::-1]
    cosine[2 * quarter :] = -cosine[: 2 * quarter]
    return cosine, np.roll(cosine, quarter)


def basis(width):
    cosine, sine = waves(width)
    half = width // 2
    phase = np.arange(half)[:, None] * np.arange(width)[None, :] % width
    low, high = cosine[phase], sine[phase]
    high[0] = cosine[half * np.arange(width) % width]
    return np.concatenate([low, high], axis=0)


def two_terms(table):
    high = table.astype(np.float32).astype(jnp.bfloat16)
    low = (table - high.astype(np.float64)).astype(np.float32).astype(jnp.bfloat16)
    return high, low


def spread(table, width):
    half = width // 2
    wide = np.zeros((4, width, 2, 4, half))
    for patch in range(4):
        for side in range(2):
            wide[patch, :, side, patch, :] = table[:, side * half : (side + 1) * half]
    return wide.reshape(4 * width, 4 * width)


def tables(width):
    plain = basis(width)
    half = width // 2
    norm = np.full((width, 1), math.sqrt(2.0 / width))
    norm[0] = norm[half] = math.sqrt(1.0 / width)
    unit = plain * norm
    right = np.concatenate(two_terms(spread(unit.T, width)), axis=0)
    right_back = np.concatenate(two_terms(spread(plain.T, width).T), axis=0)
    lefts = []
    for table in (unit, plain.T):
        high, low = two_terms(table)
        lefts.append(np.concatenate([high, high, low], axis=1))
    energy = np.full(width, width / 2.0)
    energy[0] = energy[half] = width
    signed = np.where(np.arange(width) < half, np.arange(width), np.arange(width) - width) * (width / 2.0)
    slot_sum = np.zeros((2, 4, half, 128))
    place_sum = np.zeros((4, width, 128))
    for patch in range(4):
        for side in range(2):
            slot_sum[side, patch, :, patch] = energy[side * half : (side + 1) * half]
        place_sum[patch, :, patch] = signed
    sums = np.concatenate([slot_sum.reshape(4 * width, 128), place_sum.reshape(4 * width, 128)], axis=1)
    sums = sums / float(width) ** 4
    ones = np.kron(np.eye(4), np.ones((half, half)))
    return (right, right_back, np.stack(lefts), sums.astype(jnp.bfloat16), ones.astype(jnp.bfloat16))


def dot(left, right):
    return jnp.dot(left, right, preferred_element_type=F32)


def split(value):
    high = value.astype(BF16)
    return high, (value - high.astype(F32)).astype(BF16)


def split3(value):
    high = value.astype(BF16)
    rest = value - high.astype(F32)
    middle = rest.astype(BF16)
    return high, middle, (rest - middle.astype(F32)).astype(BF16)


def exact_dot(value, table):
    rows = value.shape[0]
    high, middle, low = split3(value)
    out = dot(jnp.concatenate([high, middle, low], axis=0), table)
    return out[:rows] + out[rows : 2 * rows] + out[2 * rows :]


def turns_of(start_ref, sizes):
    width, cell, count = sizes
    offsets = [start_ref[k] - k * cell for k in range(count)]
    return [width - offset if k % 2 else (cell - offset) & (cell - 1) for k, offset in enumerate(offsets)]


def cut_into(target, source, turns, sizes):
    width, cell, count = sizes
    lane = lax.broadcasted_iota(jnp.int32, (width, cell), 1)
    for pair in range(count // 2):
        even, odd = (
            pltpu.roll(source[:, k * cell : (k + 1) * cell], turns[k], 1) for k in (2 * pair, 2 * pair + 1)
        )
        side = slice(pair % 2 * cell, (pair % 2 + 1) * cell)
        target[pair // 2, :, side] = jnp.where(lane < width, even, odd)


def forward(source, q_ref, e_ref, right_ref, left_ref, first, groups, width):
    span = 4 * width
    lane = lax.broadcasted_iota(jnp.int32, (8, span // 2), 1)
    row = lax.broadcasted_iota(jnp.int32, (8, span // 2), 0)
    keep = jnp.where((row == 0) & (lane % (width // 2) == 0), 0.0, 1.0)
    step = 4
    for i in range(0, groups, step):
        data = source(i)
        y = dot(jnp.concatenate([data, data], axis=1), right_ref[...])
        high, low = split(y)
        for j in range(step):
            rows = slice(j * width, (j + 1) * width)
            stack = jnp.concatenate([high[rows], low[rows], high[rows]], axis=0)
            q = dot(left_ref[0], stack)
            index = first + i + j
            head = q[0:8, : span // 2] * keep
            q_ref[index, 0:8, 0 : span // 2] = head
            q_ref[index, 0:8, span // 2 :] = q[0:8, span // 2 :]
            q_ref[index, 8:width, :] = q[8:width]
            squares = head * head
            for r in range(8, width, 8):
                squares = squares + q[r : r + 8, : span // 2] * q[r : r + 8, : span // 2]
            for r in range(0, width, 8):
                squares = squares + q[r : r + 8, span // 2 :] * q[r : r + 8, span // 2 :]
            e_ref[pl.ds(index, 1), :] = jnp.sum(squares, axis=0, keepdims=True)


def products(f, g, width):
    half = width // 2
    span = 2 * width
    lane = lax.broadcasted_iota(jnp.int32, (8, span), 1)
    row = lax.broadcasted_iota(jnp.int32, (8, span), 0)
    plain_lane = lane % half != 0
    plain_row = row != 0
    out = [[], [], [], []]
    for r in range(0, half, 8):
        fcc, fcs = f[r : r + 8, :span], f[r : r + 8, span:]
        fsc, fss = f[half + r : half + r + 8, :span], f[half + r : half + r + 8, span:]
        gcc, gcs = g[r : r + 8, :span], g[r : r + 8, span:]
        gsc, gss = g[half + r : half + r + 8, :span], g[half + r : half + r + 8, span:]
        gcc_s = jnp.where(plain_lane, gcc, gcs)
        gsc_s = jnp.where(plain_lane, gsc, gss)
        gcs = jnp.where(plain_lane, gcs, 0.0)
        gss = jnp.where(plain_lane, gss, 0.0)
        hcc, hcs, hcc_s = gcc, gcs, gcc_s
        if r == 0:
            hcc = jnp.where(plain_row, gcc, gsc)
            hcs = jnp.where(plain_row, gcs, gss)
            hcc_s = jnp.where(plain_row, gcc_s, gsc_s)
            gsc = jnp.where(plain_row, gsc, 0.0)
            gss = jnp.where(plain_row, gss, 0.0)
            gsc_s = jnp.where(plain_row, gsc_s, 0.0)
        out[0].append((fcc * gcc + fcs * gcs) + (fsc * gsc + fss * gss))
        out[1].append((fcs * gcc_s - fcc * gcs) + (fss * gsc_s - fsc * gss))
        out[2].append((fsc * hcc + fss * hcs) - (fcc * gsc + fcs * gss))
        out[3].append((fss * hcc_s - fsc * hcs) - (fcs * gsc_s - fcc * gss))
    top = jnp.concatenate([jnp.concatenate(out[0], 0), jnp.concatenate(out[1], 0)], axis=1)
    low = jnp.concatenate([jnp.concatenate(out[2], 0), jnp.concatenate(out[3], 0)], axis=1)
    return jnp.concatenate([top, low], axis=0)


def factors(energies, ones_ref, width):
    energy = exact_dot(energies, ones_ref[...])
    return lax.rsqrt(energy * (1.0 / (width * width)) + EPS_VAR)


def backward(load_f, load_g, scales, sum_ref, right_ref, left_ref, groups, width, place=None):
    span = 4 * width
    row = lax.broadcasted_iota(jnp.int32, (8, span), 0)
    special = jnp.where(row == 0, 2.0, 1.0)
    step = 4
    table = right_ref[...]
    table = jnp.concatenate([table[:span], table[:span], table[span:]], axis=0)
    for i in range(0, groups, step):
        highs, lows = [], []
        for j in range(step):
            scale = jnp.broadcast_to(scales[i + j : i + j + 1], (width, span // 2))
            scale = jnp.concatenate([scale, scale], axis=1)
            z = products(load_f(i + j) * scale, load_g(i + j), width)
            high, low = split(z)
            highs.append(high)
            lows.append(low)
        high = jnp.concatenate(highs, axis=0)
        low = jnp.concatenate(lows, axis=0)
        v = dot(jnp.concatenate([high, low, high], axis=1), table)
        for j in range(step):
            u = dot(left_ref[1], jnp.concatenate([highs[j], lows[j], highs[j]], axis=0))
            strength = jnp.zeros((8, span), F32)
            across = jnp.zeros((8, span), F32)
            along = jnp.zeros((8, span), F32)
            for r in range(0, width, 8):
                square = u[r : r + 8] * u[r : r + 8]
                strength = strength + square
                first = r if r < width // 2 else r - width
                across = across + square * (row + first).astype(F32)
                piece = v[j * width + r : j * width + r + 8]
                piece = piece * piece
                if r % (width // 2) == 0:
                    piece = piece * special
                along = along + piece
            tile = i // step if place is None else place[i // step]
            for kind, value in enumerate((strength, across, along)):
                sum_ref[kind, j, pl.ds(tile, 1), :] = jnp.sum(value, axis=0, keepdims=True)


def finish(sum_ref, sums_ref):
    _, quads, rows, span = sum_ref.shape
    flat = jnp.concatenate([sum_ref[kind, quad] for kind in range(3) for quad in range(quads)], axis=0)
    done = exact_dot(flat, sums_ref[...])
    kinds = []
    for kind in range(3):
        value = jnp.zeros((rows, 128), F32)
        for quad in range(quads):
            base = (kind * quads + quad) * rows
            part = done[base : base + rows, :128] if kind < 2 else done[base : base + rows, 128:]
            value = value + (pltpu.roll(part, 4 * quad, 1) if quad else part)
        kinds.append(value)
    strength, across, along = kinds
    across = across / (strength + EPS_WEIGHT)
    along = along / (strength + EPS_WEIGHT)
    return strength, across, along


def pack(strength, across, along, where, offset):
    lane = lax.broadcasted_iota(jnp.int32, (8, 128), 1)
    total = jnp.sum(strength, axis=1, keepdims=True) + EPS_WEIGHT
    first = jnp.sum(strength * across, axis=1, keepdims=True) / total
    second = jnp.sum(strength * along, axis=1, keepdims=True) / total
    shifts = (pltpu.roll(across, where, 1) if where else across) + pltpu.roll(along, where + 16, 1)
    return shifts + jnp.where(lane == offset, first, 0.0) + jnp.where(lane == offset + 1, second, 0.0)


class Copies:
    def __init__(self, sems):
        self.sems, self.count = sems, 0

    def start(self, source, target):
        copy = pltpu.make_async_copy(source, target, self.sems.at[self.count])
        self.count += 1
        copy.start()
        return copy

    def start_either(self, even, first, second, target):
        sem = self.sems.at[self.count]
        self.count += 1

        @pl.when(even)
        def _():
            pltpu.make_async_copy(first, target, sem).start()

        @pl.when(jnp.logical_not(even))
        def _():
            pltpu.make_async_copy(second, target, sem).start()

        return pltpu.make_async_copy(first, target, sem)


def gx_is_odd():
    return lax.rem(lax.axis_index("gx"), 2)


def cut_kernel(sizes, rows, start_hbm, west_ref, east_ref, south_ref, first_out, second_out, rim_out, start_ref, raw_ref, cut_ref, sems):
    half = rows // 2
    copies = Copies(sems)
    even = gx_is_odd() == 1
    start = copies.start(start_hbm, start_ref)
    up, down = west_ref.at[0, 0:half, 0], east_ref.at[0, half:rows, 0]
    loads = [
        copies.start_either(even, down, up, raw_ref.at[0:half]),
        copies.start_either(even, up, down, raw_ref.at[half:rows]),
        copies.start(south_ref.at[0, rows - 1 : rows, 0], raw_ref.at[rows : rows + 1]),
    ]
    stores = []
    start.wait()
    turns = turns_of(start_ref, sizes)
    for load, block, target in zip(loads, (range(half), range(half, rows), range(rows, rows + 1)), (first_out, second_out, rim_out)):
        load.wait()
        for tile in block:
            cut_into(cut_ref.at[tile], raw_ref.at[tile], turns, sizes)
        stores.append(copies.start(cut_ref.at[block[0] : block[-1] + 1], target))
    for store in stores:
        store.wait()


def south_kernel(sizes, rows, start_hbm, south_ref, north_ref, east_ref, west_ref, position_ref, col_ref, row_ref, right_ref, back_ref, left_ref, sums_ref, ones_ref, out_ref, q_out, e_out, start_ref, raw_ref, d_ref, q_ref, e_ref, sum_ref, place_ref, sems):
    width, cell, count = sizes
    quads = count // 4
    groups = rows * quads
    inner = groups - quads
    copies = Copies(sems)
    half, inside = rows // 2, rows - 1
    batches = [[copies.start(start_hbm, start_ref)], [], []]
    batches[0].append(copies.start(south_ref.at[0, 0:inside, 0], raw_ref.at[0:inside]))
    batches[1].append(copies.start(north_ref.at[0, 1:rows, 0], raw_ref.at[inside : 2 * inside]))
    base = 2 * inside
    batches[2].append(copies.start(east_ref.at[0, 0:half, 0], raw_ref.at[base : base + half]))
    batches[2].append(copies.start(west_ref.at[0, half:rows, 0], raw_ref.at[base + half : base + rows]))
    batches[2].append(copies.start(north_ref.at[0, 0:1, 0], raw_ref.at[base + rows : base + rows + 1]))
    slots = [range(0, rows - 1), range(rows - 1, 2 * rows - 2), range(2 * rows - 2, 3 * rows - 1)]

    def arrive(batch):
        for copy in batches[batch]:
            copy.wait()

    def cut(batch):
        for slot in slots[batch]:
            cut_into(d_ref.at[slot], raw_ref.at[slot], turns, sizes)

    def transform(batch):
        first = slots[batch][0]

        def source(i):
            return d_ref[first + i // quads].reshape(quads * width, 4 * width)

        forward(source, q_ref, e_ref, right_ref, left_ref, first * quads, len(slots[batch]) * quads, width)

    arrive(0)
    turns = turns_of(start_ref, sizes)
    cut(0)
    arrive(1)
    transform(0)
    cut(1)
    arrive(2)
    transform(1)
    cut(2)
    transform(2)
    kept = slots[2][0] * quads
    own = copies.start(q_ref.at[kept : kept + groups + quads], q_out)
    e_out[...] = factors(e_ref[kept : kept + groups + quads], ones_ref, width)
    scales = factors(e_ref[:inner], ones_ref, width) * factors(e_ref[inner : 2 * inner], ones_ref, width)
    sum_ref[...] = jnp.zeros_like(sum_ref)
    backward(lambda i: q_ref[i], lambda i: q_ref[inner + i], scales, sum_ref, back_ref, left_ref, inner, width)
    strength, across, along = finish(sum_ref, sums_ref)
    place_ref[...] = jnp.zeros_like(place_ref)
    place_ref[0:2, 0:rows] = position_ref[0, 0]
    place_ref[2:3, 0:rows] = col_ref[0]
    place_ref[3:4, 0:rows] = row_ref[0]
    lane = lax.broadcasted_iota(jnp.int32, (8, 128), 1)
    row = lax.broadcasted_iota(jnp.int32, (8, 128), 0)
    packet = pack(strength, across, along, SOUTH, D_SOUTH)
    for field, where in enumerate((POSITION, POSITION + 1, COL, ROW)):
        value = jnp.where(lane == row, place_ref[field : field + 1, :], 0.0)
        packet = packet + jnp.where(lane == where, jnp.sum(value, axis=1, keepdims=True), 0.0)
    out_ref[...] = packet
    own.wait()


def east_kernel(sizes, rows, first_ref, second_ref, rim_ref, q_own, own_factors, south_ref, right_ref, back_ref, left_ref, sums_ref, ones_ref, out_ref, q_first, q_second, q_rim, e_first, e_second, e_rim, sum_ref, sems):
    width, cell, count = sizes
    quads = count // 4
    half = rows // 2 * quads
    copies = Copies(sems)
    odd = gx_is_odd()
    first, second = pl.multiple_of((1 - odd) * half, half), pl.multiple_of(odd * half, half)
    own = [
        copies.start(q_own.at[pl.ds(first, half)], q_first.at[0]),
        copies.start(q_own.at[pl.ds(second, half)], q_second.at[0]),
        copies.start(q_own.at[2 * half : 2 * half + quads], q_rim.at[0]),
    ]
    sum_ref[...] = jnp.zeros_like(sum_ref)

    def transform(source, q_ref, e_ref, number):
        def data(i):
            return source[i // quads].reshape(quads * width, 4 * width)

        forward(data, q_ref.at[1], e_ref, right_ref, left_ref, 0, number, width)

    def scales(energies, base):
        return factors(energies, ones_ref, width) * own_factors[pl.ds(base, energies.shape[0]), :]

    def correlate(q_ref, mine, factor, place):
        def load_first(i):
            return q_ref[1 - mine, i]

        def load_second(i):
            return q_ref[mine, i]

        backward(load_first, load_second, factor, sum_ref, back_ref, left_ref, factor.shape[0], width, place)

    def work(with_rim):
        transform(first_ref, q_first, e_first, half)
        transform(second_ref, q_second, e_second, half)
        if with_rim:
            transform(rim_ref, q_rim, e_rim, quads)
        first_scales = scales(e_first[...], first)
        second_scales = scales(e_second[...], second)
        for copy in own:
            copy.wait()
        correlate(q_first, odd, first_scales, [(1 - odd) * (rows // 2) + tile for tile in range(rows // 2)])
        correlate(q_second, 1 - odd, second_scales, [odd * (rows // 2) + tile for tile in range(rows // 2)])
        if with_rim:
            correlate(q_rim, 0, scales(e_rim[...], 2 * half), [rows])

    has_rim = lax.axis_index("gy") > 0

    @pl.when(has_rim)
    def _():
        work(True)

    @pl.when(jnp.logical_not(has_rim))
    def _():
        work(False)

    found = finish(sum_ref, sums_ref)
    row = lax.broadcasted_iota(jnp.int32, (8, 128), 0)
    east = [jnp.where(row < rows, value, 0.0) for value in found]
    rim = [jnp.where(row == rows - 1, pltpu.roll(value, 7, 0), 0.0) for value in found]
    packet = south_ref[...] + pack(*rim, SOUTH, D_SOUTH) + pack(*east, EAST, D_EAST)
    out_ref[...] = jnp.broadcast_to(packet[None, 0 : out_ref.shape[1]], out_ref.shape)


def turned(value, by):
    count = value.shape[0]
    by = by % count
    return value if by == 0 else jnp.concatenate([value[by:], value[:by]], axis=0)


def relax_kernel(counts, rows, patches, all_ref, shift_ref, placed_ref, x_ref):
    nx, nz, ny = counts
    column = ny * rows
    every = all_ref[...].reshape(nx * nz, ny, rows, 128)
    for gy in range(ny):
        x_ref[:, gy * rows : (gy + 1) * rows, :] = every[:, gy]
    packet = x_ref[...]
    sub = lax.broadcasted_iota(jnp.int32, packet.shape, 1)
    stack = lax.broadcasted_iota(jnp.int32, packet.shape, 0)
    gx, gz = stack // nz, stack % nz

    def field(where):
        return pltpu.roll(packet, 128 - where, 2)

    def one(where):
        return jnp.broadcast_to(packet[:, :, where : where + 1], packet.shape)

    def east(value):
        return turned(value, nz)

    def west(value):
        return turned(value, -nz)

    def south(value):
        return pltpu.roll(value, column - 1, 1)

    def north(value):
        return pltpu.roll(value, 1, 1)

    x = field(POSITION)
    d_east = field(D_EAST)
    d_east = jnp.where(sub % rows < rows // 2, d_east, east(d_east))
    d_south = field(D_SOUTH)
    d_south = jnp.where(sub % rows < rows - 1, d_south, pltpu.roll(d_south, column - rows, 1))
    ke = jnp.where(gx < nx - 1, one(COL), 0.0)
    ks = jnp.where(sub < column - 1, one(ROW), 0.0)
    kw, d_west = west(ke), west(d_east)
    kn, d_north = north(ks), north(d_south)
    has_next = jnp.where(gz < nz - 1, LINK_STIFF, 0.0)
    has_prev = jnp.where(gz > 0, LINK_STIFF, 0.0)
    for _ in range(ITERS):
        force = ke * (east(x) - x - d_east) - kw * (x - west(x) - d_west)
        force = force + ks * (south(x) - x - d_south) - kn * (x - north(x) - d_north)
        force = force + has_next * (turned(x, 1) - x) + has_prev * (turned(x, -1) - x)
        x = x + STEP_SIZE * force
    x_ref[...] = x
    mine = lax.axis_index("gy")
    place = lax.axis_index("gx") * nz + lax.axis_index("gz")
    me, total = place * ny + mine, nx * nz * ny
    holder, below = lax.rem(me + nz * ny, total), lax.rem(me + 1, total)
    lane = lax.broadcasted_iota(jnp.int32, (column, 128), 1)
    row = lax.broadcasted_iota(jnp.int32, (column, 128), 0)
    own = x_ref[place]
    for part in range(2):
        value = jnp.where((lane < rows) & (lane + mine * rows == row), own[:, part : part + 1], 0.0)
        placed_ref[0, 0, part : part + 1, :] = jnp.sum(value, axis=0, keepdims=True)[:, :rows]
    row, own = row[:rows], all_ref[me]
    easts = jnp.where(row < rows // 2, own, all_ref[holder])
    souths = jnp.where(row < rows - 1, own, all_ref[below])
    for kind, (source, where) in enumerate(((easts, EAST), (souths, SOUTH))):
        for part in range(2):
            value = source
            if where + part * patches:
                value = pltpu.roll(source, 128 - where - part * patches, 1)
            for tile in range(rows):
                shift_ref[0, tile, 0, kind, part : part + 1, :] = value[tile : tile + 1, :patches]


def exchange(block, first):
    route = []
    for low in range(first, lax.axis_size("gx") - 1, 2):
        route += [(low, low + 1), (low + 1, low)]
    return lax.ppermute(block, "gx", route)


def to_south(block):
    count = lax.axis_size("gy")
    route = [(0, 1), (1, 0)] if count == 2 else [(i - 1, i) for i in range(1, count)]
    return lax.ppermute(block, "gy", route)


def shards(east_strip, west_strip, north_strip, south_strip, patch_start, segment_offset, col_stiffness, row_stiffness):
    _, rows, _, width, length = east_strip.shape
    count = patch_start.shape[0]
    sizes = (width, length // count, count)
    quads = count // 4
    span = 4 * width
    groups = rows * quads
    counts = tuple(lax.axis_size(axis) for axis in PART)
    total = math.prod(counts)
    constants = [jnp.asarray(table) for table in tables(width)]
    vmem = pl.BlockSpec(memory_space=pltpu.VMEM)
    hbm = pl.BlockSpec(memory_space=pl.ANY)

    first_cut, second_cut, rim_cut = pl.pallas_call(
        functools.partial(cut_kernel, sizes, rows),
        out_shape=[
            jax.ShapeDtypeStruct((rows // 2, quads, width, span), BF16),
            jax.ShapeDtypeStruct((rows // 2, quads, width, span), BF16),
            jax.ShapeDtypeStruct((1, quads, width, span), BF16),
        ],
        in_specs=[hbm] * 4,
        out_specs=[hbm, hbm, hbm],
        scratch_shapes=[
            pltpu.SMEM((count,), jnp.int32),
            pltpu.VMEM((rows + 1, width, length), BF16),
            pltpu.VMEM((rows + 1, quads, width, span), BF16),
            pltpu.SemaphoreType.DMA((7,)),
        ],
        compiler_params=pltpu.CompilerParams(vmem_limit_bytes=CUT_VMEM),
        name="cut",
    )(patch_start, west_strip, east_strip, south_strip)
    first = exchange(first_cut, 1)
    second = exchange(second_cut, 0)
    rim = to_south(rim_cut)

    sums = pltpu.VMEM((3, quads, 8, span), F32)
    kept = groups + quads
    south, q_own, e_own = pl.pallas_call(
        functools.partial(south_kernel, sizes, rows),
        out_shape=[
            jax.ShapeDtypeStruct((8, 128), F32),
            jax.ShapeDtypeStruct((kept, width, span), F32),
            jax.ShapeDtypeStruct((kept, span // 2), F32),
        ],
        in_specs=[hbm] * 5 + [vmem] * 8,
        out_specs=[vmem, hbm, vmem],
        scratch_shapes=[
            pltpu.SMEM((count,), jnp.int32),
            pltpu.VMEM((3 * rows - 1, width, length), BF16),
            pltpu.VMEM((3 * rows - 1, quads, width, span), BF16),
            pltpu.VMEM((3 * groups - quads, width, span), F32),
            pltpu.VMEM((3 * groups - quads, span // 2), F32),
            sums,
            pltpu.VMEM((8, 128), F32),
            pltpu.SemaphoreType.DMA((7,)),
        ],
        compiler_params=pltpu.CompilerParams(vmem_limit_bytes=SOUTH_VMEM),
        cost_estimate=pl.CostEstimate(flops=1_000, bytes_accessed=1_000, transcendentals=0),
        name="south",
    )(
        patch_start,
        south_strip,
        north_strip,
        east_strip,
        west_strip,
        jnp.transpose(segment_offset, (0, 2, 3, 1)),
        jnp.transpose(col_stiffness, (0, 2, 1)),
        jnp.transpose(row_stiffness, (0, 2, 1)),
        *constants,
    )
    packet = pl.pallas_call(
        functools.partial(east_kernel, sizes, rows),
        out_shape=jax.ShapeDtypeStruct((total, rows, 128), F32),
        in_specs=[vmem, vmem, vmem, hbm] + [vmem] * 7,
        out_specs=vmem,
        scratch_shapes=[
            pltpu.VMEM((2, groups // 2, width, span), F32),
            pltpu.VMEM((2, groups // 2, width, span), F32),
            pltpu.VMEM((2, quads, width, span), F32),
            pltpu.VMEM((groups // 2, span // 2), F32),
            pltpu.VMEM((groups // 2, span // 2), F32),
            pltpu.VMEM((quads, span // 2), F32),
            sums,
            pltpu.SemaphoreType.DMA((3,)),
        ],
        compiler_params=pltpu.CompilerParams(vmem_limit_bytes=EAST_VMEM),
        cost_estimate=pl.CostEstimate(flops=1_000, bytes_accessed=1_000, transcendentals=0),
        name="east",
    )(first, second, rim, q_own, e_own, south, *constants)
    gathered = lax.all_to_all(packet, PART, 0, 0)
    patch_shift, placed = pl.pallas_call(
        functools.partial(relax_kernel, counts, rows, count),
        out_shape=[
            jax.ShapeDtypeStruct((1, rows, 1, 2, 2, count), F32),
            jax.ShapeDtypeStruct((1, 1, 2, rows), F32),
        ],
        in_specs=[vmem],
        out_specs=[vmem, vmem],
        scratch_shapes=[pltpu.VMEM((total // counts[2], counts[2] * rows, 128), F32)],
        compiler_params=pltpu.CompilerParams(vmem_limit_bytes=RELAX_VMEM),
        name="relax",
    )(gathered)
    return patch_shift, jnp.transpose(placed, (0, 3, 1, 2))


def solution(mesh):
    placed = (
        P(("groups", "gz"), "gy", "gx", None, None),
        P(("groups", "gz"), "gy", "gx", None, None),
        P(("groups", "gz"), "gy", "gx", None, None),
        P(("groups", "gz"), "gy", "gx", None, None),
        P(),
        P(("groups", "gz"), "gy", "gx", None),
        P(("groups", "gz"), "gy", "gx"),
        P(("groups", "gz"), "gy", "gx"),
    )
    return jax.shard_map(
        shards,
        mesh=mesh,
        in_specs=placed,
        out_specs=(
            P(("groups", "gz"), "gy", "gx", None, None, None),
            P(("groups", "gz"), "gy", "gx", None),
        ),
        check_vma=False,
    )
```
